32 devices in a mesh: dp: 8 (over y, x, core), seq: 4 (over z).
Axes of the slice: x: 2, y: 2, z: 4, core: 2. Of those that a mesh axis runs over, the one named last changes fastest.
Arguments:
- tokens: float32 [8, 1024, 1024], P('dp', 'seq'), may hold values from -6 to 6
- ln_params: float32 [4, 1024], P(None, ('dp', 'seq')), may hold values from 0.25 to 1.75
- qkv_weight: float32 [1024, 3, 1024], P(('dp', 'seq')), may hold values from -0.1875 to 0.1875
- out_weight: float32 [1024, 1024], P(('dp', 'seq')), may hold values from -3 to 3
- ffn_weight: float32 [4096, 3, 1024], P(('dp', 'seq')), may hold values from -0.1875 to 0.1875
- lengths: int32 [8, 16], P('dp'), may hold values from 1 to 896, 1024 in all within a row
- cotangent: float32 [8, 1024, 1024], P('dp', 'seq'), may hold values from -6 to 6
Outputs:
- output: float32 [8, 1024, 1024], P('dp', 'seq')
- input_grad: float32 [8, 1024, 1024], P('dp', 'seq')
- ln_grad: float32 [4, 1024], P(None, ('dp', 'seq'))
- qkv_grad: float32 [1024, 3, 1024], P(('dp', 'seq'))
- out_weight_grad: float32 [1024, 1024], P(('dp', 'seq'))
- ffn_grad: float32 [4096, 3, 1024], P(('dp', 'seq'))
The draws below stay inside these ranges and needn't reach their ends.
Inputs may be any that keep to these rules, and one draw needn't show every extreme that they name: Each row's 16 lengths sum to 1024; one of them is exactly 896.
All inputs are finite; a program needn't handle non-finite values.
Results may differ from the reference program's by a relative error of at most 0.013.
The reference program's roundings to bfloat16 on the way count: a program that leaves them out, or rounds other values in their place, can miss the bound.
Values may be sent and summed in bfloat16 or wider, within the bound.
A program may use at most 320 MiB of HBM per device.

```python
import math
import jax
import jax.numpy as jnp
import numpy as np
from jax import lax

HEAD_DIM = 64
D = 1024
FF = 4096
TOK_DEV = 256
SEGS = 16
ROWS = 8
L = 1024


def block_scale(stream_key, dims, split, least, high):
    level, own = 1.0, jax.random.fold_in(stream_key, 6)
    for dim, shards_of in split:
        steps = jnp.exp(jax.random.uniform(jax.random.fold_in(own, dim), (shards_of,), jnp.float32, least / len(split), high / len(split)))
        level = level * jnp.repeat(steps, dims[dim] // shards_of).reshape([-1 if axis == dim else 1 for axis in range(len(dims))])
    return level


def profile(amount, total, most, slope):
    loads = [(1 << 20) // math.isqrt(grade ** slope) + 1 for grade in range(2, amount + 1)]
    rest, given = total - most - (amount - 1), [1] * (amount - 1)
    while rest > 0:
        free = [i for i in range(amount - 1) if given[i] < most]
        whole, budget = sum([loads[i] for i in free]), rest
        for i in free:
            extra = min(most - given[i], max(1, budget * loads[i] // whole), rest)
            given[i] = given[i] + extra
            rest = rest - extra
    return np.array([most] + given)


def uneven(rng, count, total, bound, skew):
    if count == 2:
        one = jax.random.randint(rng, (), max(1, total - bound), min(bound, total - 1) + 1)
        return jnp.stack([one, total - one])
    tallies = jnp.asarray(profile(count, total, bound, skew), jnp.int32)
    pairs = (count - 1) // 2
    donor, receiver = tallies[1:1 + 2 * pairs:2], tallies[2:2 + 2 * pairs:2]
    room = jnp.minimum(donor - 1, bound - receiver)
    moved = jax.random.randint(jax.random.fold_in(rng, 1), (pairs,), 0, 1 << 20) % (room + 1)
    tallies = tallies.at[1:1 + 2 * pairs:2].set(donor - moved).at[2:2 + 2 * pairs:2].set(receiver + moved)
    return tallies[jax.random.permutation(jax.random.fold_in(rng, 2), count)]


def normal_values(rng, dims, deviation, limit, cuts=(), held_as=jnp.bfloat16):
    entries = deviation * jax.random.normal(rng, dims, jnp.float32)
    if cuts:
        entries = entries * block_scale(rng, dims, cuts, -0.22, 0.18)
    return jnp.clip(entries, -limit, limit).astype(held_as)


def setup_inputs(seed: int = 0) -> dict:
    splits = jax.random.split(jax.random.key(seed), 8)
    tokens = normal_values(splits[0], (ROWS, L, D), 1.0, 6.0, ((0, 8), (1, 4)), jnp.float32)
    ln_params = jnp.clip(1.0 + 0.15 * jax.random.normal(splits[1], (4, D), jnp.float32), 0.25, 1.75)
    qkv_weight = normal_values(splits[2], (D, 3, D), D ** -0.5, 0.1875, ((0, 32),), jnp.float32)
    out_weight = normal_values(splits[3], (D, D), (max(D // 256, 1)) ** -0.5, 3.0, ((0, 32),), jnp.float32)
    ffn_weight = normal_values(splits[4], (FF, 3, D), D ** -0.5, 0.1875, ((0, 32),), jnp.float32)
    lengths = jax.vmap(lambda own: uneven(own, SEGS, L, L - TOK_DEV // 2, 2))(jax.random.split(splits[5], ROWS)).reshape((ROWS, SEGS)).astype(jnp.int32)
    cotangent = normal_values(splits[6], (ROWS, L, D), 1.0, 6.0, ((0, 8), (1, 4)), jnp.float32)
    return dict(tokens=tokens, ln_params=ln_params, qkv_weight=qkv_weight, out_weight=out_weight, ffn_weight=ffn_weight, lengths=lengths, cotangent=cotangent)


@jax.custom_vjp
def low(v):
    return lax.optimization_barrier(v.astype(jnp.bfloat16)).astype(jnp.float32)

@jax.custom_vjp
def low_back(v):
    return v

def low_keep(v):
    return (low(v), None)

def low_pass(kept, grad):
    return (grad,)

def back_keep(v):
    return (v, None)

def back_low(kept, grad):
    return (low(grad),)
low.defvjp(low_keep, low_pass)
low_back.defvjp(back_keep, back_low)

def layer_norm(value, gain, shift):
    mean = lax.optimization_barrier(jnp.mean(value, axis=-1, keepdims=True))
    centred = value - mean
    var = lax.optimization_barrier(jnp.mean(centred * centred, axis=-1, keepdims=True))
    return centred * lax.rsqrt(var + 1e-05) * gain + shift

def segment_layout(seg_lengths, count):
    ends = jnp.cumsum(seg_lengths).astype(jnp.int32)
    place = jnp.arange(count, dtype=jnp.int32)
    done = place[:, None] >= ends[None, :]
    segment = lax.optimization_barrier(jnp.sum(done.astype(jnp.int32), axis=1)).astype(jnp.int32)
    start = lax.optimization_barrier(jnp.sum(jnp.where(done, seg_lengths[None, :], 0), axis=1)).astype(jnp.int32)
    return (segment, place - start)

def rotate(value, place):
    half = value.shape[-1] // 2
    rate = jnp.exp(jnp.arange(half, dtype=jnp.float32) * (-math.log(10000.0) / half))
    angle = place.astype(jnp.float32)[:, None] * rate[None, :]
    cosine = jnp.cos(angle)[:, None, :]
    sine = jnp.sin(angle)[:, None, :]
    first = value[..., :half]
    second = value[..., half:]
    return jnp.concatenate([first * cosine - second * sine, second * cosine + first * sine], axis=-1)

def row_forward(weights, inputs):
    ln_w, qkv_w, out_w, ffn_w = weights
    row, seg_lengths = inputs
    count, width = row.shape
    heads = width // HEAD_DIM
    segment, place = segment_layout(seg_lengths, count)
    hi = lax.Precision.HIGHEST
    normed1 = low(layer_norm(row, ln_w[0], ln_w[1]))
    qkv = jnp.einsum('td,dkf->tkf', normed1, qkv_w, precision=hi)
    query = low(rotate(low_back(qkv[:, 0]).reshape(count, heads, HEAD_DIM), place))
    key = low(rotate(low_back(qkv[:, 1]).reshape(count, heads, HEAD_DIM), place))
    value = low(low_back(qkv[:, 2])).reshape(count, heads, HEAD_DIM)
    same = segment[:, None] == segment[None, :]

    def one_head(parts):
        q_head, k_head, v_head = parts
        score = low_back(jnp.dot(q_head, k_head.T, precision=hi)) * 0.125
        score = jnp.where(same, score, -1e+30)
        top = lax.optimization_barrier(jnp.max(score, axis=1, keepdims=True))
        weight = jnp.exp(score - top)
        prob = low(weight / lax.optimization_barrier(jnp.sum(weight, axis=1, keepdims=True)))
        return jnp.dot(prob, v_head, precision=hi)
    mixed = lax.map(jax.checkpoint(one_head), (query.transpose(1, 0, 2), key.transpose(1, 0, 2), value.transpose(1, 0, 2)))
    attended = low(low_back(mixed.transpose(1, 0, 2).reshape(count, width)))
    middle = row + low_back(jnp.dot(attended, out_w, precision=hi))
    normed2 = low(layer_norm(middle, ln_w[2], ln_w[3]))
    gate = low_back(jnp.dot(normed2, ffn_w[:, 0, :].T, precision=hi))
    up_proj = low_back(jnp.dot(normed2, ffn_w[:, 1, :].T, precision=hi))
    hidden = low(jax.nn.silu(gate) * up_proj)
    return middle + low_back(jnp.dot(hidden, ffn_w[:, 2, :], precision=hi))

def reference(tokens, ln_params, qkv_weight, out_weight, ffn_weight, lengths, cotangent):

    def forward(tokens_f, ln_f, qkv_f, out_f, ffn_f):
        weights = (low(ln_f), low(qkv_f), low(out_f), low(ffn_f))
        step = jax.checkpoint(lambda inputs: row_forward(weights, inputs))
        return lax.map(step, (tokens_f, lengths))
    output, pullback = jax.vjp(forward, tokens, ln_params, qkv_weight, out_weight, ffn_weight)
    grads = pullback(cotangent)
    return (output, grads[0], grads[1], grads[2], grads[3], grads[4])
```

```python
import functools
import math

import jax
import jax.numpy as jnp
from jax import lax
from jax.experimental import pallas as pl
from jax.experimental.pallas import tpu as pltpu
from jax.sharding import PartitionSpec as P

HEAD_DIM = 64
GROUP = 8
LANES = 128
BF = jnp.bfloat16
F32 = jnp.float32
MESH = pl.DeviceIdType.MESH
NT = (((1,), (1,)), ((), ()))
NN = (((1,), (0,)), ((), ()))
TN = (((0,), (0,)), ((), ()))
EPS = 1e-05


def dot(a, b, dims):
    return lax.dot_general(a, b, dims, preferred_element_type=F32)


def remote(src, dst, send, recv, device):
    return pltpu.make_async_remote_copy(
        src_ref=src, dst_ref=dst, send_sem=send, recv_sem=recv, device_id=device, device_id_type=MESH
    )


def local(src, dst, sem):
    return pltpu.make_async_copy(src, dst, sem)


def greet(peers):
    barrier = pltpu.get_barrier_semaphore()
    for peer in peers:
        pl.semaphore_signal(barrier, inc=1, device_id=peer, device_id_type=MESH)
    pl.semaphore_wait(barrier, len(peers))


def greet_all(dp, seq):
    barrier = pltpu.get_barrier_semaphore()
    total = dp * seq
    me = lax.axis_index("dp") * seq + lax.axis_index("seq")

    def hello(j, carry):
        other = lax.rem(me + j, total)
        pl.semaphore_signal(
            barrier, inc=1, device_id=(other // seq, lax.rem(other, seq)), device_id_type=MESH
        )
        return carry

    lax.fori_loop(1, total, hello, 0)
    pl.semaphore_wait(barrier, total - 1)


class Place:
    def __init__(self, dp, seq):
        self.dp, self.seq = dp, seq
        self.d, self.s = lax.axis_index("dp"), lax.axis_index("seq")
        self.c, self.k = self.d // 2, lax.rem(self.d, 2)
        self.sib = self.d + 1 - 2 * self.k
        self.chips = dp // 2
        self.group = min(dp, GROUP)
        self.groups = dp // self.group
        self.g, self.p = self.d // self.group, lax.rem(self.d, self.group)
        self.gc = self.p // 2
        self.gchips = self.group // 2
        self.half = seq // 2
        self.r, self.h = self.s // self.half, lax.rem(self.s, self.half)
        self.hg = 2 * self.h + self.k
        self.n = self.d * seq + self.s
        self.total = dp * seq

    def in_group(self, chip, core):
        return self.g * self.group + 2 * chip + core


def normalise(value):
    mean = jnp.mean(value, axis=-1, keepdims=True)
    centred = value - mean
    var = jnp.mean(centred * centred, axis=-1, keepdims=True)
    scale = lax.rsqrt(var + EPS)
    return centred * scale, scale


def norm_back(grad, normal, scale, gain):
    scaled = grad * gain
    return scale * (
        scaled
        - jnp.mean(scaled, axis=-1, keepdims=True)
        - normal * jnp.mean(scaled * normal, axis=-1, keepdims=True)
    )


def gather_kernel(
    dp,
    seq,
    tok,
    lnb,
    lens,
    wq,
    wo,
    cot,
    xrow,
    wq_full,
    wo_full,
    ln_out,
    lens_pair,
    dyb_all,
    ln_all,
    wcol,
    xown,
    dyb,
    ln_sem,
    len_sem,
    loc,
    wq1s,
    wq1r,
    wq2s,
    wq2r,
    wo1s,
    wo1r,
    wo2s,
    wo2r,
    wo3s,
    wo3r,
    xs,
    xr,
    xfs,
    xfr,
    dys,
    dyr,
    dyfs,
    dyfr,
):
    me = Place(dp, seq)
    count, width = tok.shape
    wr = wo.shape[0]
    cr = wr * seq
    pair = wcol.shape[2]
    head = pair // 2
    halfrows = count // 2
    dyb[...] = cot[...].astype(BF)
    ln_all[me.n] = lnb[...]
    lens_pair[me.k] = lens[...]
    greet_all(dp, seq)

    def send_ln(j, carry):
        other = lax.rem(me.n + j, me.total)
        remote(
            lnb, ln_all.at[me.n], ln_sem.at[0], ln_sem.at[1], (other // seq, lax.rem(other, seq))
        ).start()
        return carry

    lax.fori_loop(1, me.total, send_ln, 0)
    len_copy = remote(
        lens, lens_pair.at[me.k], len_sem.at[0], len_sem.at[1], (me.sib, me.s)
    )
    len_copy.start()
    row0 = pl.multiple_of(me.s * wr, wr)
    out0 = pl.multiple_of(me.n * wr, wr)
    wq_first, wo_first = [], []
    for j in range(1, seq):
        to = lax.rem(me.s + j, seq)
        col = pl.multiple_of(lax.rem(to, me.half) * pair, pair)
        wq_first.append(
            remote(
                wq.at[:, :, pl.ds(col, pair)],
                wcol.at[:, pl.ds(row0, wr), :],
                wq1s.at[j],
                wq1r.at[j],
                (me.d, to),
            )
        )
    for copy in wq_first:
        copy.start()
    own_col = pl.multiple_of(me.h * pair, pair)
    own_wq = local(wq.at[:, :, pl.ds(own_col, pair)], wcol.at[:, pl.ds(row0, wr), :], loc.at[0])
    own_wq.start()
    own_wo = local(wo, wo_full.at[pl.ds(out0, wr), :], loc.at[1])
    own_wo.start()
    own_dy = local(dyb, dyb_all.at[me.p], loc.at[2])
    own_dy.start()
    normal, _ = normalise(tok[...])
    remote(
        ln_all.at[pl.ds(0, me.total - 1)],
        ln_all.at[pl.ds(0, me.total - 1)],
        ln_sem.at[0],
        ln_sem.at[1],
        (me.sib, me.s),
    ).wait()
    tiles = width // LANES
    per = me.total // tiles
    for t in range(tiles):
        part = ln_all[t * per]
        for i in range(1, per):
            part = part + ln_all[t * per + i]
        ln_out[:, t * LANES : (t + 1) * LANES] = part
    xown[...] = (normal * ln_out[0:1, :] + ln_out[1:2, :]).astype(BF)
    rows0 = pl.multiple_of(me.s * count, count)
    for j in range(me.half):
        to = me.k * me.half + lax.rem(me.h + j, me.half)
        for core in range(2):
            src = xown.at[pl.ds(core * halfrows, halfrows), :]
            dst = xrow.at[pl.ds(rows0 + core * halfrows, halfrows), :]
            here = jnp.logical_and(to == me.s, core == me.k)

            @pl.when(jnp.logical_not(here))
            def _(src=src, dst=dst, core=core, to=to, j=j):
                remote(src, dst, xs.at[j, core], xr.at[me.s], (2 * me.c + core, to)).start()

            @pl.when(here)
            def _(src=src, dst=dst):
                local(src, dst, xr.at[me.s]).start()

    for j in range(1, seq):
        to = lax.rem(me.s + j, seq)
        wo_first.append(
            remote(wo, wo_full.at[pl.ds(out0, wr), :], wo1s.at[j], wo1r.at[j], (me.d, to))
        )
    for copy in wo_first:
        copy.start()
    for copy in wq_first:
        copy.wait()
    own_wq.wait()
    crow0 = pl.multiple_of(me.d * cr, cr)

    def send_wq(j, carry):
        to = lax.rem(me.d + j, dp)
        col = pl.multiple_of(lax.rem(to, 2) * head, head)
        remote(
            wcol.at[:, :, pl.ds(col, head)],
            wq_full.at[:, pl.ds(crow0, cr), :],
            wq2s.at[j],
            wq2r.at[j],
            (to, me.s),
        ).start()
        return carry

    lax.fori_loop(1, dp, send_wq, 0)
    own_half = local(
        wcol.at[:, :, pl.ds(pl.multiple_of(me.k * head, head), head)],
        wq_full.at[:, pl.ds(crow0, cr), :],
        loc.at[3],
    )
    own_half.start()
    for copy in wo_first:
        copy.wait()
    own_wo.wait()
    mine = wo_full.at[pl.ds(crow0, cr), :]
    wo_sends = [remote(mine, mine, wo3s.at[0], wo3r.at[0], (me.sib, me.s))]
    for j in range(1, me.chips):
        to = 2 * lax.rem(me.c + j, me.chips) + me.k
        wo_sends.append(remote(mine, mine, wo2s.at[j], wo2r.at[j], (to, me.s)))
    dy_sends = [remote(dyb, dyb_all.at[me.p], dyfs.at[0], dyfr.at[0], (me.sib, me.s))]
    for j in range(1, me.gchips):
        to = me.in_group(lax.rem(me.gc + j, me.gchips), me.k)
        dy_sends.append(remote(dyb, dyb_all.at[me.p], dys.at[j], dyr.at[j], (to, me.s)))
    for copy in wo_sends + dy_sends:
        copy.start()
    for j in range(seq):
        source = lax.rem(me.s + j, seq)
        part = xrow.at[pl.ds(pl.multiple_of(source * count + me.k * halfrows, halfrows), halfrows), :]
        local(part, part, xr.at[source]).wait()
        remote(part, part, xfs.at[j], xfr.at[j], (me.sib, me.s)).start()
    for j in range(1, me.chips):
        source = 2 * lax.rem(me.c + me.chips - j, me.chips) + me.k
        part = wo_full.at[pl.ds(pl.multiple_of(source * cr, cr), cr), :]
        remote(part, part, wo2s.at[j], wo2r.at[j], (me.sib, me.s)).wait_recv()
        remote(part, part, wo3s.at[j], wo3r.at[j], (me.sib, me.s)).start()
    for j in range(1, me.gchips):
        source = 2 * lax.rem(me.gc + me.gchips - j, me.gchips) + me.k
        part = dyb_all.at[source]
        remote(part, part, dys.at[j], dyr.at[j], (me.sib, me.s)).wait_recv()
        remote(part, part, dyfs.at[j], dyfr.at[j], (me.sib, me.s)).start()
    for j in range(me.half):
        to = me.k * me.half + lax.rem(me.h + j, me.half)
        for core in range(2):
            src = xown.at[pl.ds(core * halfrows, halfrows), :]
            here = jnp.logical_and(to == me.s, core == me.k)

            @pl.when(jnp.logical_not(here))
            def _(src=src, j=j, core=core):
                remote(src, src, xs.at[j, core], xr.at[0], (me.sib, me.s)).wait_send()

    for j in range(seq):
        part = xrow.at[pl.ds(0, halfrows), :]
        remote(part, part, xfs.at[j], xfr.at[j], (me.sib, me.s)).wait()

    def wait_wq(j, carry):
        part = wq_full.at[:, pl.ds(0, cr), :]
        remote(part, part, wq2s.at[j], wq2r.at[j], (me.sib, me.s)).wait()
        return carry

    lax.fori_loop(1, dp, wait_wq, 0)
    own_half.wait()
    own_dy.wait()
    len_copy.wait()
    for j in range(1, me.chips):
        remote(mine, mine, wo2s.at[j], wo2r.at[j], (me.sib, me.s)).wait_send()
        remote(mine, mine, wo3s.at[j], wo3r.at[j], (me.sib, me.s)).wait()
    remote(mine, mine, wo3s.at[0], wo3r.at[0], (me.sib, me.s)).wait()
    for j in range(1, me.gchips):
        remote(dyb, dyb, dys.at[j], dyr.at[j], (me.sib, me.s)).wait_send()
        remote(dyb, dyb, dyfs.at[j], dyfr.at[j], (me.sib, me.s)).wait()
    remote(dyb, dyb, dyfs.at[0], dyfr.at[0], (me.sib, me.s)).wait()


def swap_halves(value):
    half = HEAD_DIM // 2
    width = value.shape[1]
    lane = lax.broadcasted_iota(jnp.int32, value.shape, 1)
    up = pltpu.roll(value, width - half, 1)
    down = pltpu.roll(value, half, 1)
    return jnp.where(lax.rem(lane, HEAD_DIM) < half, up, down)


def head_mask(shape, h):
    lane = lax.broadcasted_iota(jnp.int32, shape, 1)
    return jnp.logical_and(lane >= h * HEAD_DIM, lane < (h + 1) * HEAD_DIM)


def attend_kernel(
    dp,
    seq,
    segs,
    xrow,
    wq,
    lens,
    wf,
    q_out,
    k_out,
    v_out,
    lse_out,
    cos_out,
    sin_out,
    seg_col,
    seg_row,
    mixed_in,
    wf_full,
    mixed,
    ms,
    mr,
    fs,
    fr,
    loc,
):
    me = Place(dp, seq)
    total = xrow.shape[0]
    count = total // seq
    width = wq.shape[2]
    heads = width // HEAD_DIM
    units = wf.shape[1]
    slots = me.groups * seq
    slot = me.g * seq + me.s
    greet_all(dp, seq)
    mine = wf_full.at[:, pl.ds(pl.multiple_of(slot * units, units), units), :]
    own_wf = local(wf, mine, loc.at[0])
    own_wf.start()
    for j in range(1, slots):
        other = lax.rem(slot + j, slots)
        to = ((other // seq) * me.group + me.p, lax.rem(other, seq))
        remote(wf, mine, fs.at[j], fr.at[j], to).start()
    row = lens[me.r]
    place_row = lax.broadcasted_iota(jnp.int32, (8, total), 1)
    place_col = lax.broadcasted_iota(jnp.int32, (total, LANES), 0)
    end = jnp.zeros((1, 1), jnp.int32)
    segr = jnp.zeros((8, total), jnp.int32)
    segc = jnp.zeros((total, LANES), jnp.int32)
    start = jnp.zeros((total, LANES), jnp.int32)
    for j in range(segs):
        length = row[0:1, j : j + 1]
        end = end + length
        segr = segr + (place_row >= end).astype(jnp.int32)
        past = place_col >= end
        segc = segc + past.astype(jnp.int32)
        start = start + jnp.where(past, length, 0)
    seg_row[...] = segr
    seg_col[...] = segc
    half = HEAD_DIM // 2
    lane = lax.broadcasted_iota(jnp.int32, (1, LANES), 1)
    rate = jnp.exp(lax.rem(lane, half).astype(F32) * (-math.log(10000.0) / half))
    angle = (place_col - start).astype(F32) * rate
    cos_out[...] = jnp.cos(angle)
    sign = jnp.where(lax.rem(lane, HEAD_DIM) < half, -1.0, 1.0)
    sin_out[...] = jnp.sin(angle) * sign

    def project(i, carry):
        rows = pl.ds(pl.multiple_of(i * count, count), count)
        x = xrow[rows, :]
        cosine = jnp.concatenate([cos_out[rows, :]] * (width // LANES), axis=1)
        sine = jnp.concatenate([sin_out[rows, :]] * (width // LANES), axis=1)
        raw = dot(x, wq[0], NN)
        q_out[rows, :] = (raw * cosine + swap_halves(raw) * sine).astype(BF)
        raw = dot(x, wq[1], NN)
        k_out[rows, :] = (raw * cosine + swap_halves(raw) * sine).astype(BF)
        v_out[rows, :] = dot(x, wq[2], NN).astype(BF)
        return carry

    lax.fori_loop(0, seq, project, 0)

    def chunk(step, carry):
        i = lax.rem(me.s + step, seq)
        rows = pl.ds(pl.multiple_of(i * count, count), count)
        q = q_out[rows, :]
        bias = jnp.where(seg_col[rows, 0:1] == seg_row[0:1, :], 0.0, -1e30)
        lane = lax.broadcasted_iota(jnp.int32, (count, LANES), 1)
        lse = jnp.zeros((count, LANES), F32)
        out = jnp.zeros((count, width), F32)
        for h in range(heads):
            mask = head_mask((count, width), h)
            score = dot(jnp.where(mask, q, jnp.zeros_like(q)), k_out[...], NT) * 0.125 + bias
            top = jnp.max(score, axis=1, keepdims=True)
            weight = jnp.exp(score - top)
            tally = jnp.sum(weight, axis=1, keepdims=True)
            prob = (weight * (1.0 / tally)).astype(BF)
            out = jnp.where(mask, dot(prob, v_out[...], NN), out)
            lse = jnp.where(lane == h, top + jnp.log(tally), lse)
        lse_out[rows, :] = lse
        mixed[i] = out.astype(BF)
        owner = 2 * me.c + me.r
        here = jnp.logical_and(i == me.s, owner == me.d)

        @pl.when(jnp.logical_not(here))
        def _():
            remote(mixed.at[i], mixed_in.at[me.hg], ms.at[i], mr.at[me.hg], (owner, i)).start()

        @pl.when(here)
        def _():
            local(mixed.at[i], mixed_in.at[me.hg], mr.at[me.hg]).start()

        return carry

    lax.fori_loop(0, seq, chunk, 0)
    for j in range(seq):
        local(mixed.at[j], mixed_in.at[j], mr.at[j]).wait()
        here = jnp.logical_and(j == me.s, me.r == me.k)

        @pl.when(jnp.logical_not(here))
        def _(j=j):
            remote(mixed.at[j], mixed.at[j], ms.at[j], mr.at[j], (me.sib, me.s)).wait_send()

    own_wf.wait()
    for j in range(1, slots):
        remote(wf, mine, fs.at[j], fr.at[j], (me.sib, me.s)).wait()


def ffn_kernel(
    dp,
    seq,
    tok,
    mixed_in,
    wo,
    ln,
    dyb_all,
    wf,
    cot,
    mid_out,
    dmid_out,
    ln2_out,
    br_out,
    gf_out,
    xn2,
    xall,
    hid,
    dg,
    du,
    dpart,
    dsib,
    dsum,
    drecv,
    bpart,
    bsib,
    normal2,
    scale2,
    loc,
    xs,
    xr,
    xfs,
    xfr,
    dss,
    dsr,
    dps,
    dpr,
    bss,
    bsr,
):
    me = Place(dp, seq)
    count, width = tok.shape
    units = wf.shape[1]
    nc = me.gchips
    tile = min(256, units)
    cols = 256
    sib = (me.sib, me.s)
    mid = tok[...]
    block = mixed_in.shape[2]
    for h in range(mixed_in.shape[0]):
        mid = mid + dot(mixed_in[h], wo[h * block : (h + 1) * block, :], NN)
    mid_out[...] = mid
    normal, scale = normalise(mid)
    normal2[...] = normal
    scale2[...] = jnp.broadcast_to(scale, scale2.shape)
    low = (normal * ln[2:3, :] + ln[3:4, :]).astype(BF)
    xn2[...] = low
    greet([sib] + [(me.in_group(lax.rem(me.gc + j, nc), me.k), me.s) for j in range(1, nc)])
    sends = [remote(xn2, xall.at[me.gc, me.k], xfs.at[0], xfr.at[0], sib)]
    for j in range(1, nc):
        to = me.in_group(lax.rem(me.gc + j, nc), me.k)
        sends.append(remote(xn2, xall.at[me.gc, me.k], xs.at[j], xr.at[j], (to, me.s)))
    for copy in sends:
        copy.start()
    xall[me.gc, me.k] = low

    def chip(j, carry):
        cj = lax.rem(me.gc + nc - j, nc)

        @pl.when(j > 0)
        def _():
            part = xall.at[cj, me.k]
            remote(part, part, xs.at[j], xr.at[j], sib).wait_recv()
            remote(part, part, xfs.at[j], xfr.at[j], sib).start()

        theirs = xall.at[cj, 1 - me.k]
        remote(theirs, theirs, xfs.at[j], xfr.at[j], sib).wait_recv()
        rows = pl.ds(pl.multiple_of(cj * 2 * count, 2 * count), 2 * count)
        x = xall[cj].reshape(2 * count, width)
        dy = dyb_all[pl.ds(2 * cj, 2)].reshape(2 * count, width)
        for t in range(units // tile):
            span = slice(t * tile, (t + 1) * tile)
            gate = dot(x, wf[0, span, :], NT)
            up = dot(x, wf[1, span, :], NT)
            dh = dot(dy, wf[2, span, :], NT)
            sigma = 1.0 / (1.0 + jnp.exp(-gate))
            active = gate * sigma
            hid[rows, span] = (active * up).astype(BF)
            dg[rows, span] = (dh * up * (sigma * (1.0 + gate * (1.0 - sigma)))).astype(BF)
            du[rows, span] = (dh * active).astype(BF)
        for t in range(width // cols):
            span = slice(t * cols, (t + 1) * cols)
            value = dot(dg[rows, :], wf[0, :, span], NN) + dot(du[rows, :], wf[1, :, span], NN)
            dpart[j, :, :, span] = value.astype(BF).reshape(2, count, cols)
        remote(dpart.at[j, 1 - me.k], dsib.at[j], dss.at[j], dsr.at[j], sib).start()
        for t in range(width // cols):
            span = slice(t * cols, (t + 1) * cols)
            value = dot(hid[rows, :], wf[2, :, span], NN)
            bpart[j, :, :, span] = value.astype(BF).reshape(2, count, cols)
        remote(bpart.at[j, 1 - me.k], bsib.at[j], bss.at[j], bsr.at[j], sib).start()
        remote(dsib.at[j], dsib.at[j], dss.at[j], dsr.at[j], sib).wait()
        dsum[j] = (dpart[j, me.k].astype(F32) + dsib[j].astype(F32)).astype(BF)

        @pl.when(j > 0)
        def _():
            remote(
                dsum.at[j], drecv.at[j], dps.at[j], dpr.at[j], (me.in_group(cj, me.k), me.s)
            ).start()

        return carry

    lax.fori_loop(0, nc, chip, 0)

    def grads(t, carry):
        span = pl.ds(pl.multiple_of(t * tile, tile), tile)
        x = xall[...].reshape(nc * 2 * count, width)
        dy = dyb_all[...].reshape(nc * 2 * count, width)
        gf_out[0, span, :] = dot(dg[:, span], x, TN).astype(BF)
        gf_out[1, span, :] = dot(du[:, span], x, TN).astype(BF)
        gf_out[2, span, :] = dot(hid[:, span], dy, TN).astype(BF)
        return carry

    lax.fori_loop(0, units // tile, grads, 0)
    for j in range(nc):
        remote(bsib.at[j], bsib.at[j], bss.at[j], bsr.at[j], sib).wait()
        br_out[j] = (bpart[j, me.k].astype(F32) + bsib[j].astype(F32)).astype(BF)
        remote(xn2, xn2, xfs.at[j], xfr.at[j], sib).wait_send()
    dn2 = dsum[0].astype(F32)
    for j in range(1, nc):
        remote(dsum.at[j], drecv.at[j], dps.at[j], dpr.at[j], sib).wait()
        remote(xn2, xn2, xs.at[j], xr.at[j], sib).wait_send()
        dn2 = dn2 + drecv[j].astype(F32)
    normal = normal2[...]
    dmid_out[...] = cot[...] + norm_back(dn2, normal, scale2[:, 0:1], ln[2:3, :])
    ln2_out[0:1, :] = jnp.sum(dn2 * normal, axis=0, keepdims=True)
    ln2_out[1:2, :] = jnp.sum(dn2, axis=0, keepdims=True)
    ln2_out[2:8, :] = jnp.zeros((6, width), F32)


def back_kernel(
    dp,
    seq,
    tok,
    mid,
    dmid,
    ln,
    ln2,
    brsum,
    gf,
    mixed_in,
    wo,
    wq,
    xrow,
    q_in,
    k_in,
    v_in,
    lse_in,
    cos_in,
    sin_in,
    seg_col,
    seg_row,
    out,
    input_grad,
    lng,
    qg,
    og,
    fg,
    dmix,
    dmix_row,
    brr,
    ogp,
    ogsib,
    ogs,
    ogpl,
    ogc,
    ogz,
    dq,
    dk,
    dv,
    dnp,
    dnsib,
    dns,
    dnr,
    qgp,
    qgt,
    qgpl,
    qgc,
    qgz,
    fgr,
    lnp,
    lnr,
    loc,
    dms,
    dmr,
    brs,
    brrs,
    gs,
    gr,
    o1,
    o2s,
    o2r,
    o3s,
    o3r,
    n1,
    n2s,
    n2r,
    q1s,
    q1r,
    q2s,
    q2r,
    lnsem,
):
    me = Place(dp, seq)
    count, width = tok.shape
    total = xrow.shape[0]
    block = q_in.shape[1]
    heads = block // HEAD_DIM
    wr = og.shape[0]
    cr = wr * seq
    units = fg.shape[1]
    slots = me.groups * seq
    slot = me.g * seq + me.s
    sib = (me.sib, me.s)
    greet_all(dp, seq)
    dmb = dmid[...].astype(BF)
    for hg in range(seq):
        dmix[hg] = dot(dmb, wo[hg * block : (hg + 1) * block, :], NT).astype(BF)
        to = (2 * me.c + hg % 2, me.k * me.half + hg // 2)
        here = jnp.logical_and(to[0] == me.d, to[1] == me.s)
        src, dst = dmix.at[hg], dmix_row.at[me.s]

        @pl.when(jnp.logical_not(here))
        def _(src=src, dst=dst, hg=hg, to=to):
            remote(src, dst, dms.at[hg], dmr.at[me.s], to).start()

        @pl.when(here)
        def _(src=src, dst=dst):
            local(src, dst, dmr.at[me.s]).start()

    for j in range(1, me.gchips):
        to = me.in_group(lax.rem(me.gc + me.gchips - j, me.gchips), me.k)
        remote(brsum.at[j], brr.at[j], brs.at[j], brrs.at[j], (to, me.s)).start()
    for j in range(1, slots):
        other = lax.rem(slot + j, slots)
        to = ((other // seq) * me.group + me.p, lax.rem(other, seq))
        src = gf.at[:, pl.ds(pl.multiple_of(other * units, units), units), :]
        remote(src, fgr.at[j], gs.at[j], gr.at[j], to).start()
    for h in range(seq):
        part = dot(mixed_in[h], dmb, TN).astype(BF)
        for t in range(block // cr):
            first = h * (block // cr) + t
            ogp[first % 2, first // 2] = part[t * cr : (t + 1) * cr]
    remote(ogp.at[1 - me.k], ogsib, o1.at[0], o1.at[1], sib).start()
    for j in range(seq):
        local(dmix.at[j], dmix_row.at[j], dmr.at[j]).wait()
    remote(ogp.at[1 - me.k], ogsib, o1.at[0], o1.at[1], sib).wait()
    ogs[...] = (ogp[me.k].astype(F32) + ogsib[...].astype(F32)).astype(BF)

    def send_og(j, carry):
        chip = lax.rem(me.c + j, me.chips)
        remote(ogs.at[chip], ogpl.at[j], o2s.at[j], o2r.at[j], (2 * chip + me.k, me.s)).start()
        return carry

    lax.fori_loop(1, me.chips, send_og, 0)
    dk[...] = jnp.zeros_like(dk)
    dv[...] = jnp.zeros_like(dv)

    def chunk(i, carry):
        rows = pl.ds(pl.multiple_of(i * count, count), count)
        q = q_in[rows, :]
        dm = dmix_row[i]
        lse = lse_in[rows, :]
        bias = jnp.where(seg_col[rows, 0:1] == seg_row[0:1, :], 0.0, -1e30)
        grad_q = jnp.zeros((count, block), F32)
        for h in range(heads):
            mask = head_mask((count, block), h)
            qh = jnp.where(mask, q, jnp.zeros_like(q))
            dmh = jnp.where(mask, dm, jnp.zeros_like(dm))
            score = dot(qh, k_in[...], NT) * 0.125 + bias
            prob = jnp.exp(score - lse[:, h : h + 1])
            dprob = dot(dmh, v_in[...], NT)
            centre = jnp.sum(prob * dprob, axis=1, keepdims=True)
            ds = (0.125 * prob * (dprob - centre)).astype(BF)
            grad_q = jnp.where(mask, dot(ds, k_in[...], NN), grad_q)
            dk[...] += dot(ds, qh, TN)
            dv[...] += dot(prob.astype(BF), dmh, TN)
        dq[rows, :] = grad_q
        return carry

    lax.fori_loop(0, seq, chunk, 0)

    def back_chunk(i):
        rows = pl.ds(pl.multiple_of(i * count, count), count)
        cosine = jnp.concatenate([cos_in[rows, :]] * (block // LANES), axis=1)
        sine = jnp.concatenate([sin_in[rows, :]] * (block // LANES), axis=1)
        a = dq[rows, :]
        a = (a * cosine - swap_halves(a) * sine).astype(BF)
        b = dk[rows, :]
        b = (b * cosine - swap_halves(b) * sine).astype(BF)
        c = dv[rows, :].astype(BF)
        qgp[0, rows, :] = a
        qgp[1, rows, :] = b
        qgp[2, rows, :] = c
        value = dot(a, wq[0], NT) + dot(b, wq[1], NT) + dot(c, wq[2], NT)
        dnp[lax.rem(i, 2), i // 2] = value.astype(BF)

    def other_half(j, carry):
        back_chunk(2 * j + 1 - me.k)
        return carry

    def own_half(j, carry):
        back_chunk(2 * j + me.k)
        return carry

    lax.fori_loop(0, me.half, other_half, 0)
    remote(dnp.at[1 - me.k], dnsib, n1.at[0], n1.at[1], sib).start()
    lax.fori_loop(0, me.half, own_half, 0)
    remote(dnp.at[1 - me.k], dnsib, n1.at[0], n1.at[1], sib).wait()
    owner = 2 * me.c + me.r
    for j in range(me.half):
        dns[j] = (dnp[me.k, j].astype(F32) + dnsib[j].astype(F32)).astype(BF)
        i = 2 * j + me.k
        here = jnp.logical_and(owner == me.d, i == me.s)

        @pl.when(jnp.logical_not(here))
        def _(j=j, i=i):
            remote(dns.at[j], dnr.at[me.h], n2s.at[j], n2r.at[me.h], (owner, i)).start()

        @pl.when(here)
        def _(j=j):
            local(dns.at[j], dnr.at[me.h], n2r.at[me.h]).start()

    acc = ogs[me.c].astype(F32)
    for j in range(1, me.chips):
        remote(ogs.at[0], ogpl.at[j], o2s.at[j], o2r.at[j], sib).wait()
        acc = acc + ogpl[j].astype(F32)
    ogc[...] = acc.astype(BF)
    for j in range(1, seq):
        to = lax.rem(me.s + j, seq)
        src = ogc.at[pl.ds(pl.multiple_of(to * wr, wr), wr), :]
        remote(src, ogz.at[j], o3s.at[j], o3r.at[j], (me.d, to)).start()
    span_rows = 2 * cr

    tile_rows = qgt.shape[2]
    per_tile = tile_rows // span_rows

    def qkv_terms(j, carry):
        at = lax.rem(me.c // per_tile + j, width // tile_rows)
        x = xrow[:, pl.ds(pl.multiple_of(at * tile_rows, tile_rows), tile_rows)]
        for t in range(3):
            qgt[at, t] = dot(x, qgp[t], TN).astype(BF)
        for i in range(per_tile):
            chip = at * per_tile + i

            @pl.when(chip != me.c)
            def _(i=i, chip=chip):
                src = qgt.at[at, :, i * span_rows : (i + 1) * span_rows, :]
                to = (2 * chip + me.k, me.s)
                remote(src, qgpl.at[me.c], q1s.at[chip], q1r.at[me.c], to).start()

        return carry

    tiles_of = width // tile_rows
    lax.fori_loop(1, tiles_of, qkv_terms, 0)
    qkv_terms(0, 0)
    own = pl.ds(pl.multiple_of(lax.rem(me.c, per_tile) * span_rows, span_rows), span_rows)
    sums = [qgt[me.c // per_tile, t, own, :].astype(F32) for t in range(3)]
    for j in range(1, me.chips):
        chip = lax.rem(me.c + j, me.chips)
        remote(qgpl.at[chip], qgpl.at[chip], q1s.at[chip], q1r.at[chip], sib).wait()
        for t in range(3):
            sums[t] = sums[t] + qgpl[chip, t].astype(F32)
    for t in range(3):
        qgc[t] = sums[t].astype(BF)
    source = me.k * seq + me.s
    for core in range(2):
        for j in range(seq):
            to = lax.rem(me.s + j, seq)
            src = qgc.at[:, pl.ds(pl.multiple_of((core * seq + to) * wr, wr), wr), :]
            here = jnp.logical_and(core == me.k, to == me.s)

            @pl.when(jnp.logical_not(here))
            def _(src=src, core=core, to=to, j=j):
                remote(
                    src, qgz.at[source], q2s.at[core, j], q2r.at[source], (2 * me.c + core, to)
                ).start()

            @pl.when(here)
            def _(src=src):
                local(src, qgz.at[source], q2r.at[source]).start()

    dn1 = jnp.zeros((count, width), F32)
    for h in range(me.half):
        local(dnr.at[h], dnr.at[h], n2r.at[h]).wait()
        dn1 = dn1 + dnr[h].astype(F32)
    normal, scale = normalise(tok[...])
    input_grad[...] = dmid[...] + norm_back(dn1, normal, scale, ln[0:1, :])
    gain1 = jnp.sum(dn1 * normal, axis=0, keepdims=True)
    shift1 = jnp.sum(dn1, axis=0, keepdims=True)
    tiles = width // LANES
    per = me.total // tiles
    for t in range(tiles):
        lanes = slice(t * LANES, (t + 1) * LANES)
        lnp[t, 0:1, :] = gain1[:, lanes]
        lnp[t, 1:2, :] = shift1[:, lanes]
        lnp[t, 2:4, :] = ln2[0:2, lanes]
        lnp[t, 4:8, :] = ln2[2:6, lanes]

    def send_ln(j, carry):
        other = lax.rem(me.n + j, me.total)
        remote(
            lnp.at[other // per],
            lnr.at[me.n],
            lnsem.at[0],
            lnsem.at[1],
            (other // seq, lax.rem(other, seq)),
        ).start()
        return carry

    lax.fori_loop(1, me.total, send_ln, 0)
    lnr[me.n] = lnp[me.n // per]
    value = mid[...] + brsum[0].astype(F32)
    for j in range(1, me.gchips):
        remote(brsum.at[j], brr.at[j], brs.at[j], brrs.at[j], sib).wait()
        value = value + brr[j].astype(F32)
    out[...] = value
    acc = ogc[pl.ds(pl.multiple_of(me.s * wr, wr), wr), :].astype(F32)
    for j in range(1, seq):
        remote(ogz.at[j], ogz.at[j], o3s.at[j], o3r.at[j], sib).wait()
        acc = acc + ogz[j].astype(F32)
    og[...] = acc
    acc = gf[:, pl.ds(pl.multiple_of(slot * units, units), units), :].astype(F32)
    for j in range(1, slots):
        remote(fgr.at[j], fgr.at[j], gs.at[j], gr.at[j], sib).wait()
        acc = acc + fgr[j].astype(F32)
    fg[...] = acc
    for j in range(2 * seq):
        local(qgz.at[j], qgz.at[j], q2r.at[j]).wait()
    for hg in range(seq):
        core, h = hg % 2, hg // 2
        acc = qgz[core * seq + h].astype(F32)
        for r in range(1, 2):
            acc = acc + qgz[core * seq + r * me.half + h].astype(F32)
        qg[:, :, hg * block : (hg + 1) * block] = acc
    rest = lnr.at[pl.ds(0, me.total - 1)]
    remote(rest, rest, lnsem.at[0], lnsem.at[1], sib).wait()
    acc = lnr[0]
    for j in range(1, me.total):
        acc = acc + lnr[j]
    lng[...] = acc
    for hg in range(seq):
        to = (2 * me.c + hg % 2, me.k * me.half + hg // 2)
        here = jnp.logical_and(to[0] == me.d, to[1] == me.s)

        @pl.when(jnp.logical_not(here))
        def _(hg=hg):
            remote(dmix.at[hg], dmix.at[hg], dms.at[hg], dmr.at[0], sib).wait_send()

    for j in range(me.half):
        here = jnp.logical_and(owner == me.d, 2 * j + me.k == me.s)

        @pl.when(jnp.logical_not(here))
        def _(j=j):
            remote(dns.at[j], dns.at[j], n2s.at[j], n2r.at[0], sib).wait_send()

    for core in range(2):
        for j in range(seq):
            here = jnp.logical_and(core == me.k, j == 0)
            src = qgc.at[:, pl.ds(0, wr), :]

            @pl.when(jnp.logical_not(here))
            def _(src=src, core=core, j=j):
                remote(src, src, q2s.at[core, j], q2r.at[0], sib).wait_send()


def shape(dims, dtype):
    return jax.ShapeDtypeStruct(dims, dtype)


def call(kernel, name, number, operands, outs, scratch, flops):
    vmem = pl.BlockSpec(memory_space=pltpu.VMEM)
    return pl.pallas_call(
        kernel,
        out_shape=tuple(outs),
        in_specs=[vmem] * len(operands),
        out_specs=tuple([vmem] * len(outs)),
        scratch_shapes=scratch,
        compiler_params=pltpu.CompilerParams(
            collective_id=number, has_side_effects=True, vmem_limit_bytes=60 * 2**20
        ),
        cost_estimate=pl.CostEstimate(
            flops=flops, bytes_accessed=2**24, transcendentals=0
        ),
        name=name,
    )(*operands)


def body(dp, seq, tokens, ln_params, qkv_weight, out_weight, ffn_weight, lengths, cotangent):
    count, width = tokens.shape[1], tokens.shape[2]
    ranks = dp * seq
    total = count * seq
    wr = qkv_weight.shape[0]
    units = ffn_weight.shape[0]
    block = width // seq
    group = min(dp, GROUP)
    gchips, chips, slots = group // 2, dp // 2, (dp // group) * seq
    held = units * slots
    share = ln_params.shape[1]
    sem = pltpu.SemaphoreType.DMA
    vm = pltpu.VMEM
    tok = tokens.reshape(count, width)
    cot = cotangent.reshape(count, width)
    rank = lax.axis_index("dp") * seq + lax.axis_index("seq")
    fit = LANES // share
    lane = jnp.arange(LANES)
    gains = jnp.tile(ln_params.astype(BF).astype(F32), (1, fit))
    lnb = jnp.where((lane // share == rank % fit)[None, :], gains, 0.0)
    lnb = jnp.pad(lnb, ((0, 4), (0, 0)))
    lens = jnp.pad(lengths, ((0, 7), (0, LANES - lengths.shape[1])))
    wq = qkv_weight.astype(BF).transpose(1, 0, 2)
    wo = out_weight.astype(BF)
    wf = ffn_weight.astype(BF).transpose(1, 0, 2)

    xrow, wq_full, wo_full, ln, lens_pair, dyb_all = call(
        functools.partial(gather_kernel, dp, seq),
        "gather",
        1,
        (tok, lnb, lens, wq, wo, cot),
        (
            shape((total, width), BF),
            shape((3, width, block), BF),
            shape((width, width), BF),
            shape((8, width), F32),
            shape((2, 8, LANES), jnp.int32),
            shape((group, count, width), BF),
        ),
        [
            vm((ranks, 8, LANES), F32),
            vm((3, wr * seq, 2 * block), BF),
            vm((count, width), BF),
            vm((count, width), BF),
            sem((2,)),
            sem((2,)),
            sem((4,)),
            sem((seq,)),
            sem((seq,)),
            sem((dp,)),
            sem((dp,)),
            sem((seq,)),
            sem((seq,)),
            sem((chips,)),
            sem((chips,)),
            sem((chips,)),
            sem((chips,)),
            sem((seq, 2)),
            sem((seq,)),
            sem((seq,)),
            sem((seq,)),
            sem((gchips,)),
            sem((gchips,)),
            sem((gchips,)),
            sem((gchips,)),
        ],
        10**6,
    )
    q, k, v, lse, cosine, sine, seg_col, seg_row, mixed_in, wf_full = call(
        functools.partial(attend_kernel, dp, seq, lengths.shape[1]),
        "attend",
        2,
        (xrow, wq_full, lens_pair, wf),
        (
            shape((total, block), BF),
            shape((total, block), BF),
            shape((total, block), BF),
            shape((total, LANES), F32),
            shape((total, LANES), F32),
            shape((total, LANES), F32),
            shape((total, LANES), jnp.int32),
            shape((8, total), jnp.int32),
            shape((seq, count, block), BF),
            shape((3, held, width), BF),
        ),
        [
            vm((seq, count, block), BF),
            sem((seq,)),
            sem((seq,)),
            sem((slots,)),
            sem((slots,)),
            sem((1,)),
        ],
        4 * 10**9,
    )
    mid, dmid, ln2, brsum, gf = call(
        functools.partial(ffn_kernel, dp, seq),
        "ffn",
        3,
        (tok, mixed_in, wo_full, ln, dyb_all, wf_full, cot),
        (
            shape((count, width), F32),
            shape((count, width), F32),
            shape((8, width), F32),
            shape((gchips, count, width), BF),
            shape((3, held, width), BF),
        ),
        [
            vm((count, width), BF),
            vm((gchips, 2, count, width), BF),
            vm((group * count, held), BF),
            vm((group * count, held), BF),
            vm((group * count, held), BF),
            vm((gchips, 2, count, width), BF),
            vm((gchips, count, width), BF),
            vm((gchips, count, width), BF),
            vm((gchips, count, width), BF),
            vm((gchips, 2, count, width), BF),
            vm((gchips, count, width), BF),
            vm((count, width), F32),
            vm((count, LANES), F32),
            sem((1,)),
        ]
        + [sem((gchips,))] * 10,
        20 * 10**9,
    )
    out, input_grad, lng, qg, og, fg = call(
        functools.partial(back_kernel, dp, seq),
        "back",
        4,
        (
            tok,
            mid,
            dmid,
            ln,
            ln2,
            brsum,
            gf,
            mixed_in,
            wo_full,
            wq_full,
            xrow,
            q,
            k,
            v,
            lse,
            cosine,
            sine,
            seg_col,
            seg_row,
        ),
        (
            shape((count, width), F32),
            shape((count, width), F32),
            shape((8, LANES), F32),
            shape((3, wr, width), F32),
            shape((wr, width), F32),
            shape((3, units, width), F32),
        ),
        [
            vm((seq, count, block), BF),
            vm((seq, count, block), BF),
            vm((gchips, count, width), BF),
            vm((2, chips, wr * seq, width), BF),
            vm((chips, wr * seq, width), BF),
            vm((chips, wr * seq, width), BF),
            vm((chips, wr * seq, width), BF),
            vm((wr * seq, width), BF),
            vm((seq, wr, width), BF),
            vm((total, block), F32),
            vm((total, block), F32),
            vm((total, block), F32),
            vm((2, seq // 2, count, width), BF),
            vm((seq // 2, count, width), BF),
            vm((seq // 2, count, width), BF),
            vm((seq // 2, count, width), BF),
            vm((3, total, block), BF),
            vm((width // block, 3, block, block), BF),
            vm((chips, 3, 2 * wr * seq, block), BF),
            vm((3, 2 * wr * seq, block), BF),
            vm((2 * seq, 3, wr, block), BF),
            vm((slots, 3, units, width), BF),
            vm((width // LANES, 8, LANES), F32),
            vm((ranks, 8, LANES), F32),
            sem((1,)),
            sem((seq,)),
            sem((seq,)),
            sem((gchips,)),
            sem((gchips,)),
            sem((slots,)),
            sem((slots,)),
            sem((2,)),
            sem((chips,)),
            sem((chips,)),
            sem((seq,)),
            sem((seq,)),
            sem((2,)),
            sem((seq,)),
            sem((seq,)),
            sem((chips,)),
            sem((chips,)),
            sem((2, seq)),
            sem((2 * seq,)),
            sem((2,)),
        ],
        8 * 10**9,
    )
    first = (rank % fit) * share
    ln_grad = lax.dynamic_slice(lng, (0, first), (4, share))
    return (
        out.reshape(1, count, width),
        input_grad.reshape(1, count, width),
        ln_grad,
        qg.transpose(1, 0, 2),
        og,
        fg.transpose(1, 0, 2),
    )


def solution(mesh):
    dp, seq = mesh.shape["dp"], mesh.shape["seq"]
    both = ("dp", "seq")
    in_specs = (
        P("dp", "seq", None),
        P(None, both),
        P(both, None, None),
        P(both, None),
        P(both, None, None),
        P("dp", None),
        P("dp", "seq", None),
    )
    out_specs = (
        P("dp", "seq", None),
        P("dp", "seq", None),
        P(None, both),
        P(both, None, None),
        P(both, None),
        P(both, None, None),
    )
    return jax.shard_map(
        functools.partial(body, dp, seq),
        mesh=mesh,
        in_specs=in_specs,
        out_specs=out_specs,
        check_vma=False,
    )
```

```python
import functools
import math

import jax
import jax.numpy as jnp
from jax import lax
from jax.experimental import pallas as pl
from jax.experimental.pallas import tpu as pltpu
from jax.sharding import PartitionSpec as P

HEAD_DIM = 64
GROUP = 8
LANES = 128
BF = jnp.bfloat16
F32 = jnp.float32
MESH = pl.DeviceIdType.MESH
NT = (((1,), (1,)), ((), ()))
NN = (((1,), (0,)), ((), ()))
TN = (((0,), (0,)), ((), ()))
EPS = 1e-05


def dot(a, b, dims):
    return lax.dot_general(a, b, dims, preferred_element_type=F32)


def remote(src, dst, send, recv, device):
    return pltpu.make_async_remote_copy(
        src_ref=src, dst_ref=dst, send_sem=send, recv_sem=recv, device_id=device, device_id_type=MESH
    )


def local(src, dst, sem):
    return pltpu.make_async_copy(src, dst, sem)


def greet(peers):
    barrier = pltpu.get_barrier_semaphore()
    for peer in peers:
        pl.semaphore_signal(barrier, inc=1, device_id=peer, device_id_type=MESH)
    pl.semaphore_wait(barrier, len(peers))


def greet_all(dp, seq):
    barrier = pltpu.get_barrier_semaphore()
    total = dp * seq
    me = lax.axis_index("dp") * seq + lax.axis_index("seq")

    def hello(j, carry):
        other = lax.rem(me + j, total)
        pl.semaphore_signal(
            barrier, inc=1, device_id=(other // seq, lax.rem(other, seq)), device_id_type=MESH
        )
        return carry

    lax.fori_loop(1, total, hello, 0)
    pl.semaphore_wait(barrier, total - 1)


class Place:
    def __init__(self, dp, seq):
        self.dp, self.seq = dp, seq
        self.d, self.s = lax.axis_index("dp"), lax.axis_index("seq")
        self.c, self.k = self.d // 2, lax.rem(self.d, 2)
        self.sib = self.d + 1 - 2 * self.k
        self.chips = dp // 2
        self.group = min(dp, GROUP)
        self.groups = dp // self.group
        self.g, self.p = self.d // self.group, lax.rem(self.d, self.group)
        self.gc = self.p // 2
        self.gchips = self.group // 2
        self.half = seq // 2
        self.r, self.h = self.s // self.half, lax.rem(self.s, self.half)
        self.hg = 2 * self.h + self.k
        self.n = self.d * seq + self.s
        self.total = dp * seq

    def in_group(self, chip, core):
        return self.g * self.group + 2 * chip + core


def normalise(value):
    mean = jnp.mean(value, axis=-1, keepdims=True)
    centred = value - mean
    var = jnp.mean(centred * centred, axis=-1, keepdims=True)
    scale = lax.rsqrt(var + EPS)
    return centred * scale, scale


def norm_back(grad, normal, scale, gain):
    scaled = grad * gain
    return scale * (
        scaled
        - jnp.mean(scaled, axis=-1, keepdims=True)
        - normal * jnp.mean(scaled * normal, axis=-1, keepdims=True)
    )


def gather_kernel(
    dp,
    seq,
    tok,
    lnb,
    lens,
    wq,
    wo,
    cot,
    xrow,
    wq_full,
    wo_full,
    ln_out,
    lens_pair,
    dyb_all,
    ln_own,
    ln_all,
    wcol,
    xown,
    dyb,
    ln_sem,
    len_sem,
    loc,
    wq1s,
    wq1r,
    wq2s,
    wq2r,
    wo1s,
    wo1r,
    wo2s,
    wo2r,
    wo3s,
    wo3r,
    xs,
    xr,
    xfs,
    xfr,
    dys,
    dyr,
    dyfs,
    dyfr,
):
    me = Place(dp, seq)
    count, width = tok.shape
    wr = wo.shape[0]
    cr = wr * seq
    pair = wcol.shape[2]
    head = pair // 2
    halfrows = count // 2
    dyb[...] = cot[...].astype(BF)
    low = lnb[...].astype(BF).astype(F32)
    ln_own[...] = low
    ln_all[me.n] = low
    lens_pair[me.k] = lens[...]
    greet_all(dp, seq)

    def send_ln(j, carry):
        other = lax.rem(me.n + j, me.total)
        remote(
            ln_own, ln_all.at[me.n], ln_sem.at[0], ln_sem.at[1], (other // seq, lax.rem(other, seq))
        ).start()
        return carry

    lax.fori_loop(1, me.total, send_ln, 0)
    len_copy = remote(
        lens, lens_pair.at[me.k], len_sem.at[0], len_sem.at[1], (me.sib, me.s)
    )
    len_copy.start()
    row0 = pl.multiple_of(me.s * wr, wr)
    out0 = pl.multiple_of(me.n * wr, wr)
    wq_first, wo_first = [], []
    for j in range(1, seq):
        to = lax.rem(me.s + j, seq)
        col = pl.multiple_of(lax.rem(to, me.half) * pair, pair)
        wq_first.append(
            remote(
                wq.at[:, :, pl.ds(col, pair)],
                wcol.at[:, pl.ds(row0, wr), :],
                wq1s.at[j],
                wq1r.at[j],
                (me.d, to),
            )
        )
    for copy in wq_first:
        copy.start()
    own_col = pl.multiple_of(me.h * pair, pair)
    own_wq = local(wq.at[:, :, pl.ds(own_col, pair)], wcol.at[:, pl.ds(row0, wr), :], loc.at[0])
    own_wq.start()
    own_wo = local(wo, wo_full.at[pl.ds(out0, wr), :], loc.at[1])
    own_wo.start()
    own_dy = local(dyb, dyb_all.at[me.p], loc.at[2])
    own_dy.start()
    normal, _ = normalise(tok[...])
    remote(
        ln_all.at[pl.ds(0, me.total - 1)],
        ln_all.at[pl.ds(0, me.total - 1)],
        ln_sem.at[0],
        ln_sem.at[1],
        (me.sib, me.s),
    ).wait()
    tiles = width // LANES
    per = me.total // tiles
    for t in range(tiles):
        part = ln_all[t * per]
        for i in range(1, per):
            part = part + ln_all[t * per + i]
        ln_out[:, t * LANES : (t + 1) * LANES] = part
    xown[...] = (normal * ln_out[0:1, :] + ln_out[1:2, :]).astype(BF)
    rows0 = pl.multiple_of(me.s * count, count)
    for j in range(me.half):
        to = me.k * me.half + lax.rem(me.h + j, me.half)
        for core in range(2):
            src = xown.at[pl.ds(core * halfrows, halfrows), :]
            dst = xrow.at[pl.ds(rows0 + core * halfrows, halfrows), :]
            here = jnp.logical_and(to == me.s, core == me.k)

            @pl.when(jnp.logical_not(here))
            def _(src=src, dst=dst, core=core, to=to, j=j):
                remote(src, dst, xs.at[j, core], xr.at[me.s], (2 * me.c + core, to)).start()

            @pl.when(here)
            def _(src=src, dst=dst):
                local(src, dst, xr.at[me.s]).start()

    for j in range(1, seq):
        to = lax.rem(me.s + j, seq)
        wo_first.append(
            remote(wo, wo_full.at[pl.ds(out0, wr), :], wo1s.at[j], wo1r.at[j], (me.d, to))
        )
    for copy in wo_first:
        copy.start()
    for copy in wq_first:
        copy.wait()
    own_wq.wait()
    crow0 = pl.multiple_of(me.d * cr, cr)

    def send_wq(j, carry):
        to = lax.rem(me.d + j, dp)
        col = pl.multiple_of(lax.rem(to, 2) * head, head)
        remote(
            wcol.at[:, :, pl.ds(col, head)],
            wq_full.at[:, pl.ds(crow0, cr), :],
            wq2s.at[j],
            wq2r.at[j],
            (to, me.s),
        ).start()
        return carry

    lax.fori_loop(1, dp, send_wq, 0)
    own_half = local(
        wcol.at[:, :, pl.ds(pl.multiple_of(me.k * head, head), head)],
        wq_full.at[:, pl.ds(crow0, cr), :],
        loc.at[3],
    )
    own_half.start()
    for copy in wo_first:
        copy.wait()
    own_wo.wait()
    mine = wo_full.at[pl.ds(crow0, cr), :]
    wo_sends = [remote(mine, mine, wo3s.at[0], wo3r.at[0], (me.sib, me.s))]
    for j in range(1, me.chips):
        to = 2 * lax.rem(me.c + j, me.chips) + me.k
        wo_sends.append(remote(mine, mine, wo2s.at[j], wo2r.at[j], (to, me.s)))
    dy_sends = [remote(dyb, dyb_all.at[me.p], dyfs.at[0], dyfr.at[0], (me.sib, me.s))]
    for j in range(1, me.gchips):
        to = me.in_group(lax.rem(me.gc + j, me.gchips), me.k)
        dy_sends.append(remote(dyb, dyb_all.at[me.p], dys.at[j], dyr.at[j], (to, me.s)))
    for copy in wo_sends + dy_sends:
        copy.start()
    for j in range(seq):
        source = lax.rem(me.s + j, seq)
        part = xrow.at[pl.ds(pl.multiple_of(source * count + me.k * halfrows, halfrows), halfrows), :]
        local(part, part, xr.at[source]).wait()
        remote(part, part, xfs.at[j], xfr.at[j], (me.sib, me.s)).start()
    for j in range(1, me.chips):
        source = 2 * lax.rem(me.c + me.chips - j, me.chips) + me.k
        part = wo_full.at[pl.ds(pl.multiple_of(source * cr, cr), cr), :]
        remote(part, part, wo2s.at[j], wo2r.at[j], (me.sib, me.s)).wait_recv()
        remote(part, part, wo3s.at[j], wo3r.at[j], (me.sib, me.s)).start()
    for j in range(1, me.gchips):
        source = 2 * lax.rem(me.gc + me.gchips - j, me.gchips) + me.k
        part = dyb_all.at[source]
        remote(part, part, dys.at[j], dyr.at[j], (me.sib, me.s)).wait_recv()
        remote(part, part, dyfs.at[j], dyfr.at[j], (me.sib, me.s)).start()
    for j in range(me.half):
        to = me.k * me.half + lax.rem(me.h + j, me.half)
        for core in range(2):
            src = xown.at[pl.ds(core * halfrows, halfrows), :]
            here = jnp.logical_and(to == me.s, core == me.k)

            @pl.when(jnp.logical_not(here))
            def _(src=src, j=j, core=core):
                remote(src, src, xs.at[j, core], xr.at[0], (me.sib, me.s)).wait_send()

    for j in range(seq):
        part = xrow.at[pl.ds(0, halfrows), :]
        remote(part, part, xfs.at[j], xfr.at[j], (me.sib, me.s)).wait()

    def wait_wq(j, carry):
        part = wq_full.at[:, pl.ds(0, cr), :]
        remote(part, part, wq2s.at[j], wq2r.at[j], (me.sib, me.s)).wait()
        return carry

    lax.fori_loop(1, dp, wait_wq, 0)
    own_half.wait()
    own_dy.wait()
    len_copy.wait()
    for j in range(1, me.chips):
        remote(mine, mine, wo2s.at[j], wo2r.at[j], (me.sib, me.s)).wait_send()
        remote(mine, mine, wo3s.at[j], wo3r.at[j], (me.sib, me.s)).wait()
    remote(mine, mine, wo3s.at[0], wo3r.at[0], (me.sib, me.s)).wait()
    for j in range(1, me.gchips):
        remote(dyb, dyb, dys.at[j], dyr.at[j], (me.sib, me.s)).wait_send()
        remote(dyb, dyb, dyfs.at[j], dyfr.at[j], (me.sib, me.s)).wait()
    remote(dyb, dyb, dyfs.at[0], dyfr.at[0], (me.sib, me.s)).wait()


def swap_halves(value):
    half = HEAD_DIM // 2
    width = value.shape[1]
    lane = lax.broadcasted_iota(jnp.int32, value.shape, 1)
    up = pltpu.roll(value, width - half, 1)
    down = pltpu.roll(value, half, 1)
    return jnp.where(lax.rem(lane, HEAD_DIM) < half, up, down)


def head_mask(shape, h):
    lane = lax.broadcasted_iota(jnp.int32, shape, 1)
    return jnp.logical_and(lane >= h * HEAD_DIM, lane < (h + 1) * HEAD_DIM)


def attend_kernel(
    dp,
    seq,
    segs,
    xrow,
    wq,
    lens,
    wf,
    q_out,
    k_out,
    v_out,
    lse_out,
    cos_out,
    sin_out,
    seg_col,
    seg_row,
    mixed_in,
    wf_full,
    mixed,
    ms,
    mr,
    fs,
    fr,
    loc,
):
    me = Place(dp, seq)
    total = xrow.shape[0]
    count = total // seq
    width = wq.shape[2]
    heads = width // HEAD_DIM
    units = wf.shape[1]
    slots = me.groups * seq
    slot = me.g * seq + me.s
    greet_all(dp, seq)
    mine = wf_full.at[:, pl.ds(pl.multiple_of(slot * units, units), units), :]
    own_wf = local(wf, mine, loc.at[0])
    own_wf.start()
    for j in range(1, slots):
        other = lax.rem(slot + j, slots)
        to = ((other // seq) * me.group + me.p, lax.rem(other, seq))
        remote(wf, mine, fs.at[j], fr.at[j], to).start()
    row = lens[me.r]
    place_row = lax.broadcasted_iota(jnp.int32, (8, total), 1)
    place_col = lax.broadcasted_iota(jnp.int32, (total, LANES), 0)
    end = jnp.zeros((1, 1), jnp.int32)
    segr = jnp.zeros((8, total), jnp.int32)
    segc = jnp.zeros((total, LANES), jnp.int32)
    start = jnp.zeros((total, LANES), jnp.int32)
    for j in range(segs):
        length = row[0:1, j : j + 1]
        end = end + length
        segr = segr + (place_row >= end).astype(jnp.int32)
        past = place_col >= end
        segc = segc + past.astype(jnp.int32)
        start = start + jnp.where(past, length, 0)
    seg_row[...] = segr
    seg_col[...] = segc
    half = HEAD_DIM // 2
    lane = lax.broadcasted_iota(jnp.int32, (1, LANES), 1)
    rate = jnp.exp(lax.rem(lane, half).astype(F32) * (-math.log(10000.0) / half))
    angle = (place_col - start).astype(F32) * rate
    cos_out[...] = jnp.cos(angle)
    sign = jnp.where(lax.rem(lane, HEAD_DIM) < half, -1.0, 1.0)
    sin_out[...] = jnp.sin(angle) * sign

    def project(i, carry):
        rows = pl.ds(pl.multiple_of(i * count, count), count)
        x = xrow[rows, :]
        cosine = jnp.concatenate([cos_out[rows, :]] * (width // LANES), axis=1)
        sine = jnp.concatenate([sin_out[rows, :]] * (width // LANES), axis=1)
        raw = dot(x, wq[0], NN)
        q_out[rows, :] = (raw * cosine + swap_halves(raw) * sine).astype(BF)
        raw = dot(x, wq[1], NN)
        k_out[rows, :] = (raw * cosine + swap_halves(raw) * sine).astype(BF)
        v_out[rows, :] = dot(x, wq[2], NN).astype(BF)
        return carry

    lax.fori_loop(0, seq, project, 0)

    def chunk(step, carry):
        i = lax.rem(me.s + step, seq)
        rows = pl.ds(pl.multiple_of(i * count, count), count)
        q = q_out[rows, :]
        bias = jnp.where(seg_col[rows, 0:1] == seg_row[0:1, :], 0.0, -1e30)
        lane = lax.broadcasted_iota(jnp.int32, (count, LANES), 1)
        lse = jnp.zeros((count, LANES), F32)
        out = jnp.zeros((count, width), F32)
        for h in range(heads):
            mask = head_mask((count, width), h)
            score = dot(jnp.where(mask, q, jnp.zeros_like(q)), k_out[...], NT) * 0.125 + bias
            top = jnp.max(score, axis=1, keepdims=True)
            weight = jnp.exp(score - top)
            tally = jnp.sum(weight, axis=1, keepdims=True)
            prob = (weight * (1.0 / tally)).astype(BF)
            out = jnp.where(mask, dot(prob, v_out[...], NN), out)
            lse = jnp.where(lane == h, top + jnp.log(tally), lse)
        lse_out[rows, :] = lse
        mixed[i] = out.astype(BF)
        owner = 2 * me.c + me.r
        here = jnp.logical_and(i == me.s, owner == me.d)

        @pl.when(jnp.logical_not(here))
        def _():
            remote(mixed.at[i], mixed_in.at[me.hg], ms.at[i], mr.at[me.hg], (owner, i)).start()

        @pl.when(here)
        def _():
            local(mixed.at[i], mixed_in.at[me.hg], mr.at[me.hg]).start()

        return carry

    lax.fori_loop(0, seq, chunk, 0)
    for j in range(seq):
        local(mixed.at[j], mixed_in.at[j], mr.at[j]).wait()
        here = jnp.logical_and(j == me.s, me.r == me.k)

        @pl.when(jnp.logical_not(here))
        def _(j=j):
            remote(mixed.at[j], mixed.at[j], ms.at[j], mr.at[j], (me.sib, me.s)).wait_send()

    own_wf.wait()
    for j in range(1, slots):
        remote(wf, mine, fs.at[j], fr.at[j], (me.sib, me.s)).wait()


def ffn_kernel(
    dp,
    seq,
    tok,
    mixed_in,
    wo,
    ln,
    dyb_all,
    wf,
    cot,
    mid_out,
    dmid_out,
    ln2_out,
    br_out,
    gf_out,
    xn2,
    xall,
    hid,
    dg,
    du,
    dpart,
    dsib,
    dsum,
    drecv,
    bpart,
    bsib,
    normal2,
    scale2,
    loc,
    xs,
    xr,
    xfs,
    xfr,
    dss,
    dsr,
    dps,
    dpr,
    bss,
    bsr,
):
    me = Place(dp, seq)
    count, width = tok.shape
    units = wf.shape[1]
    nc = me.gchips
    tile = min(256, units)
    cols = 256
    sib = (me.sib, me.s)
    mid = tok[...]
    block = mixed_in.shape[2]
    for h in range(mixed_in.shape[0]):
        mid = mid + dot(mixed_in[h], wo[h * block : (h + 1) * block, :], NN)
    mid_out[...] = mid
    normal, scale = normalise(mid)
    normal2[...] = normal
    scale2[...] = jnp.broadcast_to(scale, scale2.shape)
    low = (normal * ln[2:3, :] + ln[3:4, :]).astype(BF)
    xn2[...] = low
    greet([sib] + [(me.in_group(lax.rem(me.gc + j, nc), me.k), me.s) for j in range(1, nc)])
    sends = [remote(xn2, xall.at[me.gc, me.k], xfs.at[0], xfr.at[0], sib)]
    for j in range(1, nc):
        to = me.in_group(lax.rem(me.gc + j, nc), me.k)
        sends.append(remote(xn2, xall.at[me.gc, me.k], xs.at[j], xr.at[j], (to, me.s)))
    for copy in sends:
        copy.start()
    xall[me.gc, me.k] = low

    def chip(j, carry):
        cj = lax.rem(me.gc + nc - j, nc)

        @pl.when(j > 0)
        def _():
            part = xall.at[cj, me.k]
            remote(part, part, xs.at[j], xr.at[j], sib).wait_recv()
            remote(part, part, xfs.at[j], xfr.at[j], sib).start()

        theirs = xall.at[cj, 1 - me.k]
        remote(theirs, theirs, xfs.at[j], xfr.at[j], sib).wait_recv()
        rows = pl.ds(pl.multiple_of(cj * 2 * count, 2 * count), 2 * count)
        x = xall[cj].reshape(2 * count, width)
        dy = dyb_all[pl.ds(2 * cj, 2)].reshape(2 * count, width)
        for t in range(units // tile):
            span = slice(t * tile, (t + 1) * tile)
            gate = dot(x, wf[0, span, :], NT)
            up = dot(x, wf[1, span, :], NT)
            dh = dot(dy, wf[2, span, :], NT)
            sigma = 1.0 / (1.0 + jnp.exp(-gate))
            active = gate * sigma
            hid[rows, span] = (active * up).astype(BF)
            dg[rows, span] = (dh * up * (sigma * (1.0 + gate * (1.0 - sigma)))).astype(BF)
            du[rows, span] = (dh * active).astype(BF)
        for t in range(width // cols):
            span = slice(t * cols, (t + 1) * cols)
            value = dot(dg[rows, :], wf[0, :, span], NN) + dot(du[rows, :], wf[1, :, span], NN)
            dpart[j, :, :, span] = value.astype(BF).reshape(2, count, cols)
        remote(dpart.at[j, 1 - me.k], dsib.at[j], dss.at[j], dsr.at[j], sib).start()
        for t in range(width // cols):
            span = slice(t * cols, (t + 1) * cols)
            value = dot(hid[rows, :], wf[2, :, span], NN)
            bpart[j, :, :, span] = value.astype(BF).reshape(2, count, cols)
        remote(bpart.at[j, 1 - me.k], bsib.at[j], bss.at[j], bsr.at[j], sib).start()
        remote(dsib.at[j], dsib.at[j], dss.at[j], dsr.at[j], sib).wait()
        dsum[j] = (dpart[j, me.k].astype(F32) + dsib[j].astype(F32)).astype(BF)

        @pl.when(j > 0)
        def _():
            remote(
                dsum.at[j], drecv.at[j], dps.at[j], dpr.at[j], (me.in_group(cj, me.k), me.s)
            ).start()

        return carry

    lax.fori_loop(0, nc, chip, 0)

    def grads(t, carry):
        span = pl.ds(pl.multiple_of(t * tile, tile), tile)
        x = xall[...].reshape(nc * 2 * count, width)
        dy = dyb_all[...].reshape(nc * 2 * count, width)
        gf_out[0, span, :] = dot(dg[:, span], x, TN).astype(BF)
        gf_out[1, span, :] = dot(du[:, span], x, TN).astype(BF)
        gf_out[2, span, :] = dot(hid[:, span], dy, TN).astype(BF)
        return carry

    lax.fori_loop(0, units // tile, grads, 0)
    for j in range(nc):
        remote(bsib.at[j], bsib.at[j], bss.at[j], bsr.at[j], sib).wait()
        br_out[j] = (bpart[j, me.k].astype(F32) + bsib[j].astype(F32)).astype(BF)
        remote(xn2, xn2, xfs.at[j], xfr.at[j], sib).wait_send()
    dn2 = dsum[0].astype(F32)
    for j in range(1, nc):
        remote(dsum.at[j], drecv.at[j], dps.at[j], dpr.at[j], sib).wait()
        remote(xn2, xn2, xs.at[j], xr.at[j], sib).wait_send()
        dn2 = dn2 + drecv[j].astype(F32)
    normal = normal2[...]
    dmid_out[...] = cot[...] + norm_back(dn2, normal, scale2[:, 0:1], ln[2:3, :])
    ln2_out[0:1, :] = jnp.sum(dn2 * normal, axis=0, keepdims=True)
    ln2_out[1:2, :] = jnp.sum(dn2, axis=0, keepdims=True)
    ln2_out[2:8, :] = jnp.zeros((6, width), F32)


def back_kernel(
    dp,
    seq,
    tok,
    mid,
    dmid,
    ln,
    ln2,
    brsum,
    gf,
    mixed_in,
    wo,
    wq,
    xrow,
    q_in,
    k_in,
    v_in,
    lse_in,
    cos_in,
    sin_in,
    seg_col,
    seg_row,
    out,
    input_grad,
    lng,
    qg,
    og,
    fg,
    dmix,
    dmix_row,
    brr,
    ogp,
    ogsib,
    ogs,
    ogpl,
    ogc,
    ogz,
    dq,
    dk,
    dv,
    dnp,
    dnsib,
    dns,
    dnr,
    qgp,
    qgt,
    qgpl,
    qgc,
    qgz,
    fgr,
    lnp,
    lnr,
    loc,
    dms,
    dmr,
    brs,
    brrs,
    gs,
    gr,
    o1,
    o2s,
    o2r,
    o3s,
    o3r,
    n1,
    n2s,
    n2r,
    q1s,
    q1r,
    q2s,
    q2r,
    lnsem,
):
    me = Place(dp, seq)
    count, width = tok.shape
    total = xrow.shape[0]
    block = q_in.shape[1]
    heads = block // HEAD_DIM
    wr = og.shape[0]
    cr = wr * seq
    units = fg.shape[1]
    slots = me.groups * seq
    slot = me.g * seq + me.s
    sib = (me.sib, me.s)
    greet_all(dp, seq)
    dmb = dmid[...].astype(BF)
    for hg in range(seq):
        dmix[hg] = dot(dmb, wo[hg * block : (hg + 1) * block, :], NT).astype(BF)
        to = (2 * me.c + hg % 2, me.k * me.half + hg // 2)
        here = jnp.logical_and(to[0] == me.d, to[1] == me.s)
        src, dst = dmix.at[hg], dmix_row.at[me.s]

        @pl.when(jnp.logical_not(here))
        def _(src=src, dst=dst, hg=hg, to=to):
            remote(src, dst, dms.at[hg], dmr.at[me.s], to).start()

        @pl.when(here)
        def _(src=src, dst=dst):
            local(src, dst, dmr.at[me.s]).start()

    for j in range(1, me.gchips):
        to = me.in_group(lax.rem(me.gc + me.gchips - j, me.gchips), me.k)
        remote(brsum.at[j], brr.at[j], brs.at[j], brrs.at[j], (to, me.s)).start()
    for j in range(1, slots):
        other = lax.rem(slot + j, slots)
        to = ((other // seq) * me.group + me.p, lax.rem(other, seq))
        src = gf.at[:, pl.ds(pl.multiple_of(other * units, units), units), :]
        remote(src, fgr.at[j], gs.at[j], gr.at[j], to).start()
    for h in range(seq):
        part = dot(mixed_in[h], dmb, TN).astype(BF)
        for t in range(block // cr):
            first = h * (block // cr) + t
            ogp[first % 2, first // 2] = part[t * cr : (t + 1) * cr]
    remote(ogp.at[1 - me.k], ogsib, o1.at[0], o1.at[1], sib).start()
    for j in range(seq):
        local(dmix.at[j], dmix_row.at[j], dmr.at[j]).wait()
    remote(ogp.at[1 - me.k], ogsib, o1.at[0], o1.at[1], sib).wait()
    ogs[...] = (ogp[me.k].astype(F32) + ogsib[...].astype(F32)).astype(BF)

    def send_og(j, carry):
        chip = lax.rem(me.c + j, me.chips)
        remote(ogs.at[chip], ogpl.at[j], o2s.at[j], o2r.at[j], (2 * chip + me.k, me.s)).start()
        return carry

    lax.fori_loop(1, me.chips, send_og, 0)
    dk[...] = jnp.zeros_like(dk)
    dv[...] = jnp.zeros_like(dv)

    def chunk(i, carry):
        rows = pl.ds(pl.multiple_of(i * count, count), count)
        q = q_in[rows, :]
        dm = dmix_row[i]
        lse = lse_in[rows, :]
        bias = jnp.where(seg_col[rows, 0:1] == seg_row[0:1, :], 0.0, -1e30)
        grad_q = jnp.zeros((count, block), F32)
        for h in range(heads):
            mask = head_mask((count, block), h)
            qh = jnp.where(mask, q, jnp.zeros_like(q))
            dmh = jnp.where(mask, dm, jnp.zeros_like(dm))
            score = dot(qh, k_in[...], NT) * 0.125 + bias
            prob = jnp.exp(score - lse[:, h : h + 1])
            dprob = dot(dmh, v_in[...], NT)
            centre = jnp.sum(prob * dprob, axis=1, keepdims=True)
            ds = (0.125 * prob * (dprob - centre)).astype(BF)
            grad_q = jnp.where(mask, dot(ds, k_in[...], NN), grad_q)
            dk[...] += dot(ds, qh, TN)
            dv[...] += dot(prob.astype(BF), dmh, TN)
        dq[rows, :] = grad_q
        return carry

    lax.fori_loop(0, seq, chunk, 0)

    def back_chunk(i):
        rows = pl.ds(pl.multiple_of(i * count, count), count)
        cosine = jnp.concatenate([cos_in[rows, :]] * (block // LANES), axis=1)
        sine = jnp.concatenate([sin_in[rows, :]] * (block // LANES), axis=1)
        a = dq[rows, :]
        a = (a * cosine - swap_halves(a) * sine).astype(BF)
        b = dk[rows, :]
        b = (b * cosine - swap_halves(b) * sine).astype(BF)
        c = dv[rows, :].astype(BF)
        qgp[0, rows, :] = a
        qgp[1, rows, :] = b
        qgp[2, rows, :] = c
        value = dot(a, wq[0], NT) + dot(b, wq[1], NT) + dot(c, wq[2], NT)
        dnp[lax.rem(i, 2), i // 2] = value.astype(BF)

    def other_half(j, carry):
        back_chunk(2 * j + 1 - me.k)
        return carry

    def own_half(j, carry):
        back_chunk(2 * j + me.k)
        return carry

    lax.fori_loop(0, me.half, other_half, 0)
    remote(dnp.at[1 - me.k], dnsib, n1.at[0], n1.at[1], sib).start()
    lax.fori_loop(0, me.half, own_half, 0)
    remote(dnp.at[1 - me.k], dnsib, n1.at[0], n1.at[1], sib).wait()
    owner = 2 * me.c + me.r
    for j in range(me.half):
        dns[j] = (dnp[me.k, j].astype(F32) + dnsib[j].astype(F32)).astype(BF)
        i = 2 * j + me.k
        here = jnp.logical_and(owner == me.d, i == me.s)

        @pl.when(jnp.logical_not(here))
        def _(j=j, i=i):
            remote(dns.at[j], dnr.at[me.h], n2s.at[j], n2r.at[me.h], (owner, i)).start()

        @pl.when(here)
        def _(j=j):
            local(dns.at[j], dnr.at[me.h], n2r.at[me.h]).start()

    acc = ogs[me.c].astype(F32)
    for j in range(1, me.chips):
        remote(ogs.at[0], ogpl.at[j], o2s.at[j], o2r.at[j], sib).wait()
        acc = acc + ogpl[j].astype(F32)
    ogc[...] = acc.astype(BF)
    for j in range(1, seq):
        to = lax.rem(me.s + j, seq)
        src = ogc.at[pl.ds(pl.multiple_of(to * wr, wr), wr), :]
        remote(src, ogz.at[j], o3s.at[j], o3r.at[j], (me.d, to)).start()
    span_rows = 2 * cr

    tile_rows = qgt.shape[2]
    per_tile = tile_rows // span_rows

    def qkv_terms(j, carry):
        at = lax.rem(me.c // per_tile + j, width // tile_rows)
        x = xrow[:, pl.ds(pl.multiple_of(at * tile_rows, tile_rows), tile_rows)]
        for t in range(3):
            qgt[at, t] = dot(x, qgp[t], TN).astype(BF)
        for i in range(per_tile):
            chip = at * per_tile + i

            @pl.when(chip != me.c)
            def _(i=i, chip=chip):
                src = qgt.at[at, :, i * span_rows : (i + 1) * span_rows, :]
                to = (2 * chip + me.k, me.s)
                remote(src, qgpl.at[me.c], q1s.at[chip], q1r.at[me.c], to).start()

        return carry

    tiles_of = width // tile_rows
    lax.fori_loop(1, tiles_of, qkv_terms, 0)
    qkv_terms(0, 0)
    own = pl.ds(pl.multiple_of(lax.rem(me.c, per_tile) * span_rows, span_rows), span_rows)
    sums = [qgt[me.c // per_tile, t, own, :].astype(F32) for t in range(3)]
    for j in range(1, me.chips):
        chip = lax.rem(me.c + j, me.chips)
        remote(qgpl.at[chip], qgpl.at[chip], q1s.at[chip], q1r.at[chip], sib).wait()
        for t in range(3):
            sums[t] = sums[t] + qgpl[chip, t].astype(F32)
    for t in range(3):
        qgc[t] = sums[t].astype(BF)
    source = me.k * seq + me.s
    for core in range(2):
        for j in range(seq):
            to = lax.rem(me.s + j, seq)
            src = qgc.at[:, pl.ds(pl.multiple_of((core * seq + to) * wr, wr), wr), :]
            here = jnp.logical_and(core == me.k, to == me.s)

            @pl.when(jnp.logical_not(here))
            def _(src=src, core=core, to=to, j=j):
                remote(
                    src, qgz.at[source], q2s.at[core, j], q2r.at[source], (2 * me.c + core, to)
                ).start()

            @pl.when(here)
            def _(src=src):
                local(src, qgz.at[source], q2r.at[source]).start()

    dn1 = jnp.zeros((count, width), F32)
    for h in range(me.half):
        local(dnr.at[h], dnr.at[h], n2r.at[h]).wait()
        dn1 = dn1 + dnr[h].astype(F32)
    normal, scale = normalise(tok[...])
    input_grad[...] = dmid[...] + norm_back(dn1, normal, scale, ln[0:1, :])
    gain1 = jnp.sum(dn1 * normal, axis=0, keepdims=True)
    shift1 = jnp.sum(dn1, axis=0, keepdims=True)
    tiles = width // LANES
    per = me.total // tiles
    for t in range(tiles):
        lanes = slice(t * LANES, (t + 1) * LANES)
        lnp[t, 0:1, :] = gain1[:, lanes]
        lnp[t, 1:2, :] = shift1[:, lanes]
        lnp[t, 2:4, :] = ln2[0:2, lanes]
        lnp[t, 4:8, :] = ln2[2:6, lanes]

    def send_ln(j, carry):
        other = lax.rem(me.n + j, me.total)
        remote(
            lnp.at[other // per],
            lnr.at[me.n],
            lnsem.at[0],
            lnsem.at[1],
            (other // seq, lax.rem(other, seq)),
        ).start()
        return carry

    lax.fori_loop(1, me.total, send_ln, 0)
    lnr[me.n] = lnp[me.n // per]
    value = mid[...] + brsum[0].astype(F32)
    for j in range(1, me.gchips):
        remote(brsum.at[j], brr.at[j], brs.at[j], brrs.at[j], sib).wait()
        value = value + brr[j].astype(F32)
    out[...] = value
    acc = ogc[pl.ds(pl.multiple_of(me.s * wr, wr), wr), :].astype(F32)
    for j in range(1, seq):
        remote(ogz.at[j], ogz.at[j], o3s.at[j], o3r.at[j], sib).wait()
        acc = acc + ogz[j].astype(F32)
    og[...] = acc
    acc = gf[:, pl.ds(pl.multiple_of(slot * units, units), units), :].astype(F32)
    for j in range(1, slots):
        remote(fgr.at[j], fgr.at[j], gs.at[j], gr.at[j], sib).wait()
        acc = acc + fgr[j].astype(F32)
    fg[...] = acc
    for j in range(2 * seq):
        local(qgz.at[j], qgz.at[j], q2r.at[j]).wait()
    for hg in range(seq):
        core, h = hg % 2, hg // 2
        acc = qgz[core * seq + h].astype(F32)
        for r in range(1, 2):
            acc = acc + qgz[core * seq + r * me.half + h].astype(F32)
        qg[:, :, hg * block : (hg + 1) * block] = acc
    rest = lnr.at[pl.ds(0, me.total - 1)]
    remote(rest, rest, lnsem.at[0], lnsem.at[1], sib).wait()
    acc = lnr[0]
    for j in range(1, me.total):
        acc = acc + lnr[j]
    lng[...] = acc
    for hg in range(seq):
        to = (2 * me.c + hg % 2, me.k * me.half + hg // 2)
        here = jnp.logical_and(to[0] == me.d, to[1] == me.s)

        @pl.when(jnp.logical_not(here))
        def _(hg=hg):
            remote(dmix.at[hg], dmix.at[hg], dms.at[hg], dmr.at[0], sib).wait_send()

    for j in range(me.half):
        here = jnp.logical_and(owner == me.d, 2 * j + me.k == me.s)

        @pl.when(jnp.logical_not(here))
        def _(j=j):
            remote(dns.at[j], dns.at[j], n2s.at[j], n2r.at[0], sib).wait_send()

    for core in range(2):
        for j in range(seq):
            here = jnp.logical_and(core == me.k, j == 0)
            src = qgc.at[:, pl.ds(0, wr), :]

            @pl.when(jnp.logical_not(here))
            def _(src=src, core=core, j=j):
                remote(src, src, q2s.at[core, j], q2r.at[0], sib).wait_send()


def shape(dims, dtype):
    return jax.ShapeDtypeStruct(dims, dtype)


def call(kernel, name, number, operands, outs, scratch, flops):
    vmem = pl.BlockSpec(memory_space=pltpu.VMEM)
    return pl.pallas_call(
        kernel,
        out_shape=tuple(outs),
        in_specs=[vmem] * len(operands),
        out_specs=tuple([vmem] * len(outs)),
        scratch_shapes=scratch,
        compiler_params=pltpu.CompilerParams(
            collective_id=number, has_side_effects=True, vmem_limit_bytes=60 * 2**20
        ),
        cost_estimate=pl.CostEstimate(
            flops=flops, bytes_accessed=2**24, transcendentals=0
        ),
        name=name,
    )(*operands)


def body(dp, seq, tokens, ln_params, qkv_weight, out_weight, ffn_weight, lengths, cotangent):
    count, width = tokens.shape[1], tokens.shape[2]
    ranks = dp * seq
    total = count * seq
    wr = qkv_weight.shape[0]
    units = ffn_weight.shape[0]
    block = width // seq
    group = min(dp, GROUP)
    gchips, chips, slots = group // 2, dp // 2, (dp // group) * seq
    held = units * slots
    share = ln_params.shape[1]
    sem = pltpu.SemaphoreType.DMA
    vm = pltpu.VMEM
    tok = tokens.reshape(count, width)
    cot = cotangent.reshape(count, width)
    rank = lax.axis_index("dp") * seq + lax.axis_index("seq")
    fit = LANES // share
    lane = jnp.arange(LANES)
    gains = jnp.tile(ln_params, (1, fit))
    lnb = jnp.where((lane // share == rank % fit)[None, :], gains, 0.0)
    lnb = jnp.pad(lnb, ((0, 4), (0, 0)))
    lens = jnp.pad(lengths, ((0, 7), (0, LANES - lengths.shape[1])))
    wq = qkv_weight.astype(BF).transpose(1, 0, 2)
    wo = out_weight.astype(BF)
    wf = ffn_weight.astype(BF).transpose(1, 0, 2)

    xrow, wq_full, wo_full, ln, lens_pair, dyb_all = call(
        functools.partial(gather_kernel, dp, seq),
        "gather",
        1,
        (tok, lnb, lens, wq, wo, cot),
        (
            shape((total, width), BF),
            shape((3, width, block), BF),
            shape((width, width), BF),
            shape((8, width), F32),
            shape((2, 8, LANES), jnp.int32),
            shape((group, count, width), BF),
        ),
        [
            vm((8, LANES), F32),
            vm((ranks, 8, LANES), F32),
            vm((3, wr * seq, 2 * block), BF),
            vm((count, width), BF),
            vm((count, width), BF),
            sem((2,)),
            sem((2,)),
            sem((4,)),
            sem((seq,)),
            sem((seq,)),
            sem((dp,)),
            sem((dp,)),
            sem((seq,)),
            sem((seq,)),
            sem((chips,)),
            sem((chips,)),
            sem((chips,)),
            sem((chips,)),
            sem((seq, 2)),
            sem((seq,)),
            sem((seq,)),
            sem((seq,)),
            sem((gchips,)),
            sem((gchips,)),
            sem((gchips,)),
            sem((gchips,)),
        ],
        10**6,
    )
    q, k, v, lse, cosine, sine, seg_col, seg_row, mixed_in, wf_full = call(
        functools.partial(attend_kernel, dp, seq, lengths.shape[1]),
        "attend",
        2,
        (xrow, wq_full, lens_pair, wf),
        (
            shape((total, block), BF),
            shape((total, block), BF),
            shape((total, block), BF),
            shape((total, LANES), F32),
            shape((total, LANES), F32),
            shape((total, LANES), F32),
            shape((total, LANES), jnp.int32),
            shape((8, total), jnp.int32),
            shape((seq, count, block), BF),
            shape((3, held, width), BF),
        ),
        [
            vm((seq, count, block), BF),
            sem((seq,)),
            sem((seq,)),
            sem((slots,)),
            sem((slots,)),
            sem((1,)),
        ],
        4 * 10**9,
    )
    mid, dmid, ln2, brsum, gf = call(
        functools.partial(ffn_kernel, dp, seq),
        "ffn",
        3,
        (tok, mixed_in, wo_full, ln, dyb_all, wf_full, cot),
        (
            shape((count, width), F32),
            shape((count, width), F32),
            shape((8, width), F32),
            shape((gchips, count, width), BF),
            shape((3, held, width), BF),
        ),
        [
            vm((count, width), BF),
            vm((gchips, 2, count, width), BF),
            vm((group * count, held), BF),
            vm((group * count, held), BF),
            vm((group * count, held), BF),
            vm((gchips, 2, count, width), BF),
            vm((gchips, count, width), BF),
            vm((gchips, count, width), BF),
            vm((gchips, count, width), BF),
            vm((gchips, 2, count, width), BF),
            vm((gchips, count, width), BF),
            vm((count, width), F32),
            vm((count, LANES), F32),
            sem((1,)),
        ]
        + [sem((gchips,))] * 10,
        20 * 10**9,
    )
    out, input_grad, lng, qg, og, fg = call(
        functools.partial(back_kernel, dp, seq),
        "back",
        4,
        (
            tok,
            mid,
            dmid,
            ln,
            ln2,
            brsum,
            gf,
            mixed_in,
            wo_full,
            wq_full,
            xrow,
            q,
            k,
            v,
            lse,
            cosine,
            sine,
            seg_col,
            seg_row,
        ),
        (
            shape((count, width), F32),
            shape((count, width), F32),
            shape((8, LANES), F32),
            shape((3, wr, width), F32),
            shape((wr, width), F32),
            shape((3, units, width), F32),
        ),
        [
            vm((seq, count, block), BF),
            vm((seq, count, block), BF),
            vm((gchips, count, width), BF),
            vm((2, chips, wr * seq, width), BF),
            vm((chips, wr * seq, width), BF),
            vm((chips, wr * seq, width), BF),
            vm((chips, wr * seq, width), BF),
            vm((wr * seq, width), BF),
            vm((seq, wr, width), BF),
            vm((total, block), F32),
            vm((total, block), F32),
            vm((total, block), F32),
            vm((2, seq // 2, count, width), BF),
            vm((seq // 2, count, width), BF),
            vm((seq // 2, count, width), BF),
            vm((seq // 2, count, width), BF),
            vm((3, total, block), BF),
            vm((width // block, 3, block, block), BF),
            vm((chips, 3, 2 * wr * seq, block), BF),
            vm((3, 2 * wr * seq, block), BF),
            vm((2 * seq, 3, wr, block), BF),
            vm((slots, 3, units, width), BF),
            vm((width // LANES, 8, LANES), F32),
            vm((ranks, 8, LANES), F32),
            sem((1,)),
            sem((seq,)),
            sem((seq,)),
            sem((gchips,)),
            sem((gchips,)),
            sem((slots,)),
            sem((slots,)),
            sem((2,)),
            sem((chips,)),
            sem((chips,)),
            sem((seq,)),
            sem((seq,)),
            sem((2,)),
            sem((seq,)),
            sem((seq,)),
            sem((chips,)),
            sem((chips,)),
            sem((2, seq)),
            sem((2 * seq,)),
            sem((2,)),
        ],
        8 * 10**9,
    )
    first = (rank % fit) * share
    ln_grad = lax.dynamic_slice(lng, (0, first), (4, share))
    return (
        out.reshape(1, count, width),
        input_grad.reshape(1, count, width),
        ln_grad,
        qg.transpose(1, 0, 2),
        og,
        fg.transpose(1, 0, 2),
    )


def solution(mesh):
    dp, seq = mesh.shape["dp"], mesh.shape["seq"]
    both = ("dp", "seq")
    in_specs = (
        P("dp", "seq", None),
        P(None, both),
        P(both, None, None),
        P(both, None),
        P(both, None, None),
        P("dp", None),
        P("dp", "seq", None),
    )
    out_specs = (
        P("dp", "seq", None),
        P("dp", "seq", None),
        P(None, both),
        P(both, None, None),
        P(both, None),
        P(both, None, None),
    )
    return jax.shard_map(
        functools.partial(body, dp, seq),
        mesh=mesh,
        in_specs=in_specs,
        out_specs=out_specs,
        check_vma=False,
    )
```

```python
import functools
import math
import types

import jax
import jax.numpy as jnp
from jax import lax
from jax.experimental import pallas as pl
from jax.experimental.pallas import tpu as pltpu
from jax.sharding import PartitionSpec as P

HEAD_DIM = 64
GROUP = 8
LANES = 128
BF = jnp.bfloat16
F32 = jnp.float32
MESH = pl.DeviceIdType.MESH
NT = (((1,), (1,)), ((), ()))
NN = (((1,), (0,)), ((), ()))
TN = (((0,), (0,)), ((), ()))
EPS = 1e-05
VMEM_BYTES = 62 * 2**20


def dot(a, b, dims):
    return lax.dot_general(a, b, dims, preferred_element_type=F32)


def remote(src, dst, send, recv, device):
    return pltpu.make_async_remote_copy(
        src_ref=src, dst_ref=dst, send_sem=send, recv_sem=recv, device_id=device, device_id_type=MESH
    )


def local(src, dst, sem):
    return pltpu.make_async_copy(src, dst, sem)


class Place:
    def __init__(self, dp, seq):
        self.dp, self.seq = dp, seq
        self.d, self.s = lax.axis_index("dp"), lax.axis_index("seq")
        self.c, self.k = self.d // 2, lax.rem(self.d, 2)
        self.sib = self.d + 1 - 2 * self.k
        self.chips = dp // 2
        self.group = min(dp, GROUP)
        self.groups = dp // self.group
        self.g, self.p = self.d // self.group, lax.rem(self.d, self.group)
        self.gc = self.p // 2
        self.gchips = self.group // 2
        self.half = seq // 2
        self.r, self.h = self.s // self.half, lax.rem(self.s, self.half)
        self.hg = 2 * self.h + self.k
        self.n = self.d * seq + self.s
        self.total = dp * seq

    def of_rank(self, rank):
        return (rank // self.seq, lax.rem(rank, self.seq))

    def in_group(self, chip, core):
        return self.g * self.group + 2 * chip + core


def normalise(value):
    mean = jnp.mean(value, axis=-1, keepdims=True)
    centred = value - mean
    var = jnp.mean(centred * centred, axis=-1, keepdims=True)
    scale = lax.rsqrt(var + EPS)
    return centred * scale, scale


def norm_back(grad, normal, scale, gain):
    scaled = grad * gain
    return scale * (
        scaled
        - jnp.mean(scaled, axis=-1, keepdims=True)
        - normal * jnp.mean(scaled * normal, axis=-1, keepdims=True)
    )


def swap_halves(value):
    half = HEAD_DIM // 2
    width = value.shape[1]
    lane = lax.broadcasted_iota(jnp.int32, value.shape, 1)
    up = pltpu.roll(value, width - half, 1)
    down = pltpu.roll(value, half, 1)
    return jnp.where(lax.rem(lane, HEAD_DIM) < half, up, down)


def head_mask(shape, h):
    lane = lax.broadcasted_iota(jnp.int32, shape, 1)
    return jnp.logical_and(lane >= h * HEAD_DIM, lane < (h + 1) * HEAD_DIM)


def tall(value, rows):
    return pl.multiple_of(value, rows)


def meet(me):
    barrier = pltpu.get_barrier_semaphore()

    def hello(j, carry):
        other = lax.rem(me.n + j, me.total)
        pl.semaphore_signal(barrier, inc=1, device_id=me.of_rank(other), device_id_type=MESH)
        return carry

    lax.fori_loop(1, me.total, hello, 0)


def met(me):
    pl.semaphore_wait(pltpu.get_barrier_semaphore(), me.total - 1)


def send_or_keep(here, src, dst, send, recv, device):
    @pl.when(jnp.logical_not(here))
    def _():
        remote(src, dst, send, recv, device).start()

    @pl.when(here)
    def _():
        local(src, dst, recv).start()


def sent(here, src, send, device):
    @pl.when(jnp.logical_not(here))
    def _():
        remote(src, src, send, send, device).wait_send()


def arrived(dst, recv):
    local(dst, dst, recv).wait()


def layer_kernel(names, dp, seq, segs, *refs):
    b = types.SimpleNamespace(**dict(zip(names, refs)))
    me = Place(dp, seq)
    count, width = b.out.shape
    total = count * seq
    wr = b.og.shape[0]
    cr = wr * seq
    block = b.q.shape[1]
    heads = block // HEAD_DIM
    units = b.fg.shape[1]
    held = b.wf_full.shape[1]
    band = me.groups * units
    nc = me.gchips
    sib = (me.sib, me.s)
    share = b.ln.shape[1]
    fit = LANES // share
    tiles = width // LANES
    per = me.total // tiles
    halfrows = count // 2
    last = []

    meet(me)
    loads = [
        local(b.tok, b.out, b.load.at[0]),
        local(b.wq, b.qg, b.load.at[1]),
        local(b.wo, b.og, b.load.at[2]),
        local(b.wf, b.fg, b.load.at[3]),
        local(b.cot, b.ig, b.load.at[4]),
    ]
    for copy in loads:
        copy.start()
    b.lens_own[...] = jnp.zeros_like(b.lens_own)
    b.lens_own[0:1, 0:segs] = b.lens[...]
    b.lens_pair[me.k] = b.lens_own[...]
    gains = jnp.concatenate([b.ln[...].astype(BF).astype(F32)] * fit, axis=1)
    lane = lax.broadcasted_iota(jnp.int32, gains.shape, 1)
    b.ln_own[...] = jnp.zeros_like(b.ln_own)
    b.ln_own[0:4, :] = jnp.where(lane // share == lax.rem(me.n, fit), gains, 0.0)
    b.ln_all[me.n] = b.ln_own[...]
    loads[1].wait()
    b.wq_own[...] = b.qg[...].astype(BF)
    loads[0].wait()
    normal, _ = normalise(b.out[...])
    b.norm[...] = normal
    met(me)

    def send_ln(j, carry):
        other = lax.rem(me.n + j, me.total)
        remote(
            b.ln_own, b.ln_all.at[me.n], b.lns.at[0], b.lns.at[1], me.of_rank(other)
        ).start()
        return carry

    lax.fori_loop(1, me.total, send_ln, 0)
    len_copy = remote(b.lens_own, b.lens_pair.at[me.k], b.lens_sem.at[0], b.lens_sem.at[1], sib)
    len_copy.start()
    pair = 2 * block
    row0 = tall(me.s * wr, wr)
    out0 = tall(me.n * wr, wr)
    wq_first = []
    for j in range(1, seq):
        to = lax.rem(me.s + j, seq)
        col = tall(lax.rem(to, me.half) * pair, pair)
        wq_first.append(
            remote(
                b.wq_own.at[:, :, pl.ds(col, pair)],
                b.wcol.at[:, pl.ds(row0, wr), :],
                b.wq1s.at[j],
                b.wq1r.at[j],
                (me.d, to),
            )
        )
    for copy in wq_first:
        copy.start()
    own_wq = local(
        b.wq_own.at[:, :, pl.ds(tall(me.h * pair, pair), pair)],
        b.wcol.at[:, pl.ds(row0, wr), :],
        b.load.at[5],
    )
    own_wq.start()
    loads[2].wait()
    b.wo_full[pl.ds(out0, wr), :] = b.og[...].astype(BF)
    rest = b.ln_all.at[pl.ds(0, me.total - 1)]
    remote(rest, rest, b.lns.at[0], b.lns.at[1], sib).wait()
    for t in range(tiles):
        part = b.ln_all[t * per]
        for i in range(1, per):
            part = part + b.ln_all[t * per + i]
        b.gain[:, t * LANES : (t + 1) * LANES] = part
    b.xown[...] = (b.norm[...] * b.gain[0:1, :] + b.gain[1:2, :]).astype(BF)
    rows0 = tall(me.s * count, count)
    for j in range(me.half):
        to = me.k * me.half + lax.rem(me.h + j, me.half)
        for core in range(2):
            src = b.xown.at[pl.ds(core * halfrows, halfrows), :]
            dst = b.xrow.at[pl.ds(rows0 + core * halfrows, halfrows), :]
            here = jnp.logical_and(to == me.s, core == me.k)
            send_or_keep(
                here, src, dst, b.xs.at[j, core], b.xr.at[me.s], (2 * me.c + core, to)
            )
            last.append(
                functools.partial(sent, here, src, b.xs.at[j, core], (2 * me.c + core, to))
            )
    wo_own = b.wo_full.at[pl.ds(out0, wr), :]
    wo_first = []
    for j in range(1, seq):
        to = (me.d, lax.rem(me.s + j, seq))
        wo_first.append(remote(wo_own, wo_own, b.wo1s.at[j], b.wo1r.at[j], to))
    for copy in wo_first:
        copy.start()
    for copy in wq_first:
        copy.wait()
    own_wq.wait()
    crow0 = tall(me.d * cr, cr)

    def send_wq(j, carry):
        to = lax.rem(me.d + j, dp)
        remote(
            b.wcol.at[:, :, pl.ds(tall(lax.rem(to, 2) * block, block), block)],
            b.wq_full.at[:, pl.ds(crow0, cr), :],
            b.wq2s.at[j],
            b.wq2r.at[j],
            (to, me.s),
        ).start()
        return carry

    lax.fori_loop(1, dp, send_wq, 0)
    own_half = local(
        b.wcol.at[:, :, pl.ds(tall(me.k * block, block), block)],
        b.wq_full.at[:, pl.ds(crow0, cr), :],
        b.load.at[6],
    )
    own_half.start()
    len_copy.wait()
    row = b.lens_pair[me.r]
    place_row = lax.broadcasted_iota(jnp.int32, (8, total), 1)
    place_col = lax.broadcasted_iota(jnp.int32, (total, LANES), 0)
    end = jnp.zeros((1, 1), jnp.int32)
    segr = jnp.zeros((8, total), jnp.int32)
    segc = jnp.zeros((total, LANES), jnp.int32)
    begin = jnp.zeros((total, LANES), jnp.int32)
    for j in range(segs):
        length = row[0:1, j : j + 1]
        end = end + length
        segr = segr + (place_row >= end).astype(jnp.int32)
        past = place_col >= end
        segc = segc + past.astype(jnp.int32)
        begin = begin + jnp.where(past, length, 0)
    b.seg_row[...] = segr
    b.seg_col[...] = segc
    half = HEAD_DIM // 2
    lane = lax.broadcasted_iota(jnp.int32, (1, LANES), 1)
    rate = jnp.exp(lax.rem(lane, half).astype(F32) * (-math.log(10000.0) / half))
    angle = (place_col - begin).astype(F32) * rate
    b.cos[...] = jnp.cos(angle)
    b.sin[...] = jnp.sin(angle) * jnp.where(lax.rem(lane, HEAD_DIM) < half, -1.0, 1.0)
    loads[4].wait()
    b.dyb[me.p] = b.ig[...].astype(BF)
    loads[3].wait()
    own_units = pl.ds(tall(me.s * band + me.g * units, units), units)
    b.wf_full[:, own_units, :] = b.fg[...].astype(BF)
    for j in range(seq):
        source = lax.rem(me.s + j, seq)
        part = b.xrow.at[pl.ds(tall(source * count + me.k * halfrows, halfrows), halfrows), :]
        arrived(part, b.xr.at[source])
        remote(part, part, b.xfs.at[j], b.xfr.at[j], sib).start()
    for j in range(1, me.groups):
        other = lax.rem(me.g + j, me.groups)
        mine = b.wf_full.at[:, own_units, :]
        remote(
            mine, mine, b.fgs.at[j], b.fgr_sem.at[j], (other * me.group + me.p, me.s)
        ).start()
    for j in range(1, me.groups):
        mine = b.wf_full.at[:, own_units, :]
        remote(mine, mine, b.fgs.at[j], b.fgr_sem.at[j], sib).wait()

    def column(at):
        return b.wf_full.at[:, pl.ds(tall(at * band, band), band), :]

    def hop(t):
        for way, step in ((0, 1), (1, -1)):
            at, to = me.s - step * t, me.s + step

            @pl.when((at >= 0) & (at < seq) & (to >= 0) & (to < seq))
            def _(way=way, at=at, to=to):
                remote(
                    column(at), column(at), b.hs.at[way, t], b.hr.at[way, t], (me.d, to)
                ).start()

    def hop_in(t):
        for way, step in ((0, 1), (1, -1)):
            at = me.s - step * (t + 1)

            @pl.when((at >= 0) & (at < seq))
            def _(way=way, at=at):
                arrived(column(at), b.hr.at[way, t])

    def hop_out(t):
        for way, step in ((0, 1), (1, -1)):
            at, to = me.s - step * t, me.s + step

            @pl.when((at >= 0) & (at < seq) & (to >= 0) & (to < seq))
            def _(way=way, at=at, to=to):
                remote(
                    column(at), column(at), b.hs.at[way, t], b.hr.at[way, t], (me.d, to)
                ).wait_send()

    hop(0)
    for j in range(seq):
        part = b.xrow.at[pl.ds(0, halfrows), :]
        arrived(part, b.xfr.at[j])
        last.append(functools.partial(sent, False, part, b.xfs.at[j], sib))

    def wait_wq(j, carry):
        part = b.wq_full.at[:, pl.ds(0, cr), :]
        remote(part, part, b.wq2s.at[j], b.wq2r.at[j], sib).wait()
        return carry

    lax.fori_loop(1, dp, wait_wq, 0)
    own_half.wait()
    for copy in wo_first:
        copy.wait()
    mine = b.wo_full.at[pl.ds(crow0, cr), :]
    remote(mine, mine, b.wo3s.at[0], b.wo3r.at[0], sib).start()
    for j in range(1, me.chips):
        to = 2 * lax.rem(me.c + j, me.chips) + me.k
        remote(mine, mine, b.wo2s.at[j], b.wo2r.at[j], (to, me.s)).start()
    dy_own = b.dyb.at[me.p]
    remote(dy_own, dy_own, b.dyfs.at[0], b.dyfr.at[0], sib).start()
    for j in range(1, nc):
        to = me.in_group(lax.rem(me.gc + j, nc), me.k)
        remote(dy_own, dy_own, b.dys.at[j], b.dyr.at[j], (to, me.s)).start()

    def project(i, carry):
        rows = pl.ds(tall(i * count, count), count)
        x = b.xrow[rows, :]
        cosine = jnp.concatenate([b.cos[rows, :]] * (block // LANES), axis=1)
        sine = jnp.concatenate([b.sin[rows, :]] * (block // LANES), axis=1)
        raw = dot(x, b.wq_full[0], NN)
        b.q[rows, :] = (raw * cosine + swap_halves(raw) * sine).astype(BF)
        raw = dot(x, b.wq_full[1], NN)
        b.kk[rows, :] = (raw * cosine + swap_halves(raw) * sine).astype(BF)
        b.v[rows, :] = dot(x, b.wq_full[2], NN).astype(BF)
        return carry

    lax.fori_loop(0, seq, project, 0)
    owner = 2 * me.c + me.r

    def attend(step, carry):
        i = lax.rem(me.s + step, seq)
        rows = pl.ds(tall(i * count, count), count)
        q = b.q[rows, :]
        bias = jnp.where(b.seg_col[rows, 0:1] == b.seg_row[0:1, :], 0.0, -1e30)
        lane = lax.broadcasted_iota(jnp.int32, (count, LANES), 1)
        lse = jnp.zeros((count, LANES), F32)
        out = jnp.zeros((count, block), F32)
        for h in range(heads):
            mask = head_mask((count, block), h)
            score = dot(jnp.where(mask, q, jnp.zeros_like(q)), b.kk[...], NT) * 0.125 + bias
            top = jnp.max(score, axis=1, keepdims=True)
            weight = jnp.exp(score - top)
            tally = jnp.sum(weight, axis=1, keepdims=True)
            prob = (weight * (1.0 / tally)).astype(BF)
            out = jnp.where(mask, dot(prob, b.v[...], NN), out)
            lse = jnp.where(lane == h, top + jnp.log(tally), lse)
        b.lse[rows, :] = lse
        b.mixed[i] = out.astype(BF)
        here = jnp.logical_and(i == me.s, owner == me.d)
        send_or_keep(
            here, b.mixed.at[i], b.mixed_in.at[me.hg], b.ms.at[i], b.mr.at[me.hg], (owner, i)
        )

        @pl.when(step == 1)
        def _():
            hop_in(0)
            hop(1)

        return carry

    lax.fori_loop(0, seq, attend, 0)
    for j in range(1, me.chips):
        source = 2 * lax.rem(me.c + me.chips - j, me.chips) + me.k
        part = b.wo_full.at[pl.ds(tall(source * cr, cr), cr), :]
        arrived(part, b.wo2r.at[j])
        remote(part, part, b.wo3s.at[j], b.wo3r.at[j], sib).start()
        last.append(functools.partial(sent, False, part, b.wo2s.at[j], sib))
        last.append(functools.partial(sent, False, part, b.wo3s.at[j], sib))
    last.append(functools.partial(sent, False, mine, b.wo3s.at[0], sib))
    for j in range(me.chips):
        arrived(mine, b.wo3r.at[j])
    for j in range(seq):
        arrived(b.mixed_in.at[j], b.mr.at[j])
    mid = b.out[...]
    for h in range(seq):
        mid = mid + dot(b.mixed_in[h], b.wo_full[h * block : (h + 1) * block, :], NN)
    b.out[...] = mid
    normal, scale = normalise(mid)
    b.norm[...] = normal
    b.scale[...] = jnp.broadcast_to(scale, b.scale.shape)
    b.xall[me.gc, me.k] = (normal * b.gain[2:3, :] + b.gain[3:4, :]).astype(BF)
    x_own = b.xall.at[me.gc, me.k]
    remote(x_own, x_own, b.xfs2.at[0], b.xfr2.at[0], sib).start()
    for j in range(1, nc):
        to = me.in_group(lax.rem(me.gc + j, nc), me.k)
        remote(x_own, x_own, b.xs2.at[j], b.xr2.at[j], (to, me.s)).start()
    for j in range(1, nc):
        source = 2 * lax.rem(me.gc + nc - j, nc) + me.k
        part = b.dyb.at[source]
        arrived(part, b.dyr.at[j])
        remote(part, part, b.dyfs.at[j], b.dyfr.at[j], sib).start()
        last.append(functools.partial(sent, False, part, b.dys.at[j], sib))
        last.append(functools.partial(sent, False, part, b.dyfs.at[j], sib))
    last.append(functools.partial(sent, False, dy_own, b.dyfs.at[0], sib))
    for j in range(nc):
        arrived(dy_own, b.dyfr.at[j])
    for t in range(1, seq - 1):
        hop_in(t)
        if t + 1 < seq - 1:
            hop(t + 1)
    tile = min(256, held)
    cols = 256

    def chip(j, carry):
        cj = lax.rem(me.gc + nc - j, nc)

        @pl.when(j > 0)
        def _():
            part = b.xall.at[cj, me.k]
            arrived(part, b.xr2.at[j])
            remote(part, part, b.xfs2.at[j], b.xfr2.at[j], sib).start()

        arrived(b.xall.at[cj, 1 - me.k], b.xfr2.at[j])
        rows = pl.ds(tall(cj * 2 * count, 2 * count), 2 * count)
        x = b.xall[cj].reshape(2 * count, width)
        dy = b.dyb[pl.ds(2 * cj, 2)].reshape(2 * count, width)
        for t in range(held // tile):
            span = slice(t * tile, (t + 1) * tile)
            gate = dot(x, b.wf_full[0, span, :], NT)
            up = dot(x, b.wf_full[1, span, :], NT)
            dh = dot(dy, b.wf_full[2, span, :], NT)
            sigma = 1.0 / (1.0 + jnp.exp(-gate))
            active = gate * sigma
            b.act[2, rows, span] = (active * up).astype(BF)
            b.act[0, rows, span] = (dh * up * (sigma * (1.0 + gate * (1.0 - sigma)))).astype(BF)
            b.act[1, rows, span] = (dh * active).astype(BF)
        for t in range(width // cols):
            span = slice(t * cols, (t + 1) * cols)
            value = dot(b.act[0, rows, :], b.wf_full[0, :, span], NN)
            value = value + dot(b.act[1, rows, :], b.wf_full[1, :, span], NN)
            b.dpart[lax.rem(j, 2), :, :, span] = value.astype(BF).reshape(2, count, cols)
        part = b.dpart.at[lax.rem(j, 2), 1 - me.k]
        remote(part, b.dsib.at[j], b.dss.at[j], b.dsr.at[j], sib).start()
        remote(b.dsib.at[j], b.dsib.at[j], b.dss.at[j], b.dsr.at[j], sib).wait()
        value = b.dpart[lax.rem(j, 2), me.k].astype(F32) + b.dsib[j].astype(F32)
        b.dsum[j] = value.astype(BF)

        @pl.when(j > 0)
        def _():
            to = (me.in_group(cj, me.k), me.s)
            remote(b.dsum.at[j], b.drecv.at[j - 1], b.dps.at[j], b.dpr.at[j], to).start()

        return carry

    lax.fori_loop(0, nc, chip, 0)
    for j in range(nc):
        last.append(functools.partial(sent, False, x_own, b.xfs2.at[j], sib))
        if j:
            last.append(functools.partial(sent, False, x_own, b.xs2.at[j], sib))
    for copy in last:
        copy()
    last.clear()
    for t in range(seq - 1):
        hop_out(t)

    def add_branch(j):
        arrived(b.dsib.at[j], b.bsr.at[j])
        value = b.dpart[lax.rem(j, 2), me.k].astype(F32) + b.dsib[j].astype(F32)
        value = value.astype(BF)

        @pl.when(j == 0)
        def _():
            b.xown[...] = value

        @pl.when(j > 0)
        def _():
            remote(b.dsum.at[j], b.drecv.at[j - 1], b.dps.at[j], b.dpr.at[j], sib).wait_send()
            b.dsum[j] = value
            cj = lax.rem(me.gc + nc - j, nc)
            to = (me.in_group(cj, me.k), me.s)
            remote(b.dsum.at[j], b.brr.at[j - 1], b.brs.at[j], b.brr_sem.at[j], to).start()

    def branch(j, carry):
        cj = lax.rem(me.gc + nc - j, nc)
        rows = pl.ds(tall(cj * 2 * count, 2 * count), 2 * count)

        @pl.when(j > 1)
        def _():
            sent(False, b.dpart.at[0, 0], b.bss.at[j - 2], sib)

        for t in range(width // cols):
            span = slice(t * cols, (t + 1) * cols)
            value = dot(b.act[2, rows, :], b.wf_full[2, :, span], NN)
            b.dpart[lax.rem(j, 2), :, :, span] = value.astype(BF).reshape(2, count, cols)

        @pl.when(j > 0)
        def _():
            add_branch(j - 1)

        part = b.dpart.at[lax.rem(j, 2), 1 - me.k]
        remote(part, b.dsib.at[j], b.bss.at[j], b.bsr.at[j], sib).start()
        return carry

    lax.fori_loop(0, nc, branch, 0)

    def grads(t, carry):
        span = pl.ds(tall(t * tile, tile), tile)
        x = b.xall[...].reshape(nc * 2 * count, width)
        dy = b.dyb[...].reshape(nc * 2 * count, width)
        b.wf_full[0, span, :] = dot(b.act[0, :, span], x, TN).astype(BF)
        b.wf_full[1, span, :] = dot(b.act[1, :, span], x, TN).astype(BF)
        b.wf_full[2, span, :] = dot(b.act[2, :, span], dy, TN).astype(BF)
        return carry

    lax.fori_loop(0, held // tile, grads, 0)
    add_branch(nc - 1)
    for j in range(max(nc - 2, 0), nc):
        sent(False, b.dpart.at[0, 0], b.bss.at[j], sib)
    dn2 = b.dsum[0].astype(F32)
    for j in range(1, nc):
        arrived(b.drecv.at[j - 1], b.dpr.at[j])
        dn2 = dn2 + b.drecv[j - 1].astype(F32)
    normal = b.norm[...]
    gain2 = jnp.sum(dn2 * normal, axis=0, keepdims=True)
    shift2 = jnp.sum(dn2, axis=0, keepdims=True)
    b.lnp[...] = jnp.zeros_like(b.lnp)
    for t in range(tiles):
        lanes = slice(t * LANES, (t + 1) * LANES)
        b.lnp[t, 2:3, :] = gain2[:, lanes]
        b.lnp[t, 3:4, :] = shift2[:, lanes]
    dmid = b.ig[...] + norm_back(dn2, normal, b.scale[:, 0:1], b.gain[2:3, :])
    b.ig[...] = dmid
    dmb = dmid.astype(BF)
    for i in range(seq):
        here = jnp.logical_and(i == me.s, owner == me.d)
        sent(here, b.mixed.at[i], b.ms.at[i], sib)
    for hg in range(seq):
        b.mixed[hg] = dot(dmb, b.wo_full[hg * block : (hg + 1) * block, :], NT).astype(BF)
        to = (2 * me.c + hg % 2, me.k * me.half + hg // 2)
        here = jnp.logical_and(to[0] == me.d, to[1] == me.s)
        send_or_keep(
            here, b.mixed.at[hg], b.dmix_row.at[me.s], b.dms.at[hg], b.dmr.at[me.s], to
        )
        last.append(functools.partial(sent, here, b.mixed.at[hg], b.dms.at[hg], sib))
    slots = me.groups * seq
    slot = me.s * me.groups + me.g
    for j in range(1, slots):
        other = lax.rem(slot + j, slots)
        to = (lax.rem(other, me.groups) * me.group + me.p, other // me.groups)
        src = b.wf_full.at[:, pl.ds(tall(other * units, units), units), :]
        remote(src, b.fgr.at[j - 1], b.gs.at[j], b.gr.at[j], to).start()
    pieces = width // 2 // count

    def og_rows(parity):
        return b.dyb.at[pl.ds(parity * pieces, pieces)]

    for h in range(seq):
        part = dot(b.mixed_in[h], dmb, TN).astype(BF)
        for t in range(block // cr):
            first = h * (block // cr) + t
            row = (first // 2) * cr
            b.dyb[(first % 2) * pieces + row // count, row % count : row % count + cr, :] = part[
                t * cr : (t + 1) * cr
            ]
    remote(og_rows(1 - me.k), b.ogsib, b.o1.at[0], b.o1.at[1], sib).start()
    for j in range(seq):
        arrived(b.dmix_row.at[j], b.dmr.at[j])
    b.dk[...] = jnp.zeros_like(b.dk)
    b.dv[...] = jnp.zeros_like(b.dv)

    def og_sum():
        remote(b.ogsib, b.ogsib, b.o1.at[0], b.o1.at[1], sib).wait()
        for i in range(pieces):
            value = b.dyb[me.k * pieces + i].astype(F32) + b.ogsib[i].astype(F32)
            b.dyb[2 * pieces + i] = value.astype(BF)

        def send_og(j, carry):
            chip = lax.rem(me.c + j, me.chips)
            row = chip * cr
            src = b.dyb.at[2 * pieces + row // count, pl.ds(tall(lax.rem(row, count), cr), cr), :]
            remote(src, b.ogpl.at[j], b.o2s.at[j], b.o2r.at[j], (2 * chip + me.k, me.s)).start()
            return carry

        lax.fori_loop(1, me.chips, send_og, 0)

    def og_column():
        row = me.c * cr
        at = pl.ds(tall(lax.rem(row, count), cr), cr)
        acc = b.dyb[2 * pieces + row // count, at, :].astype(F32)
        for j in range(1, me.chips):
            remote(b.ogpl.at[j], b.ogpl.at[j], b.o2s.at[j], b.o2r.at[j], sib).wait()
            acc = acc + b.ogpl[j].astype(F32)
        b.ogc[...] = acc.astype(BF)
        for j in range(1, seq):
            to = lax.rem(me.s + j, seq)
            src = b.ogc.at[pl.ds(tall(to * wr, wr), wr), :]
            remote(src, b.ogz.at[j], b.o3s.at[j], b.o3r.at[j], (me.d, to)).start()

    def attend_back(i, carry):
        rows = pl.ds(tall(i * count, count), count)
        q = b.q[rows, :]
        dm = b.dmix_row[i]
        lse = b.lse[rows, :]
        bias = jnp.where(b.seg_col[rows, 0:1] == b.seg_row[0:1, :], 0.0, -1e30)
        grad_q = jnp.zeros((count, block), F32)
        for h in range(heads):
            mask = head_mask((count, block), h)
            qh = jnp.where(mask, q, jnp.zeros_like(q))
            dmh = jnp.where(mask, dm, jnp.zeros_like(dm))
            score = dot(qh, b.kk[...], NT) * 0.125 + bias
            prob = jnp.exp(score - lse[:, h : h + 1])
            dprob = dot(dmh, b.v[...], NT)
            centre = jnp.sum(prob * dprob, axis=1, keepdims=True)
            ds = (0.125 * prob * (dprob - centre)).astype(BF)
            grad_q = jnp.where(mask, dot(ds, b.kk[...], NN), grad_q)
            b.dk[...] += dot(ds, qh, TN)
            b.dv[...] += dot(prob.astype(BF), dmh, TN)
        cosine = jnp.concatenate([b.cos[rows, :]] * (block // LANES), axis=1)
        sine = jnp.concatenate([b.sin[rows, :]] * (block // LANES), axis=1)
        b.act[0, rows, 0:block] = (grad_q * cosine - swap_halves(grad_q) * sine).astype(BF)

        @pl.when(i == 0)
        def _():
            og_sum()

        return carry

    lax.fori_loop(0, seq, attend_back, 0)

    def back_chunk(i):
        rows = pl.ds(tall(i * count, count), count)
        cosine = jnp.concatenate([b.cos[rows, :]] * (block // LANES), axis=1)
        sine = jnp.concatenate([b.sin[rows, :]] * (block // LANES), axis=1)
        grad_k = b.dk[rows, :]
        dk = (grad_k * cosine - swap_halves(grad_k) * sine).astype(BF)
        dv = b.dv[rows, :].astype(BF)
        b.act[1, rows, 0:block] = dk
        b.act[2, rows, 0:block] = dv
        value = dot(b.act[0, rows, 0:block], b.wq_full[0], NT)
        value = value + dot(dk, b.wq_full[1], NT) + dot(dv, b.wq_full[2], NT)
        at = lax.rem(i, 2) * me.half + i // 2
        b.xall[at // 2, lax.rem(at, 2)] = value.astype(BF)

    def other_half(j, carry):
        back_chunk(2 * j + 1 - me.k)
        return carry

    def own_half_chunks(j, carry):
        back_chunk(2 * j + me.k)
        return carry

    lax.fori_loop(0, me.half, other_half, 0)
    quarter = me.half // 2
    dn_other = b.xall.at[pl.ds((1 - me.k) * quarter, quarter)]
    remote(dn_other, b.dnsib, b.n1.at[0], b.n1.at[1], sib).start()
    lax.fori_loop(0, me.half, own_half_chunks, 0)
    remote(b.dnsib, b.dnsib, b.n1.at[0], b.n1.at[1], sib).wait()
    for j in range(me.half):
        value = b.xall[me.k * quarter + j // 2, j % 2].astype(F32)
        b.dpart[0, j] = (value + b.dnsib[j // 2, j % 2].astype(F32)).astype(BF)
        i = 2 * j + me.k
        here = jnp.logical_and(owner == me.d, i == me.s)
        send_or_keep(
            here, b.dpart.at[0, j], b.dnr.at[me.h], b.n2s.at[j], b.n2r.at[me.h], (owner, i)
        )
        last.append(functools.partial(sent, here, b.dpart.at[0, j], b.n2s.at[j], sib))
    span_rows = 2 * cr
    per_tile = block // span_rows

    def qkv_terms(j, carry):
        at = lax.rem(me.c // per_tile + j, width // block)
        x = b.xrow[:, pl.ds(tall(at * block, block), block)]
        rows = pl.ds(tall(total + at * block, block), block)
        for t in range(3):
            b.act[t, rows, 0:block] = dot(x, b.act[t, 0:total, 0:block], TN).astype(BF)
        for i in range(per_tile):
            chip = at * per_tile + i

            @pl.when(chip != me.c)
            def _(chip=chip):
                src = b.act.at[:, pl.ds(tall(total + chip * span_rows, span_rows), span_rows), 0:block]
                to = (2 * chip + me.k, me.s)
                remote(src, b.qgpl.at[me.c], b.q1s.at[chip], b.q1r.at[me.c], to).start()

        return carry

    lax.fori_loop(1, width // block, qkv_terms, 0)
    qkv_terms(0, 0)
    og_column()
    tok = local(b.tok, b.norm, b.load.at[0])
    tok.start()
    dn1 = jnp.zeros((count, width), F32)
    tok.wait()
    normal, scale = normalise(b.norm[...])
    for h in range(me.half):
        arrived(b.dnr.at[h], b.n2r.at[h])
        dn1 = dn1 + b.dnr[h].astype(F32)
    b.ig[...] = b.ig[...] + norm_back(dn1, normal, scale, b.gain[0:1, :])
    gain1 = jnp.sum(dn1 * normal, axis=0, keepdims=True)
    shift1 = jnp.sum(dn1, axis=0, keepdims=True)
    for t in range(tiles):
        lanes = slice(t * LANES, (t + 1) * LANES)
        b.lnp[t, 0:1, :] = gain1[:, lanes]
        b.lnp[t, 1:2, :] = shift1[:, lanes]

    def send_lnp(j, carry):
        other = lax.rem(me.n + j, me.total)
        remote(
            b.lnp.at[other // per], b.lnr.at[me.n], b.lnt.at[0], b.lnt.at[1], me.of_rank(other)
        ).start()
        return carry

    lax.fori_loop(1, me.total, send_lnp, 0)
    b.lnr[me.n] = b.lnp[me.n // per]
    own = pl.ds(tall(total + me.c * span_rows, span_rows), span_rows)
    sums = [b.act[t, own, 0:block].astype(F32) for t in range(3)]
    for j in range(1, me.chips):
        chip = lax.rem(me.c + j, me.chips)
        part = b.qgpl.at[chip]
        remote(part, part, b.q1s.at[chip], b.q1r.at[chip], sib).wait()
        for t in range(3):
            sums[t] = sums[t] + b.qgpl[chip, t].astype(F32)
    for t in range(3):
        b.qgc[t] = sums[t].astype(BF)
    source = me.k * seq + me.s
    for core in range(2):
        for j in range(seq):
            to = lax.rem(me.s + j, seq)
            src = b.qgc.at[:, pl.ds(tall((core * seq + to) * wr, wr), wr), :]
            here = jnp.logical_and(core == me.k, to == me.s)
            send_or_keep(
                here, src, b.qgz.at[source], b.q2s.at[core, j], b.q2r.at[source], (2 * me.c + core, to)
            )
            last.append(functools.partial(sent, here, src, b.q2s.at[core, j], sib))
    value = b.out[...] + b.xown[...].astype(F32)
    for j in range(1, nc):
        remote(b.brr.at[j - 1], b.brr.at[j - 1], b.brs.at[j], b.brr_sem.at[j], sib).wait()
        value = value + b.brr[j - 1].astype(F32)
    b.out[...] = value
    acc = b.ogc[pl.ds(tall(me.s * wr, wr), wr), :].astype(F32)
    for j in range(1, seq):
        remote(b.ogz.at[j], b.ogz.at[j], b.o3s.at[j], b.o3r.at[j], sib).wait()
        acc = acc + b.ogz[j].astype(F32)
    b.og[...] = acc
    acc = b.wf_full[:, pl.ds(tall(slot * units, units), units), :].astype(F32)
    for j in range(1, slots):
        part = b.fgr.at[j - 1]
        remote(part, part, b.gs.at[j], b.gr.at[j], sib).wait()
        acc = acc + b.fgr[j - 1].astype(F32)
    b.fg[...] = acc
    rest = b.lnr.at[pl.ds(0, me.total - 1)]
    remote(rest, rest, b.lnt.at[0], b.lnt.at[1], sib).wait()
    acc = b.lnr[0]
    for j in range(1, me.total):
        acc = acc + b.lnr[j]
    b.lng[...] = acc
    for j in range(2 * seq):
        arrived(b.qgz.at[j], b.q2r.at[j])
    for hg in range(seq):
        core, h = hg % 2, hg // 2
        acc = b.qgz[core * seq + h].astype(F32) + b.qgz[core * seq + me.half + h].astype(F32)
        b.qg[:, :, hg * block : (hg + 1) * block] = acc
    for copy in last:
        copy()


def body(dp, seq, tokens, ln_params, qkv_weight, out_weight, ffn_weight, lengths, cotangent):
    count, width = tokens.shape[1], tokens.shape[2]
    ranks = dp * seq
    total = count * seq
    wr = qkv_weight.shape[0]
    cr = wr * seq
    units = ffn_weight.shape[0]
    block = width // seq
    half = seq // 2
    group = min(dp, GROUP)
    groups = dp // group
    gchips, chips, slots = group // 2, dp // 2, groups * seq
    held = units * slots
    share = ln_params.shape[1]
    sem = pltpu.SemaphoreType.DMA
    vm = pltpu.VMEM
    anywhere = pl.BlockSpec(memory_space=pl.ANY)
    vmem = pl.BlockSpec(memory_space=pltpu.VMEM)
    operands = dict(
        tok=(tokens.reshape(count, width), anywhere),
        ln=(ln_params, vmem),
        wq=(qkv_weight.transpose(1, 0, 2), anywhere),
        wo=(out_weight, anywhere),
        wf=(ffn_weight.transpose(1, 0, 2), anywhere),
        lens=(lengths, vmem),
        cot=(cotangent.reshape(count, width), anywhere),
    )
    outs = dict(
        out=(count, width),
        ig=(count, width),
        lng=(8, LANES),
        qg=(3, wr, width),
        og=(wr, width),
        fg=(3, units, width),
    )
    scratch = dict(
        norm=vm((count, width), F32),
        scale=vm((count, LANES), F32),
        lens_own=vm((8, LANES), jnp.int32),
        lens_pair=vm((2, 8, LANES), jnp.int32),
        ln_own=vm((8, LANES), F32),
        ln_all=vm((ranks, 8, LANES), F32),
        gain=vm((8, width), F32),
        wq_own=vm((3, wr, width), BF),
        wcol=vm((3, cr, 2 * block), BF),
        xown=vm((count, width), BF),
        xrow=vm((total, width), BF),
        wq_full=vm((3, width, block), BF),
        wo_full=vm((width, width), BF),
        dyb=vm((group, count, width), BF),
        q=vm((total, block), BF),
        kk=vm((total, block), BF),
        v=vm((total, block), BF),
        lse=vm((total, LANES), F32),
        cos=vm((total, LANES), F32),
        sin=vm((total, LANES), F32),
        seg_col=vm((total, LANES), jnp.int32),
        seg_row=vm((8, total), jnp.int32),
        mixed=vm((seq, count, block), BF),
        mixed_in=vm((seq, count, block), BF),
        dmix_row=vm((seq, count, block), BF),
        wf_full=vm((3, held, width), BF),
        xall=vm((gchips, 2, count, width), BF),
        act=vm((3, group * count, held), BF),
        dpart=vm((2, 2, count, width), BF),
        dsib=vm((gchips, count, width), BF),
        dsum=vm((gchips, count, width), BF),
        drecv=vm((gchips - 1, count, width), BF),
        brr=vm((gchips - 1, count, width), BF),
        ogsib=vm((width // 2 // count, count, width), BF),
        ogpl=vm((chips, cr, width), BF),
        ogc=vm((cr, width), BF),
        ogz=vm((seq, wr, width), BF),
        dk=vm((total, block), F32),
        dv=vm((total, block), F32),
        dnsib=vm((half // 2, 2, count, width), BF),
        dnr=vm((half, count, width), BF),
        qgpl=vm((chips, 3, 2 * cr, block), BF),
        qgc=vm((3, 2 * cr, block), BF),
        qgz=vm((2 * seq, 3, wr, block), BF),
        fgr=vm((slots - 1, 3, units, width), BF),
        lnp=vm((width // LANES, 8, LANES), F32),
        lnr=vm((ranks, 8, LANES), F32),
        load=sem((7,)),
        lns=sem((2,)),
        lens_sem=sem((2,)),
        wq1s=sem((seq,)),
        wq1r=sem((seq,)),
        wq2s=sem((dp,)),
        wq2r=sem((dp,)),
        wo1s=sem((seq,)),
        wo1r=sem((seq,)),
        wo2s=sem((chips,)),
        wo2r=sem((chips,)),
        wo3s=sem((chips,)),
        wo3r=sem((chips,)),
        xs=sem((half, 2)),
        xr=sem((seq,)),
        xfs=sem((seq,)),
        xfr=sem((seq,)),
        dys=sem((gchips,)),
        dyr=sem((gchips,)),
        dyfs=sem((gchips,)),
        dyfr=sem((gchips,)),
        fgs=sem((groups,)),
        fgr_sem=sem((groups,)),
        hs=sem((2, seq)),
        hr=sem((2, seq)),
        ms=sem((seq,)),
        mr=sem((seq,)),
        xs2=sem((gchips,)),
        xr2=sem((gchips,)),
        xfs2=sem((gchips,)),
        xfr2=sem((gchips,)),
        dss=sem((gchips,)),
        dsr=sem((gchips,)),
        dps=sem((gchips,)),
        dpr=sem((gchips,)),
        bss=sem((gchips,)),
        bsr=sem((gchips,)),
        brs=sem((gchips,)),
        brr_sem=sem((gchips,)),
        dms=sem((seq,)),
        dmr=sem((seq,)),
        gs=sem((slots,)),
        gr=sem((slots,)),
        o1=sem((2,)),
        o2s=sem((chips,)),
        o2r=sem((chips,)),
        o3s=sem((seq,)),
        o3r=sem((seq,)),
        n1=sem((2,)),
        n2s=sem((half,)),
        n2r=sem((half,)),
        q1s=sem((chips,)),
        q1r=sem((chips,)),
        q2s=sem((2, seq)),
        q2r=sem((2 * seq,)),
        lnt=sem((2,)),
    )
    names = (*operands, *outs, *scratch)
    out, input_grad, lng, qg, og, fg = pl.pallas_call(
        functools.partial(layer_kernel, names, dp, seq, lengths.shape[1]),
        out_shape=tuple(jax.ShapeDtypeStruct(dims, F32) for dims in outs.values()),
        in_specs=[spec for _, spec in operands.values()],
        out_specs=tuple([vmem] * len(outs)),
        scratch_shapes=list(scratch.values()),
        compiler_params=pltpu.CompilerParams(
            collective_id=1, has_side_effects=True, vmem_limit_bytes=VMEM_BYTES
        ),
        cost_estimate=pl.CostEstimate(
            flops=32 * 10**9, bytes_accessed=2**24, transcendentals=10**7
        ),
        name="layer",
    )(*[value for value, _ in operands.values()])
    rank = lax.axis_index("dp") * seq + lax.axis_index("seq")
    ln_grad = lax.dynamic_slice(lng, (0, (rank % (LANES // share)) * share), (4, share))
    return (
        out.reshape(1, count, width),
        input_grad.reshape(1, count, width),
        ln_grad,
        qg.transpose(1, 0, 2),
        og,
        fg.transpose(1, 0, 2),
    )


def solution(mesh):
    dp, seq = mesh.shape["dp"], mesh.shape["seq"]
    both = ("dp", "seq")
    in_specs = (
        P("dp", "seq", None),
        P(None, both),
        P(both, None, None),
        P(both, None),
        P(both, None, None),
        P("dp", None),
        P("dp", "seq", None),
    )
    out_specs = (
        P("dp", "seq", None),
        P("dp", "seq", None),
        P(None, both),
        P(both, None, None),
        P(both, None),
        P(both, None, None),
    )
    return jax.shard_map(
        functools.partial(body, dp, seq),
        mesh=mesh,
        in_specs=in_specs,
        out_specs=out_specs,
        check_vma=False,
    )
```

```python
import functools
import math
import types

import jax
import jax.numpy as jnp
from jax import lax
from jax.experimental import pallas as pl
from jax.experimental.pallas import tpu as pltpu
from jax.sharding import PartitionSpec as P

HEAD_DIM = 64
GROUP = 8
LANES = 128
BF = jnp.bfloat16
F32 = jnp.float32
MESH = pl.DeviceIdType.MESH
NT = (((1,), (1,)), ((), ()))
NN = (((1,), (0,)), ((), ()))
TN = (((0,), (0,)), ((), ()))
EPS = 1e-05
VMEM_BYTES = 62 * 2**20


def dot(a, b, dims):
    return lax.dot_general(a, b, dims, preferred_element_type=F32)


def remote(src, dst, send, recv, device):
    return pltpu.make_async_remote_copy(
        src_ref=src, dst_ref=dst, send_sem=send, recv_sem=recv, device_id=device, device_id_type=MESH
    )


def local(src, dst, sem):
    return pltpu.make_async_copy(src, dst, sem)


class Place:
    def __init__(self, dp, seq):
        self.dp, self.seq = dp, seq
        self.d, self.s = lax.axis_index("dp"), lax.axis_index("seq")
        self.c, self.k = self.d // 2, lax.rem(self.d, 2)
        self.sib = self.d + 1 - 2 * self.k
        self.chips = dp // 2
        self.group = min(dp, GROUP)
        self.groups = dp // self.group
        self.g, self.p = self.d // self.group, lax.rem(self.d, self.group)
        self.gc = self.p // 2
        self.gchips = self.group // 2
        self.half = seq // 2
        self.r, self.h = self.s // self.half, lax.rem(self.s, self.half)
        self.hg = 2 * self.h + self.k
        self.n = self.d * seq + self.s
        self.total = dp * seq

    def of_rank(self, rank):
        return (rank // self.seq, lax.rem(rank, self.seq))

    def in_group(self, chip, core):
        return self.g * self.group + 2 * chip + core


def normalise(value):
    mean = jnp.mean(value, axis=-1, keepdims=True)
    centred = value - mean
    var = jnp.mean(centred * centred, axis=-1, keepdims=True)
    scale = lax.rsqrt(var + EPS)
    return centred * scale, scale


def norm_back(grad, normal, scale, gain):
    scaled = grad * gain
    return scale * (
        scaled
        - jnp.mean(scaled, axis=-1, keepdims=True)
        - normal * jnp.mean(scaled * normal, axis=-1, keepdims=True)
    )


def swap_halves(value):
    half = HEAD_DIM // 2
    width = value.shape[1]
    lane = lax.broadcasted_iota(jnp.int32, value.shape, 1)
    up = pltpu.roll(value, width - half, 1)
    down = pltpu.roll(value, half, 1)
    return jnp.where(lax.rem(lane, HEAD_DIM) < half, up, down)


def head_mask(shape, h):
    lane = lax.broadcasted_iota(jnp.int32, shape, 1)
    return jnp.logical_and(lane >= h * HEAD_DIM, lane < (h + 1) * HEAD_DIM)


def tall(value, rows):
    return pl.multiple_of(value, rows)


def meet(me):
    barrier = pltpu.get_barrier_semaphore()

    def hello(j, carry):
        other = lax.rem(me.n + j, me.total)
        pl.semaphore_signal(barrier, inc=1, device_id=me.of_rank(other), device_id_type=MESH)
        return carry

    lax.fori_loop(1, me.total, hello, 0)


def met(me):
    pl.semaphore_wait(pltpu.get_barrier_semaphore(), me.total - 1)


def send_or_keep(here, src, dst, send, recv, device):
    @pl.when(jnp.logical_not(here))
    def _():
        remote(src, dst, send, recv, device).start()

    @pl.when(here)
    def _():
        local(src, dst, recv).start()


def sent(here, src, send, device):
    @pl.when(jnp.logical_not(here))
    def _():
        remote(src, src, send, send, device).wait_send()


def arrived(dst, recv):
    local(dst, dst, recv).wait()


def layer_kernel(names, dp, seq, segs, *refs):
    b = types.SimpleNamespace(**dict(zip(names, refs)))
    me = Place(dp, seq)
    count, width = b.out.shape
    total = count * seq
    wr = b.og.shape[0]
    cr = wr * seq
    block = b.q.shape[1]
    heads = block // HEAD_DIM
    units = b.fg.shape[1]
    held = b.wf_full.shape[1]
    band = me.groups * units
    nc = me.gchips
    sib = (me.sib, me.s)
    share = b.ln.shape[1]
    fit = LANES // share
    tiles = width // LANES
    per = me.total // tiles
    halfrows = count // 2
    last = []

    def by_rows(step):
        def one(i, carry):
            step(pl.ds(tall(i * some, some), some))
            return carry

        lax.fori_loop(0, count // some, one, 0)

    some = 64
    results = ("out", "ig", "lng", "qg", "og", "fg")
    stores = []

    def store(i):
        name = results[i]
        stores.append(local(getattr(b, name), getattr(b, name + "_out"), b.keep.at[i]))
        stores[-1].start()

    meet(me)
    loads = [
        local(b.tok, b.out, b.load.at[0]),
        local(b.wq, b.qg, b.load.at[1]),
        local(b.wo, b.og, b.load.at[2]),
        local(b.wf, b.fg, b.load.at[3]),
        local(b.cot, b.ig, b.load.at[4]),
    ]
    for copy in loads:
        copy.start()
    b.lens_own[...] = jnp.zeros_like(b.lens_own)
    b.lens_own[0:1, 0:segs] = b.lens[...]
    b.lens_pair[me.k] = b.lens_own[...]
    gains = jnp.concatenate([b.ln[...].astype(BF).astype(F32)] * fit, axis=1)
    lane = lax.broadcasted_iota(jnp.int32, gains.shape, 1)
    b.ln_own[...] = jnp.zeros_like(b.ln_own)
    b.ln_own[0:4, :] = jnp.where(lane // share == lax.rem(me.n, fit), gains, 0.0)
    b.ln_all[me.n] = b.ln_own[...]
    loads[1].wait()
    b.wq_own[...] = b.qg[...].astype(BF)
    loads[0].wait()

    def first_norm(rows):
        b.norm[rows, :] = normalise(b.out[rows, :])[0]

    by_rows(first_norm)
    met(me)

    def send_ln(j, carry):
        other = lax.rem(me.n + j, me.total)
        remote(
            b.ln_own, b.ln_all.at[me.n], b.lns.at[0], b.lns.at[1], me.of_rank(other)
        ).start()
        return carry

    lax.fori_loop(1, me.total, send_ln, 0)
    len_copy = remote(b.lens_own, b.lens_pair.at[me.k], b.lens_sem.at[0], b.lens_sem.at[1], sib)
    len_copy.start()
    pair = 2 * block
    row0 = tall(me.s * wr, wr)
    out0 = tall(me.n * wr, wr)
    wq_first = []
    for j in range(1, seq):
        to = lax.rem(me.s + j, seq)
        col = tall(lax.rem(to, me.half) * pair, pair)
        wq_first.append(
            remote(
                b.wq_own.at[:, :, pl.ds(col, pair)],
                b.wcol.at[:, pl.ds(row0, wr), :],
                b.wq1s.at[j],
                b.wq1r.at[j],
                (me.d, to),
            )
        )
    for copy in wq_first:
        copy.start()
    own_wq = local(
        b.wq_own.at[:, :, pl.ds(tall(me.h * pair, pair), pair)],
        b.wcol.at[:, pl.ds(row0, wr), :],
        b.load.at[5],
    )
    own_wq.start()
    loads[2].wait()
    b.wo_full[pl.ds(out0, wr), :] = b.og[...].astype(BF)
    rest = b.ln_all.at[pl.ds(0, me.total - 1)]
    remote(rest, rest, b.lns.at[0], b.lns.at[1], sib).wait()
    for t in range(tiles):
        part = b.ln_all[t * per]
        for i in range(1, per):
            part = part + b.ln_all[t * per + i]
        b.gain[:, t * LANES : (t + 1) * LANES] = part

    def first_out(rows):
        b.xown[rows, :] = (b.norm[rows, :] * b.gain[0:1, :] + b.gain[1:2, :]).astype(BF)

    by_rows(first_out)
    rows0 = tall(me.s * count, count)
    for j in range(me.half):
        to = me.k * me.half + lax.rem(me.h + j, me.half)
        for core in range(2):
            src = b.xown.at[pl.ds(core * halfrows, halfrows), :]
            dst = b.xrow.at[pl.ds(rows0 + core * halfrows, halfrows), :]
            here = jnp.logical_and(to == me.s, core == me.k)
            send_or_keep(
                here, src, dst, b.xs.at[j, core], b.xr.at[me.s], (2 * me.c + core, to)
            )
            last.append(
                functools.partial(sent, here, src, b.xs.at[j, core], (2 * me.c + core, to))
            )
    for copy in wq_first:
        copy.wait()
    own_wq.wait()
    crow0 = tall(me.d * cr, cr)

    def send_wq(j, carry):
        to = lax.rem(me.d + j, dp)
        remote(
            b.wcol.at[:, :, pl.ds(tall(lax.rem(to, 2) * block, block), block)],
            b.wq_full.at[:, pl.ds(crow0, cr), :],
            b.wq2s.at[j],
            b.wq2r.at[j],
            (to, me.s),
        ).start()
        return carry

    lax.fori_loop(1, dp, send_wq, 0)
    own_half = local(
        b.wcol.at[:, :, pl.ds(tall(me.k * block, block), block)],
        b.wq_full.at[:, pl.ds(crow0, cr), :],
        b.load.at[6],
    )
    own_half.start()
    len_copy.wait()
    row = b.lens_pair[me.r]
    place_row = lax.broadcasted_iota(jnp.int32, (8, total), 1)
    ends = [row[0:1, 0:1]]
    for j in range(1, segs):
        ends.append(ends[-1] + row[0:1, j : j + 1])
    segr = jnp.zeros((8, total), jnp.int32)
    for end in ends:
        segr = segr + (place_row >= end).astype(jnp.int32)
    b.seg_row[...] = segr.astype(F32)
    half = HEAD_DIM // 2
    lane = lax.broadcasted_iota(jnp.int32, (1, LANES), 1)
    rate = jnp.exp(lax.rem(lane, half).astype(F32) * (-math.log(10000.0) / half))
    sign = jnp.where(lax.rem(lane, HEAD_DIM) < half, -1.0, 1.0)

    def angles(i, carry):
        rows = pl.ds(tall(i * LANES, LANES), LANES)
        place = lax.broadcasted_iota(jnp.int32, (LANES, LANES), 0) + i * LANES
        segment = jnp.zeros((LANES, LANES), jnp.int32)
        begin = jnp.zeros((LANES, LANES), jnp.int32)
        for end in ends:
            past = place >= end
            segment = segment + past.astype(jnp.int32)
            begin = jnp.where(past, end, begin)
        b.lse[rows, :] = segment.astype(F32)
        angle = (place - begin).astype(F32) * rate
        b.cos[rows, :] = jnp.cos(angle)
        b.sin[rows, :] = jnp.sin(angle) * sign
        return carry

    lax.fori_loop(0, total // LANES, angles, 0)
    loads[4].wait()
    b.dyb[me.p] = b.ig[...].astype(BF)
    loads[3].wait()
    own_units = pl.ds(tall(me.s * band + me.g * units, units), units)
    b.wf_full[:, own_units, :] = b.fg[...].astype(BF)
    for j in range(seq):
        source = lax.rem(me.s + j, seq)
        part = b.xrow.at[pl.ds(tall(source * count + me.k * halfrows, halfrows), halfrows), :]
        arrived(part, b.xr.at[source])
        remote(part, part, b.xfs.at[j], b.xfr.at[j], sib).start()
    wo_own = b.wo_full.at[pl.ds(out0, wr), :]
    wo_first = []
    for j in range(1, seq):
        to = (me.d, lax.rem(me.s + j, seq))
        wo_first.append(remote(wo_own, wo_own, b.wo1s.at[j], b.wo1r.at[j], to))
    for copy in wo_first:
        copy.start()
    for j in range(1, me.groups):
        other = lax.rem(me.g + j, me.groups)
        mine = b.wf_full.at[:, own_units, :]
        remote(
            mine, mine, b.fgs.at[j], b.fgr_sem.at[j], (other * me.group + me.p, me.s)
        ).start()
    for j in range(1, me.groups):
        mine = b.wf_full.at[:, own_units, :]
        remote(mine, mine, b.fgs.at[j], b.fgr_sem.at[j], sib).wait()

    near, far = me.s + 1 - 2 * lax.rem(me.s, 2), lax.rem(me.s + 2, seq)
    beyond = lax.rem(near + 2, seq)

    def column(m, at):
        return b.wf_full.at[m, pl.ds(tall(at * band, band), band), :]

    def unit_copy(way, m):
        part = column(m, far if way == 2 else me.s)
        to = (me.d, near if way else far)
        return remote(part, part, b.hs.at[way, m], b.hr.at[way, m], to)

    def send_units(m):
        unit_copy(0, m).start()
        unit_copy(1, m).start()

    def pass_units(m):
        arrived(column(m, far), b.hr.at[0, m])
        unit_copy(2, m).start()

    send_units(0)
    for j in range(seq):
        part = b.xrow.at[pl.ds(0, halfrows), :]
        arrived(part, b.xfr.at[j])
        last.append(functools.partial(sent, False, part, b.xfs.at[j], sib))

    def wait_wq(j, carry):
        part = b.wq_full.at[:, pl.ds(0, cr), :]
        remote(part, part, b.wq2s.at[j], b.wq2r.at[j], sib).wait()
        return carry

    lax.fori_loop(1, dp, wait_wq, 0)
    own_half.wait()
    def project(i, carry):
        rows = pl.ds(tall(i * count, count), count)
        x = b.xrow[rows, :]
        cosine = jnp.concatenate([b.cos[rows, :]] * (block // LANES), axis=1)
        sine = jnp.concatenate([b.sin[rows, :]] * (block // LANES), axis=1)
        raw = dot(x, b.wq_full[0], NN)
        b.q[rows, :] = (raw * cosine + swap_halves(raw) * sine).astype(BF)
        raw = dot(x, b.wq_full[1], NN)
        b.kk[rows, :] = (raw * cosine + swap_halves(raw) * sine).astype(BF)
        b.v[rows, :] = dot(x, b.wq_full[2], NN).astype(BF)
        return carry

    lax.fori_loop(0, seq, project, 0)
    owner = 2 * me.c + me.r
    mine = b.wo_full.at[pl.ds(crow0, cr), :]
    for copy in wo_first:
        copy.wait()
    remote(mine, mine, b.wo3s.at[0], b.wo3r.at[0], sib).start()
    for j in range(1, me.chips):
        to = 2 * lax.rem(me.c + j, me.chips) + me.k
        remote(mine, mine, b.wo2s.at[j], b.wo2r.at[j], (to, me.s)).start()
    dy_own = b.dyb.at[me.p]
    remote(dy_own, dy_own, b.dyfs.at[0], b.dyfr.at[0], sib).start()
    for j in range(1, nc):
        to = me.in_group(lax.rem(me.gc + j, nc), me.k)
        remote(dy_own, dy_own, b.dys.at[j], b.dyr.at[j], (to, me.s)).start()

    def attend(step, carry):
        i = lax.rem(me.s + step, seq)
        rows = pl.ds(tall(i * count, count), count)
        q = b.q[rows, :]
        segment = b.lse[rows, LANES - 1 : LANES]
        bias = jnp.where(segment == b.seg_row[0:1, :], 0.0, -1e30)
        lane = lax.broadcasted_iota(jnp.int32, (count, LANES), 1)
        lse = b.lse[rows, :]
        out = jnp.zeros((count, block), F32)
        for h in range(heads):
            mask = head_mask((count, block), h)
            score = dot(jnp.where(mask, q, jnp.zeros_like(q)), b.kk[...], NT) * 0.125 + bias
            top = jnp.max(score, axis=1, keepdims=True)
            weight = jnp.exp(score - top)
            tally = jnp.sum(weight, axis=1, keepdims=True)
            prob = (weight * (1.0 / tally)).astype(BF)
            out = jnp.where(mask, dot(prob, b.v[...], NN), out)
            lse = jnp.where(lane == h, top + jnp.log(tally), lse)
        b.lse[rows, :] = lse
        b.mixed[i] = out.astype(BF)
        here = jnp.logical_and(i == me.s, owner == me.d)
        send_or_keep(
            here, b.mixed.at[i], b.mixed_in.at[me.hg], b.ms.at[i], b.mr.at[me.hg], (owner, i)
        )

        return carry

    lax.fori_loop(0, seq, attend, 0)
    send_units(1)
    send_units(2)
    for j in range(1, me.chips):
        source = 2 * lax.rem(me.c + me.chips - j, me.chips) + me.k
        part = b.wo_full.at[pl.ds(tall(source * cr, cr), cr), :]
        arrived(part, b.wo2r.at[j])
        remote(part, part, b.wo3s.at[j], b.wo3r.at[j], sib).start()
        last.append(functools.partial(sent, False, part, b.wo2s.at[j], sib))
        last.append(functools.partial(sent, False, part, b.wo3s.at[j], sib))
    last.append(functools.partial(sent, False, mine, b.wo3s.at[0], sib))
    for j in range(me.chips):
        arrived(mine, b.wo3r.at[j])
    for j in range(seq):
        arrived(b.mixed_in.at[j], b.mr.at[j])
    for t in range(width // block):
        span = slice(t * block, (t + 1) * block)
        part = b.out[:, span]
        for h in range(seq):
            part = part + dot(b.mixed_in[h], b.wo_full[h * block : (h + 1) * block, span], NN)
        b.out[:, span] = part

    def second_norm(rows):
        normal, scale = normalise(b.out[rows, :])
        b.norm[rows, :] = normal
        b.scale[rows, :] = jnp.broadcast_to(scale, (some, LANES))
        b.xall[me.gc, me.k, rows, :] = (normal * b.gain[2:3, :] + b.gain[3:4, :]).astype(BF)

    by_rows(second_norm)
    x_own = b.xall.at[me.gc, me.k]
    remote(x_own, x_own, b.xfs2.at[0], b.xfr2.at[0], sib).start()
    for j in range(1, nc):
        to = me.in_group(lax.rem(me.gc + j, nc), me.k)
        remote(x_own, x_own, b.xs2.at[j], b.xr2.at[j], (to, me.s)).start()
    pass_units(0)
    for j in range(1, nc):
        source = 2 * lax.rem(me.gc + nc - j, nc) + me.k
        part = b.dyb.at[source]
        arrived(part, b.dyr.at[j])
        remote(part, part, b.dyfs.at[j], b.dyfr.at[j], sib).start()
        last.append(functools.partial(sent, False, part, b.dys.at[j], sib))
        last.append(functools.partial(sent, False, part, b.dyfs.at[j], sib))
    last.append(functools.partial(sent, False, dy_own, b.dyfs.at[0], sib))
    for j in range(nc):
        arrived(dy_own, b.dyfr.at[j])
    tile = 2 * band
    cols = 256
    near_tile = me.s // 2

    def chip_rows(j):
        cj = lax.rem(me.gc + nc - j, nc)
        return cj, pl.ds(tall(cj * 2 * count, 2 * count), 2 * count)

    def hidden(j, t):
        cj, rows = chip_rows(j)
        span = pl.ds(tall(t * tile, tile), tile)
        x = b.xall[cj].reshape(2 * count, width)
        dy = b.dyb[pl.ds(2 * cj, 2)].reshape(2 * count, width)
        gate = dot(x, b.wf_full[0, span, :], NT)
        up = dot(x, b.wf_full[1, span, :], NT)
        dh = dot(dy, b.wf_full[2, span, :], NT)
        sigma = 1.0 / (1.0 + jnp.exp(-gate))
        active = gate * sigma
        b.act[2, rows, span] = (active * up).astype(BF)
        b.act[0, rows, span] = (dh * up * (sigma * (1.0 + gate * (1.0 - sigma)))).astype(BF)
        b.act[1, rows, span] = (dh * active).astype(BF)

    def near_units(j, carry):
        cj, _ = chip_rows(j)

        @pl.when(j > 0)
        def _():
            part = b.xall.at[cj, me.k]
            arrived(part, b.xr2.at[j])
            remote(part, part, b.xfs2.at[j], b.xfr2.at[j], sib).start()

        @pl.when((j > 0) & (j < 3))
        def _():
            pass_units(j)

        arrived(b.xall.at[cj, 1 - me.k], b.xfr2.at[j])
        hidden(j, near_tile)
        return carry

    def far_units(j, carry):
        hidden(j, 1 - near_tile)
        return carry

    for m in range(3):
        arrived(column(m, near), b.hr.at[1, m])
    lax.fori_loop(0, nc, near_units, 0)
    for m in range(3):
        arrived(column(m, beyond), b.hr.at[2, m])
    lax.fori_loop(0, nc, far_units, 0)

    def take_dn2(j):
        part = b.dsib.at[j]
        remote(part, part, b.dss.at[j], b.dsr.at[j], sib).wait()
        value = b.dpart[lax.rem(j, 2), me.k].astype(F32) + b.dsib[j].astype(F32)
        b.dsum[j] = value.astype(BF)

        @pl.when(j > 0)
        def _():
            to = (me.in_group(chip_rows(j)[0], me.k), me.s)
            remote(b.dsum.at[j], b.drecv.at[j - 1], b.dps.at[j], b.dpr.at[j], to).start()

    def grad_tokens(i, carry):
        j = nc - 1 - i
        _, rows = chip_rows(j)
        for t in range(width // cols):
            span = slice(t * cols, (t + 1) * cols)
            value = dot(b.act[0, rows, :], b.wf_full[0, :, span], NN)
            value = value + dot(b.act[1, rows, :], b.wf_full[1, :, span], NN)
            b.dpart[lax.rem(j, 2), :, :, span] = value.astype(BF).reshape(2, count, cols)
        part = b.dpart.at[lax.rem(j, 2), 1 - me.k]
        remote(part, b.dsib.at[j], b.dss.at[j], b.dsr.at[j], sib).start()

        @pl.when(i > 0)
        def _():
            take_dn2(j + 1)

        return carry

    lax.fori_loop(0, nc, grad_tokens, 0)
    take_dn2(0)
    for j in range(nc):
        last.append(functools.partial(sent, False, x_own, b.xfs2.at[j], sib))
        if j:
            last.append(functools.partial(sent, False, x_own, b.xs2.at[j], sib))
    for copy in last:
        copy()
    last.clear()
    for m in range(3):
        for way in range(3):
            unit_copy(way, m).wait_send()
    bg = (b.wf_full.at[0], b.wf_full.at[1], b.down)

    def grads(t, then):
        span = pl.ds(tall(t * tile, tile), tile)
        tokens = nc * 2 * count
        for m in range(3):
            left = b.act[m, :, span].T
            for c in range(width // cols):
                part = slice(c * cols, (c + 1) * cols)
                if m < 2:
                    right = b.xall[:, :, :, part].reshape(tokens, cols)
                else:
                    right = b.dyb[:, :, part].reshape(tokens, cols)
                bg[m][span, part] = dot(left, right, NN).astype(BF)
            then(m)

    def band_rows(at):
        return pl.ds(tall(at * band, band), band)

    def send_terms(stage, at, to, m):
        src = bg[m].at[band_rows(at), :]
        remote(src, b.rs.at[stage, m], b.gs.at[stage, m], b.gr.at[stage, m], (me.d, to)).start()

    def cross_terms(m):
        arrived(b.rs.at[0, m], b.gr.at[0, m])
        value = bg[m][band_rows(far), :].astype(F32) + b.rs[0, m].astype(F32)
        bg[m][band_rows(far), :] = value.astype(BF)
        send_terms(2, far, far, m)

    grads(1 - near_tile, lambda m: send_terms(0, beyond, near, m))
    grads(near_tile, lambda m: None)
    def add_branch(j):
        arrived(b.dsib.at[j], b.bsr.at[j])
        value = b.dpart[lax.rem(j, 2), me.k].astype(F32) + b.dsib[j].astype(F32)
        value = value.astype(BF)

        @pl.when(j == 0)
        def _():
            b.xown[...] = value

        @pl.when(j > 0)
        def _():
            remote(b.dsum.at[j], b.drecv.at[j - 1], b.dps.at[j], b.dpr.at[j], sib).wait_send()
            b.dsum[j] = value
            cj = lax.rem(me.gc + nc - j, nc)
            to = (me.in_group(cj, me.k), me.s)
            remote(b.dsum.at[j], b.brr.at[j - 1], b.brs.at[j], b.brr_sem.at[j], to).start()

    def branch(i, carry):
        j = nc - 1 - i
        _, rows = chip_rows(j)

        @pl.when(i > 1)
        def _():
            sent(False, b.dpart.at[0, 0], b.bss.at[j + 2], sib)

        for t in range(width // cols):
            span = slice(t * cols, (t + 1) * cols)
            value = dot(b.act[2, rows, :], b.wf_full[2, :, span], NN)
            b.dpart[lax.rem(j, 2), :, :, span] = value.astype(BF).reshape(2, count, cols)

        @pl.when(i > 0)
        def _():
            add_branch(j + 1)

        part = b.dpart.at[lax.rem(j, 2), 1 - me.k]
        remote(part, b.dsib.at[j], b.bss.at[j], b.bsr.at[j], sib).start()
        return carry

    lax.fori_loop(0, nc, branch, 0)

    add_branch(0)
    cross_terms(0)
    for m in range(3):
        send_terms(1, near, near, m)
    for j in range(min(2, nc)):
        sent(False, b.dpart.at[0, 0], b.bss.at[j], sib)
    for j in range(1, nc):
        arrived(b.drecv.at[j - 1], b.dpr.at[j])

    def add_ln(row, value):
        for t in range(tiles):
            b.lnp[t, row : row + 1, :] += value[:, t * LANES : (t + 1) * LANES]

    b.lnp[...] = jnp.zeros_like(b.lnp)

    def second_back(rows):
        grad = b.dsum[0, rows, :].astype(F32)
        for j in range(1, nc):
            grad = grad + b.drecv[j - 1, rows, :].astype(F32)
        normal = b.norm[rows, :]
        add_ln(2, jnp.sum(grad * normal, axis=0, keepdims=True))
        add_ln(3, jnp.sum(grad, axis=0, keepdims=True))
        dmid = b.ig[rows, :] + norm_back(grad, normal, b.scale[rows, 0:1], b.gain[2:3, :])
        b.ig[rows, :] = dmid
        b.dmb[rows, :] = dmid.astype(BF)

    by_rows(second_back)
    dmb = b.dmb[...]
    for i in range(seq):
        here = jnp.logical_and(i == me.s, owner == me.d)
        sent(here, b.mixed.at[i], b.ms.at[i], sib)
    for hg in range(seq):
        b.mixed[hg] = dot(dmb, b.wo_full[hg * block : (hg + 1) * block, :], NT).astype(BF)
        to = (2 * me.c + hg % 2, me.k * me.half + hg // 2)
        here = jnp.logical_and(to[0] == me.d, to[1] == me.s)
        send_or_keep(
            here, b.mixed.at[hg], b.dmix_row.at[me.s], b.dms.at[hg], b.dmr.at[me.s], to
        )
        last.append(functools.partial(sent, here, b.mixed.at[hg], b.dms.at[hg], sib))
    pieces = width // 2 // count

    def og_rows(parity):
        return b.dyb.at[pl.ds(parity * pieces, pieces)]

    for h in range(seq):
        part = dot(b.mixed_in[h], dmb, TN).astype(BF)
        for t in range(block // cr):
            first = h * (block // cr) + t
            row = (first // 2) * cr
            b.dyb[(first % 2) * pieces + row // count, row % count : row % count + cr, :] = part[
                t * cr : (t + 1) * cr
            ]
    remote(og_rows(1 - me.k), b.ogsib, b.o1.at[0], b.o1.at[1], sib).start()
    for j in range(seq):
        arrived(b.dmix_row.at[j], b.dmr.at[j])
    for m in range(1, 3):
        cross_terms(m)
    b.dk[...] = jnp.zeros_like(b.dk)
    b.dv[...] = jnp.zeros_like(b.dv)

    def og_sum():
        remote(b.ogsib, b.ogsib, b.o1.at[0], b.o1.at[1], sib).wait()
        for i in range(pieces):
            value = b.dyb[me.k * pieces + i].astype(F32) + b.ogsib[i].astype(F32)
            b.dyb[2 * pieces + i] = value.astype(BF)

        def send_og(j, carry):
            chip = lax.rem(me.c + j, me.chips)
            row = chip * cr
            src = b.dyb.at[2 * pieces + row // count, pl.ds(tall(lax.rem(row, count), cr), cr), :]
            remote(src, b.ogpl.at[j], b.o2s.at[j], b.o2r.at[j], (2 * chip + me.k, me.s)).start()
            return carry

        lax.fori_loop(1, me.chips, send_og, 0)

    def og_column():
        row = me.c * cr
        at = pl.ds(tall(lax.rem(row, count), cr), cr)
        acc = b.dyb[2 * pieces + row // count, at, :].astype(F32)
        for j in range(1, me.chips):
            remote(b.ogpl.at[j], b.ogpl.at[j], b.o2s.at[j], b.o2r.at[j], sib).wait()
            acc = acc + b.ogpl[j].astype(F32)
        b.ogc[...] = acc.astype(BF)
        for j in range(1, seq):
            to = lax.rem(me.s + j, seq)
            src = b.ogc.at[pl.ds(tall(to * wr, wr), wr), :]
            remote(src, b.ogz.at[j], b.o3s.at[j], b.o3r.at[j], (me.d, to)).start()

    def attend_back(i, carry):
        rows = pl.ds(tall(i * count, count), count)
        q = b.q[rows, :]
        dm = b.dmix_row[i]
        lse = b.lse[rows, :]
        segment = b.lse[rows, LANES - 1 : LANES]
        bias = jnp.where(segment == b.seg_row[0:1, :], 0.0, -1e30)
        grad_q = jnp.zeros((count, block), F32)
        for h in range(heads):
            mask = head_mask((count, block), h)
            qh = jnp.where(mask, q, jnp.zeros_like(q))
            dmh = jnp.where(mask, dm, jnp.zeros_like(dm))
            score = dot(qh, b.kk[...], NT) * 0.125 + bias
            prob = jnp.exp(score - lse[:, h : h + 1])
            dprob = dot(dmh, b.v[...], NT)
            centre = jnp.sum(prob * dprob, axis=1, keepdims=True)
            ds = (0.125 * prob * (dprob - centre)).astype(BF)
            grad_q = jnp.where(mask, dot(ds, b.kk[...], NN), grad_q)
            b.dk[...] += dot(ds, qh, TN)
            b.dv[...] += dot(prob.astype(BF), dmh, TN)
        cosine = jnp.concatenate([b.cos[rows, :]] * (block // LANES), axis=1)
        sine = jnp.concatenate([b.sin[rows, :]] * (block // LANES), axis=1)
        b.act[0, rows, 0:block] = (grad_q * cosine - swap_halves(grad_q) * sine).astype(BF)

        @pl.when(i == 0)
        def _():
            og_sum()

        return carry

    lax.fori_loop(0, seq, attend_back, 0)

    def back_chunk(i):
        rows = pl.ds(tall(i * count, count), count)
        cosine = jnp.concatenate([b.cos[rows, :]] * (block // LANES), axis=1)
        sine = jnp.concatenate([b.sin[rows, :]] * (block // LANES), axis=1)
        grad_k = b.dk[rows, :]
        dk = (grad_k * cosine - swap_halves(grad_k) * sine).astype(BF)
        dv = b.dv[rows, :].astype(BF)
        b.act[1, rows, 0:block] = dk
        b.act[2, rows, 0:block] = dv
        value = dot(b.act[0, rows, 0:block], b.wq_full[0], NT)
        value = value + dot(dk, b.wq_full[1], NT) + dot(dv, b.wq_full[2], NT)
        at = lax.rem(i, 2) * me.half + i // 2
        b.xall[at // 2, lax.rem(at, 2)] = value.astype(BF)

    def other_half(j, carry):
        back_chunk(2 * j + 1 - me.k)
        return carry

    def own_half_chunks(j, carry):
        back_chunk(2 * j + me.k)
        return carry

    lax.fori_loop(0, me.half, other_half, 0)
    quarter = me.half // 2
    dn_other = b.xall.at[pl.ds((1 - me.k) * quarter, quarter)]
    remote(dn_other, b.dnsib, b.n1.at[0], b.n1.at[1], sib).start()
    lax.fori_loop(0, me.half, own_half_chunks, 0)
    remote(b.dnsib, b.dnsib, b.n1.at[0], b.n1.at[1], sib).wait()
    for j in range(me.half):
        value = b.xall[me.k * quarter + j // 2, j % 2].astype(F32)
        b.dpart[0, j] = (value + b.dnsib[j // 2, j % 2].astype(F32)).astype(BF)
        i = 2 * j + me.k
        here = jnp.logical_and(owner == me.d, i == me.s)
        send_or_keep(
            here, b.dpart.at[0, j], b.dnr.at[me.h], b.n2s.at[j], b.n2r.at[me.h], (owner, i)
        )
        last.append(functools.partial(sent, here, b.dpart.at[0, j], b.n2s.at[j], sib))
    span_rows = 2 * cr
    per_tile = block // span_rows

    def qkv_terms(j, carry):
        at = lax.rem(me.c // per_tile + j, width // block)
        x = b.xrow[:, pl.ds(tall(at * block, block), block)]
        rows = pl.ds(tall(total + at * block, block), block)
        for t in range(3):
            b.act[t, rows, 0:block] = dot(x, b.act[t, 0:total, 0:block], TN).astype(BF)
        for i in range(per_tile):
            chip = at * per_tile + i

            @pl.when(chip != me.c)
            def _(chip=chip):
                src = b.act.at[:, pl.ds(tall(total + chip * span_rows, span_rows), span_rows), 0:block]
                to = (2 * chip + me.k, me.s)
                remote(src, b.qgpl.at[me.c], b.q1s.at[chip], b.q1r.at[me.c], to).start()

        return carry

    lax.fori_loop(1, width // block, qkv_terms, 0)
    qkv_terms(0, 0)
    og_column()
    tok = local(b.tok, b.norm, b.load.at[0])
    tok.start()
    tok.wait()
    for h in range(me.half):
        arrived(b.dnr.at[h], b.n2r.at[h])

    def first_back(rows):
        grad = b.dnr[0, rows, :].astype(F32)
        for h in range(1, me.half):
            grad = grad + b.dnr[h, rows, :].astype(F32)
        normal, scale = normalise(b.norm[rows, :])
        b.ig[rows, :] += norm_back(grad, normal, scale, b.gain[0:1, :])
        add_ln(0, jnp.sum(grad * normal, axis=0, keepdims=True))
        add_ln(1, jnp.sum(grad, axis=0, keepdims=True))

    by_rows(first_back)
    store(1)

    def send_lnp(j, carry):
        other = lax.rem(me.n + j, me.total)
        remote(
            b.lnp.at[other // per], b.lnr.at[me.n], b.lnt.at[0], b.lnt.at[1], me.of_rank(other)
        ).start()
        return carry

    lax.fori_loop(1, me.total, send_lnp, 0)
    b.lnr[me.n] = b.lnp[me.n // per]
    own = pl.ds(tall(total + me.c * span_rows, span_rows), span_rows)
    sums = [b.act[t, own, 0:block].astype(F32) for t in range(3)]
    for j in range(1, me.chips):
        chip = lax.rem(me.c + j, me.chips)
        part = b.qgpl.at[chip]
        remote(part, part, b.q1s.at[chip], b.q1r.at[chip], sib).wait()
        for t in range(3):
            sums[t] = sums[t] + b.qgpl[chip, t].astype(F32)
    for t in range(3):
        b.qgc[t] = sums[t].astype(BF)
    source = me.k * seq + me.s
    for core in range(2):
        for j in range(seq):
            to = lax.rem(me.s + j, seq)
            src = b.qgc.at[:, pl.ds(tall((core * seq + to) * wr, wr), wr), :]
            here = jnp.logical_and(core == me.k, to == me.s)
            send_or_keep(
                here, src, b.qgz.at[source], b.q2s.at[core, j], b.q2r.at[source], (2 * me.c + core, to)
            )
            last.append(functools.partial(sent, here, src, b.q2s.at[core, j], sib))
    value = b.out[...] + b.xown[...].astype(F32)
    for j in range(1, nc):
        remote(b.brr.at[j - 1], b.brr.at[j - 1], b.brs.at[j], b.brr_sem.at[j], sib).wait()
        value = value + b.brr[j - 1].astype(F32)
    b.out[...] = value
    store(0)
    acc = b.ogc[pl.ds(tall(me.s * wr, wr), wr), :].astype(F32)
    for j in range(1, seq):
        remote(b.ogz.at[j], b.ogz.at[j], b.o3s.at[j], b.o3r.at[j], sib).wait()
        acc = acc + b.ogz[j].astype(F32)
    b.og[...] = acc
    store(4)
    for m in range(3):
        for j in range(1, 3):
            arrived(b.rs.at[j, m], b.gr.at[j, m])
        for j in range(3):
            last.append(functools.partial(sent, False, b.rs.at[0, 0], b.gs.at[j, m], sib))
        acc = bg[m][band_rows(me.s), :].astype(F32)
        acc = acc + b.rs[1, m].astype(F32) + b.rs[2, m].astype(F32)
        if me.groups == 1:
            b.fg[m] = acc
        else:
            bg[m][band_rows(me.s), :] = acc.astype(BF)
    if me.groups > 1:
        for m in range(3):
            for j in range(1, me.groups):
                other = lax.rem(me.g + j, me.groups)
                src = bg[m].at[pl.ds(tall(me.s * band + other * units, units), units), :]
                to = (other * me.group + me.p, me.s)
                remote(src, b.grp.at[j, m], b.grs.at[j, m], b.grr.at[j, m], to).start()
        for m in range(3):
            acc = bg[m][pl.ds(tall(me.s * band + me.g * units, units), units), :].astype(F32)
            for j in range(1, me.groups):
                part = b.grp.at[j, m]
                remote(part, part, b.grs.at[j, m], b.grr.at[j, m], sib).wait()
                acc = acc + b.grp[j, m].astype(F32)
            b.fg[m] = acc
    store(5)
    rest = b.lnr.at[pl.ds(0, me.total - 1)]
    remote(rest, rest, b.lnt.at[0], b.lnt.at[1], sib).wait()
    acc = b.lnr[0]
    for j in range(1, me.total):
        acc = acc + b.lnr[j]
    for i in range(fit):

        @pl.when(lax.rem(me.n, fit) == i)
        def _(i=i):
            b.lng[...] = acc[0:4, i * share : (i + 1) * share]

    store(2)
    for j in range(2 * seq):
        arrived(b.qgz.at[j], b.q2r.at[j])
    for hg in range(seq):
        core, h = hg % 2, hg // 2
        acc = b.qgz[core * seq + h].astype(F32) + b.qgz[core * seq + me.half + h].astype(F32)
        b.qg[:, :, hg * block : (hg + 1) * block] = acc
    store(3)
    for copy in last:
        copy()
    for copy in stores:
        copy.wait()


def keep_kernel(count, *refs):
    given, kept, held = refs[:count], refs[count : 2 * count], refs[2 * count : 3 * count]
    sems = refs[-1]
    ins = [local(given[i], held[i], sems.at[0, i]) for i in range(count)]
    outs = [local(held[i], kept[i], sems.at[1, i]) for i in range(count)]
    for copy in ins:
        copy.start()
    for i in range(count):
        ins[i].wait()
        outs[i].start()
    for copy in outs:
        copy.wait()


def body(dp, seq, tokens, ln_params, qkv_weight, out_weight, ffn_weight, lengths, cotangent):
    count, width = tokens.shape[1], tokens.shape[2]
    ranks = dp * seq
    total = count * seq
    wr = qkv_weight.shape[0]
    cr = wr * seq
    units = ffn_weight.shape[0]
    block = width // seq
    half = seq // 2
    group = min(dp, GROUP)
    groups = dp // group
    gchips, chips, slots = group // 2, dp // 2, groups * seq
    held = units * slots
    share = ln_params.shape[1]
    sem = pltpu.SemaphoreType.DMA
    vm = pltpu.VMEM
    anywhere = pl.BlockSpec(memory_space=pl.ANY)
    vmem = pl.BlockSpec(memory_space=pltpu.VMEM)
    operands = dict(
        tok=(tokens.reshape(count, width), anywhere),
        ln=(ln_params, vmem),
        wq=(qkv_weight.transpose(1, 0, 2), anywhere),
        wo=(out_weight, anywhere),
        wf=(ffn_weight.transpose(1, 0, 2), anywhere),
        lens=(lengths, vmem),
        cot=(cotangent.reshape(count, width), anywhere),
    )
    outs = dict(
        out=(count, width),
        ig=(count, width),
        lng=(4, share),
        qg=(3, wr, width),
        og=(wr, width),
        fg=(3, units, width),
    )
    scratch = dict(
        **{name: vm(dims, F32) for name, dims in outs.items()},
        norm=vm((count, width), F32),
        scale=vm((count, LANES), F32),
        lens_own=vm((8, LANES), jnp.int32),
        lens_pair=vm((2, 8, LANES), jnp.int32),
        ln_own=vm((8, LANES), F32),
        ln_all=vm((ranks, 8, LANES), F32),
        gain=vm((8, width), F32),
        wq_own=vm((3, wr, width), BF),
        wcol=vm((3, cr, 2 * block), BF),
        xown=vm((count, width), BF),
        dmb=vm((count, width), BF),
        xrow=vm((total, width), BF),
        wq_full=vm((3, width, block), BF),
        wo_full=vm((width, width), BF),
        dyb=vm((group, count, width), BF),
        q=vm((total, block), BF),
        kk=vm((total, block), BF),
        v=vm((total, block), BF),
        lse=vm((total, LANES), F32),
        cos=vm((total, LANES), F32),
        sin=vm((total, LANES), F32),
        seg_row=vm((8, total), F32),
        mixed=vm((seq, count, block), BF),
        mixed_in=vm((seq, count, block), BF),
        dmix_row=vm((seq, count, block), BF),
        wf_full=vm((3, held, width), BF),
        xall=vm((gchips, 2, count, width), BF),
        act=vm((3, group * count, held), BF),
        dpart=vm((2, 2, count, width), BF),
        dsib=vm((gchips, count, width), BF),
        dsum=vm((gchips, count, width), BF),
        drecv=vm((gchips - 1, count, width), BF),
        brr=vm((gchips - 1, count, width), BF),
        ogsib=vm((width // 2 // count, count, width), BF),
        ogpl=vm((chips, cr, width), BF),
        ogc=vm((cr, width), BF),
        ogz=vm((seq, wr, width), BF),
        dk=vm((total, block), F32),
        dv=vm((total, block), F32),
        dnsib=vm((half // 2, 2, count, width), BF),
        dnr=vm((half, count, width), BF),
        qgpl=vm((chips, 3, 2 * cr, block), BF),
        qgc=vm((3, 2 * cr, block), BF),
        qgz=vm((2 * seq, 3, wr, block), BF),
        rs=vm((3, 3, groups * units, width), BF),
        grp=vm((groups, 3, units, width) if groups > 1 else (8, LANES), BF),
        down=vm((held, width), BF),
        lnp=vm((width // LANES, 8, LANES), F32),
        lnr=vm((ranks, 8, LANES), F32),
        load=sem((7,)),
        keep=sem((6,)),
        lns=sem((2,)),
        lens_sem=sem((2,)),
        wq1s=sem((seq,)),
        wq1r=sem((seq,)),
        wq2s=sem((dp,)),
        wq2r=sem((dp,)),
        wo1s=sem((seq,)),
        wo1r=sem((seq,)),
        wo2s=sem((chips,)),
        wo2r=sem((chips,)),
        wo3s=sem((chips,)),
        wo3r=sem((chips,)),
        xs=sem((half, 2)),
        xr=sem((seq,)),
        xfs=sem((seq,)),
        xfr=sem((seq,)),
        dys=sem((gchips,)),
        dyr=sem((gchips,)),
        dyfs=sem((gchips,)),
        dyfr=sem((gchips,)),
        fgs=sem((groups,)),
        fgr_sem=sem((groups,)),
        hs=sem((3, 3)),
        hr=sem((3, 3)),
        ms=sem((seq,)),
        mr=sem((seq,)),
        xs2=sem((gchips,)),
        xr2=sem((gchips,)),
        xfs2=sem((gchips,)),
        xfr2=sem((gchips,)),
        dss=sem((gchips,)),
        dsr=sem((gchips,)),
        dps=sem((gchips,)),
        dpr=sem((gchips,)),
        bss=sem((gchips,)),
        bsr=sem((gchips,)),
        brs=sem((gchips,)),
        brr_sem=sem((gchips,)),
        dms=sem((seq,)),
        dmr=sem((seq,)),
        gs=sem((3, 3)),
        gr=sem((3, 3)),
        grs=sem((groups, 3)),
        grr=sem((groups, 3)),
        o1=sem((2,)),
        o2s=sem((chips,)),
        o2r=sem((chips,)),
        o3s=sem((seq,)),
        o3r=sem((seq,)),
        n1=sem((2,)),
        n2s=sem((half,)),
        n2r=sem((half,)),
        q1s=sem((chips,)),
        q1r=sem((chips,)),
        q2s=sem((2, seq)),
        q2r=sem((2 * seq,)),
        lnt=sem((2,)),
    )
    names = (*operands, *[name + "_out" for name in outs], *scratch)
    results = pl.pallas_call(
        functools.partial(layer_kernel, names, dp, seq, lengths.shape[1]),
        out_shape=tuple(jax.ShapeDtypeStruct(dims, F32) for dims in outs.values()),
        in_specs=[spec for _, spec in operands.values()],
        out_specs=tuple([anywhere] * len(outs)),
        scratch_shapes=list(scratch.values()),
        compiler_params=pltpu.CompilerParams(
            collective_id=1, has_side_effects=True, vmem_limit_bytes=VMEM_BYTES
        ),
        cost_estimate=pl.CostEstimate(
            flops=32 * 10**9, bytes_accessed=2**24, transcendentals=10**7
        ),
        name="layer",
    )(*[value for value, _ in operands.values()])
    out, input_grad, ln_grad, qg, og, fg = pl.pallas_call(
        functools.partial(keep_kernel, len(outs)),
        out_shape=tuple(jax.ShapeDtypeStruct(dims, F32) for dims in outs.values()),
        in_specs=[anywhere] * len(outs),
        out_specs=tuple([anywhere] * len(outs)),
        scratch_shapes=[*[vm(dims, F32) for dims in outs.values()], sem((2, len(outs)))],
        name="keep",
    )(*results)
    return (
        out.reshape(1, count, width),
        input_grad.reshape(1, count, width),
        ln_grad,
        qg.transpose(1, 0, 2),
        og,
        fg.transpose(1, 0, 2),
    )


def solution(mesh):
    dp, seq = mesh.shape["dp"], mesh.shape["seq"]
    both = ("dp", "seq")
    in_specs = (
        P("dp", "seq", None),
        P(None, both),
        P(both, None, None),
        P(both, None),
        P(both, None, None),
        P("dp", None),
        P("dp", "seq", None),
    )
    out_specs = (
        P("dp", "seq", None),
        P("dp", "seq", None),
        P(None, both),
        P(both, None, None),
        P(both, None),
        P(both, None, None),
    )
    return jax.shard_map(
        functools.partial(body, dp, seq),
        mesh=mesh,
        in_specs=in_specs,
        out_specs=out_specs,
        check_vma=False,
    )
```

```python
import functools
import math
import types

import jax
import jax.numpy as jnp
from jax import lax
from jax.experimental import pallas as pl
from jax.experimental.pallas import tpu as pltpu
from jax.sharding import PartitionSpec as P

HEAD_DIM = 64
GROUP = 8
LANES = 128
BF = jnp.bfloat16
F32 = jnp.float32
MESH = pl.DeviceIdType.MESH
NT = (((1,), (1,)), ((), ()))
NN = (((1,), (0,)), ((), ()))
TN = (((0,), (0,)), ((), ()))
EPS = 1e-05
VMEM_BYTES = 62 * 2**20


def dot(a, b, dims):
    return lax.dot_general(a, b, dims, preferred_element_type=F32)


def remote(src, dst, send, recv, device):
    return pltpu.make_async_remote_copy(
        src_ref=src, dst_ref=dst, send_sem=send, recv_sem=recv, device_id=device, device_id_type=MESH
    )


def local(src, dst, sem):
    return pltpu.make_async_copy(src, dst, sem)


class Place:
    def __init__(self, dp, seq):
        self.dp, self.seq = dp, seq
        self.d, self.s = lax.axis_index("dp"), lax.axis_index("seq")
        self.c, self.k = self.d // 2, lax.rem(self.d, 2)
        self.sib = self.d + 1 - 2 * self.k
        self.chips = dp // 2
        self.group = min(dp, GROUP)
        self.groups = dp // self.group
        self.g, self.p = self.d // self.group, lax.rem(self.d, self.group)
        self.gc = self.p // 2
        self.gchips = self.group // 2
        self.half = seq // 2
        self.r, self.h = self.s // self.half, lax.rem(self.s, self.half)
        self.hg = 2 * self.h + self.k
        self.n = self.d * seq + self.s
        self.total = dp * seq

    def of_rank(self, rank):
        return (rank // self.seq, lax.rem(rank, self.seq))

    def in_group(self, chip, core):
        return self.g * self.group + 2 * chip + core


def normalise(value):
    mean = jnp.mean(value, axis=-1, keepdims=True)
    centred = value - mean
    var = jnp.mean(centred * centred, axis=-1, keepdims=True)
    scale = lax.rsqrt(var + EPS)
    return centred * scale, scale


def norm_back(grad, normal, scale, gain):
    scaled = grad * gain
    return scale * (
        scaled
        - jnp.mean(scaled, axis=-1, keepdims=True)
        - normal * jnp.mean(scaled * normal, axis=-1, keepdims=True)
    )


def swap_halves(value):
    half = HEAD_DIM // 2
    width = value.shape[1]
    lane = lax.broadcasted_iota(jnp.int32, value.shape, 1)
    up = pltpu.roll(value, width - half, 1)
    down = pltpu.roll(value, half, 1)
    return jnp.where(lax.rem(lane, HEAD_DIM) < half, up, down)


def head_mask(shape, h):
    lane = lax.broadcasted_iota(jnp.int32, shape, 1)
    return jnp.logical_and(lane >= h * HEAD_DIM, lane < (h + 1) * HEAD_DIM)


def tall(value, rows):
    return pl.multiple_of(value, rows)


def meet(me):
    barrier = pltpu.get_barrier_semaphore()

    def hello(j, carry):
        other = lax.rem(me.n + j, me.total)
        pl.semaphore_signal(barrier, inc=1, device_id=me.of_rank(other), device_id_type=MESH)
        return carry

    lax.fori_loop(1, me.total, hello, 0)


def met(me):
    pl.semaphore_wait(pltpu.get_barrier_semaphore(), me.total - 1)


def send_or_keep(here, src, dst, send, recv, device):
    @pl.when(jnp.logical_not(here))
    def _():
        remote(src, dst, send, recv, device).start()

    @pl.when(here)
    def _():
        local(src, dst, recv).start()


def sent(here, src, send, device):
    @pl.when(jnp.logical_not(here))
    def _():
        remote(src, src, send, send, device).wait_send()


def arrived(dst, recv):
    local(dst, dst, recv).wait()


def layer_kernel(names, dp, seq, segs, *refs):
    b = types.SimpleNamespace(**dict(zip(names, refs)))
    me = Place(dp, seq)
    count, width = b.out.shape
    total = count * seq
    wr = b.og.shape[0]
    cr = wr * seq
    block = b.q.shape[1]
    heads = block // HEAD_DIM
    units = b.fg.shape[1]
    held = b.wf_full.shape[1]
    band = me.groups * units
    nc = me.gchips
    sib = (me.sib, me.s)
    share = b.ln.shape[1]
    fit = LANES // share
    tiles = width // LANES
    per = me.total // tiles
    halfrows = count // 2
    last = []

    def by_rows(step):
        def one(i, carry):
            step(pl.ds(tall(i * some, some), some))
            return carry

        lax.fori_loop(0, count // some, one, 0)

    some = 64
    results = ("out", "ig", "lng", "qg", "og", "fg")
    stores = []

    def store(i):
        name = results[i]
        stores.append(local(getattr(b, name), getattr(b, name + "_out"), b.keep.at[i]))
        stores[-1].start()

    meet(me)
    loads = [
        local(b.tok, b.out, b.load.at[0]),
        local(b.wq, b.qg, b.load.at[1]),
        local(b.wo, b.og, b.load.at[2]),
        local(b.wf, b.fg, b.load.at[3]),
        local(b.cot, b.ig, b.load.at[4]),
    ]
    for copy in loads:
        copy.start()
    b.lens_own[...] = jnp.zeros_like(b.lens_own)
    b.lens_own[0:1, 0:segs] = b.lens[...]
    b.lens_pair[me.k] = b.lens_own[...]
    gains = jnp.concatenate([b.ln[...].astype(BF).astype(F32)] * fit, axis=1)
    lane = lax.broadcasted_iota(jnp.int32, gains.shape, 1)
    b.ln_own[...] = jnp.zeros_like(b.ln_own)
    b.ln_own[0:4, :] = jnp.where(lane // share == lax.rem(me.n, fit), gains, 0.0)
    b.ln_all[me.n] = b.ln_own[...]
    loads[1].wait()
    b.wq_own[...] = b.qg[...].astype(BF)
    loads[0].wait()

    def first_norm(rows):
        b.norm[rows, :] = normalise(b.out[rows, :])[0]

    by_rows(first_norm)
    met(me)

    def send_ln(j, carry):
        other = lax.rem(me.n + j, me.total)
        remote(
            b.ln_own, b.ln_all.at[me.n], b.lns.at[0], b.lns.at[1], me.of_rank(other)
        ).start()
        return carry

    lax.fori_loop(1, me.total, send_ln, 0)
    len_copy = remote(b.lens_own, b.lens_pair.at[me.k], b.lens_sem.at[0], b.lens_sem.at[1], sib)
    len_copy.start()
    pair = 2 * block
    row0 = tall(me.s * wr, wr)
    out0 = tall(me.n * wr, wr)
    wq_first = []
    for j in range(1, seq):
        to = lax.rem(me.s + j, seq)
        col = tall(lax.rem(to, me.half) * pair, pair)
        wq_first.append(
            remote(
                b.wq_own.at[:, :, pl.ds(col, pair)],
                b.wcol.at[:, pl.ds(row0, wr), :],
                b.wq1s.at[j],
                b.wq1r.at[j],
                (me.d, to),
            )
        )
    for copy in wq_first:
        copy.start()
    own_wq = local(
        b.wq_own.at[:, :, pl.ds(tall(me.h * pair, pair), pair)],
        b.wcol.at[:, pl.ds(row0, wr), :],
        b.load.at[5],
    )
    own_wq.start()
    loads[2].wait()
    b.wo_full[pl.ds(out0, wr), :] = b.og[...].astype(BF)
    rest = b.ln_all.at[pl.ds(0, me.total - 1)]
    remote(rest, rest, b.lns.at[0], b.lns.at[1], sib).wait()
    for t in range(tiles):
        part = b.ln_all[t * per]
        for i in range(1, per):
            part = part + b.ln_all[t * per + i]
        b.gain[:, t * LANES : (t + 1) * LANES] = part

    def first_out(rows):
        b.xown[rows, :] = (b.norm[rows, :] * b.gain[0:1, :] + b.gain[1:2, :]).astype(BF)

    by_rows(first_out)
    rows0 = tall(me.s * count, count)
    for j in range(me.half):
        to = me.k * me.half + lax.rem(me.h + j, me.half)
        for core in range(2):
            src = b.xown.at[pl.ds(core * halfrows, halfrows), :]
            dst = b.xrow.at[pl.ds(rows0 + core * halfrows, halfrows), :]
            here = jnp.logical_and(to == me.s, core == me.k)
            send_or_keep(
                here, src, dst, b.xs.at[j, core], b.xr.at[me.s], (2 * me.c + core, to)
            )
            last.append(
                functools.partial(sent, here, src, b.xs.at[j, core], (2 * me.c + core, to))
            )
    for copy in wq_first:
        copy.wait()
    own_wq.wait()
    crow0 = tall(me.d * cr, cr)

    def send_wq(j, carry):
        to = lax.rem(me.d + j, dp)
        remote(
            b.wcol.at[:, :, pl.ds(tall(lax.rem(to, 2) * block, block), block)],
            b.wq_full.at[:, pl.ds(crow0, cr), :],
            b.wq2s.at[j],
            b.wq2r.at[j],
            (to, me.s),
        ).start()
        return carry

    lax.fori_loop(1, dp, send_wq, 0)
    own_half = local(
        b.wcol.at[:, :, pl.ds(tall(me.k * block, block), block)],
        b.wq_full.at[:, pl.ds(crow0, cr), :],
        b.load.at[6],
    )
    own_half.start()
    len_copy.wait()
    row = b.lens_pair[me.r]
    place_row = lax.broadcasted_iota(jnp.int32, (8, total), 1)
    ends = [row[0:1, 0:1]]
    for j in range(1, segs):
        ends.append(ends[-1] + row[0:1, j : j + 1])
    segr = jnp.zeros((8, total), jnp.int32)
    for end in ends:
        segr = segr + (place_row >= end).astype(jnp.int32)
    b.seg_row[...] = segr.astype(F32)
    half = HEAD_DIM // 2
    lane = lax.broadcasted_iota(jnp.int32, (1, LANES), 1)
    rate = jnp.exp(lax.rem(lane, half).astype(F32) * (-math.log(10000.0) / half))
    sign = jnp.where(lax.rem(lane, HEAD_DIM) < half, -1.0, 1.0)

    def angles(i, carry):
        rows = pl.ds(tall(i * LANES, LANES), LANES)
        place = lax.broadcasted_iota(jnp.int32, (LANES, LANES), 0) + i * LANES
        segment = jnp.zeros((LANES, LANES), jnp.int32)
        begin = jnp.zeros((LANES, LANES), jnp.int32)
        for end in ends:
            past = place >= end
            segment = segment + past.astype(jnp.int32)
            begin = jnp.where(past, end, begin)
        b.lse[rows, :] = segment.astype(F32)
        angle = (place - begin).astype(F32) * rate
        b.cos[rows, :] = jnp.cos(angle)
        b.sin[rows, :] = jnp.sin(angle) * sign
        return carry

    lax.fori_loop(0, total // LANES, angles, 0)
    loads[4].wait()
    b.dyb[me.p] = b.ig[...].astype(BF)
    loads[3].wait()
    own_units = pl.ds(tall(me.s * band + me.g * units, units), units)
    b.wf_full[:, own_units, :] = b.fg[...].astype(BF)
    for j in range(seq):
        source = lax.rem(me.s + j, seq)
        part = b.xrow.at[pl.ds(tall(source * count + me.k * halfrows, halfrows), halfrows), :]
        arrived(part, b.xr.at[source])
        remote(part, part, b.xfs.at[j], b.xfr.at[j], sib).start()
    wo_own = b.wo_full.at[pl.ds(out0, wr), :]
    wo_first = []
    for j in range(1, seq):
        to = (me.d, lax.rem(me.s + j, seq))
        wo_first.append(remote(wo_own, wo_own, b.wo1s.at[j], b.wo1r.at[j], to))
    for copy in wo_first:
        copy.start()
    for j in range(1, me.groups):
        other = lax.rem(me.g + j, me.groups)
        mine = b.wf_full.at[:, own_units, :]
        remote(
            mine, mine, b.fgs.at[j], b.fgr_sem.at[j], (other * me.group + me.p, me.s)
        ).start()
    for j in range(1, me.groups):
        mine = b.wf_full.at[:, own_units, :]
        remote(mine, mine, b.fgs.at[j], b.fgr_sem.at[j], sib).wait()

    near, far = me.s + 1 - 2 * lax.rem(me.s, 2), lax.rem(me.s + 2, seq)
    beyond = lax.rem(near + 2, seq)

    def column(m, at):
        return b.wf_full.at[m, pl.ds(tall(at * band, band), band), :]

    def unit_copy(way, m):
        part = column(m, far if way == 2 else me.s)
        to = (me.d, near if way else far)
        return remote(part, part, b.hs.at[way, m], b.hr.at[way, m], to)

    def send_units(m):
        unit_copy(0, m).start()
        unit_copy(1, m).start()

    def pass_units(m):
        arrived(column(m, far), b.hr.at[0, m])
        unit_copy(2, m).start()

    for j in range(seq):
        part = b.xrow.at[pl.ds(0, halfrows), :]
        arrived(part, b.xfr.at[j])
        last.append(functools.partial(sent, False, part, b.xfs.at[j], sib))

    def wait_wq(j, carry):
        part = b.wq_full.at[:, pl.ds(0, cr), :]
        remote(part, part, b.wq2s.at[j], b.wq2r.at[j], sib).wait()
        return carry

    lax.fori_loop(1, dp, wait_wq, 0)
    own_half.wait()
    def project(i, carry):
        rows = pl.ds(tall(i * count, count), count)
        x = b.xrow[rows, :]
        cosine = jnp.concatenate([b.cos[rows, :]] * (block // LANES), axis=1)
        sine = jnp.concatenate([b.sin[rows, :]] * (block // LANES), axis=1)
        raw = dot(x, b.wq_full[0], NN)
        b.q[rows, :] = (raw * cosine + swap_halves(raw) * sine).astype(BF)
        raw = dot(x, b.wq_full[1], NN)
        b.kk[rows, :] = (raw * cosine + swap_halves(raw) * sine).astype(BF)
        b.v[rows, :] = dot(x, b.wq_full[2], NN).astype(BF)
        return carry

    lax.fori_loop(0, seq, project, 0)
    owner = 2 * me.c + me.r
    mine = b.wo_full.at[pl.ds(crow0, cr), :]
    for copy in wo_first:
        copy.wait()
    remote(mine, mine, b.wo3s.at[0], b.wo3r.at[0], sib).start()
    for j in range(1, me.chips):
        to = 2 * lax.rem(me.c + j, me.chips) + me.k
        remote(mine, mine, b.wo2s.at[j], b.wo2r.at[j], (to, me.s)).start()
    dy_own = b.dyb.at[me.p]
    remote(dy_own, dy_own, b.dyfs.at[0], b.dyfr.at[0], sib).start()
    for j in range(1, nc):
        to = me.in_group(lax.rem(me.gc + j, nc), me.k)
        remote(dy_own, dy_own, b.dys.at[j], b.dyr.at[j], (to, me.s)).start()

    def attend(step, carry):
        i = lax.rem(me.s + step, seq)
        rows = pl.ds(tall(i * count, count), count)
        q = b.q[rows, :]
        segment = b.lse[rows, LANES - 1 : LANES]
        bias = jnp.where(segment == b.seg_row[0:1, :], 0.0, -1e30)
        lane = lax.broadcasted_iota(jnp.int32, (count, LANES), 1)
        lse = b.lse[rows, :]
        out = jnp.zeros((count, block), F32)
        for h in range(heads):
            mask = head_mask((count, block), h)
            score = dot(jnp.where(mask, q, jnp.zeros_like(q)), b.kk[...], NT) * 0.125 + bias
            top = jnp.max(score, axis=1, keepdims=True)
            weight = jnp.exp(score - top)
            tally = jnp.sum(weight, axis=1, keepdims=True)
            prob = (weight * (1.0 / tally)).astype(BF)
            out = jnp.where(mask, dot(prob, b.v[...], NN), out)
            lse = jnp.where(lane == h, top + jnp.log(tally), lse)
        b.lse[rows, :] = lse
        b.mixed[i] = out.astype(BF)
        here = jnp.logical_and(i == me.s, owner == me.d)
        send_or_keep(
            here, b.mixed.at[i], b.mixed_in.at[me.hg], b.ms.at[i], b.mr.at[me.hg], (owner, i)
        )

        return carry

    lax.fori_loop(0, seq, attend, 0)
    for m in range(3):
        send_units(m)
    for j in range(1, me.chips):
        source = 2 * lax.rem(me.c + me.chips - j, me.chips) + me.k
        part = b.wo_full.at[pl.ds(tall(source * cr, cr), cr), :]
        arrived(part, b.wo2r.at[j])
        remote(part, part, b.wo3s.at[j], b.wo3r.at[j], sib).start()
        last.append(functools.partial(sent, False, part, b.wo2s.at[j], sib))
        last.append(functools.partial(sent, False, part, b.wo3s.at[j], sib))
    last.append(functools.partial(sent, False, mine, b.wo3s.at[0], sib))
    for j in range(me.chips):
        arrived(mine, b.wo3r.at[j])
    for j in range(seq):
        arrived(b.mixed_in.at[j], b.mr.at[j])
    for t in range(width // block):
        span = slice(t * block, (t + 1) * block)
        part = b.out[:, span]
        for h in range(seq):
            part = part + dot(b.mixed_in[h], b.wo_full[h * block : (h + 1) * block, span], NN)
        b.out[:, span] = part

    def second_norm(rows):
        normal, scale = normalise(b.out[rows, :])
        b.norm[rows, :] = normal
        b.scale[rows, :] = jnp.broadcast_to(scale, (some, LANES))
        b.xall[me.gc, me.k, rows, :] = (normal * b.gain[2:3, :] + b.gain[3:4, :]).astype(BF)

    by_rows(second_norm)
    x_own = b.xall.at[me.gc, me.k]
    remote(x_own, x_own, b.xfs2.at[0], b.xfr2.at[0], sib).start()
    for j in range(1, nc):
        to = me.in_group(lax.rem(me.gc + j, nc), me.k)
        remote(x_own, x_own, b.xs2.at[j], b.xr2.at[j], (to, me.s)).start()
    pass_units(0)
    for j in range(1, nc):
        source = 2 * lax.rem(me.gc + nc - j, nc) + me.k
        part = b.dyb.at[source]
        arrived(part, b.dyr.at[j])
        remote(part, part, b.dyfs.at[j], b.dyfr.at[j], sib).start()
        last.append(functools.partial(sent, False, part, b.dys.at[j], sib))
        last.append(functools.partial(sent, False, part, b.dyfs.at[j], sib))
    last.append(functools.partial(sent, False, dy_own, b.dyfs.at[0], sib))
    for j in range(nc):
        arrived(dy_own, b.dyfr.at[j])
    tile = 2 * band
    cols = 256
    near_tile = me.s // 2

    def chip_rows(j):
        cj = lax.rem(me.gc + nc - j, nc)
        return cj, pl.ds(tall(cj * 2 * count, 2 * count), 2 * count)

    def hidden(j, t):
        cj, rows = chip_rows(j)
        span = pl.ds(tall(t * tile, tile), tile)
        x = b.xall[cj].reshape(2 * count, width)
        dy = b.dyb[pl.ds(2 * cj, 2)].reshape(2 * count, width)
        gate = dot(x, b.wf_full[0, span, :], NT)
        up = dot(x, b.wf_full[1, span, :], NT)
        dh = dot(dy, b.wf_full[2, span, :], NT)
        sigma = 1.0 / (1.0 + jnp.exp(-gate))
        active = gate * sigma
        b.act[2, rows, span] = (active * up).astype(BF)
        b.act[0, rows, span] = (dh * up * (sigma * (1.0 + gate * (1.0 - sigma)))).astype(BF)
        b.act[1, rows, span] = (dh * active).astype(BF)

    def near_units(j, carry):
        cj, _ = chip_rows(j)

        @pl.when(j > 0)
        def _():
            part = b.xall.at[cj, me.k]
            arrived(part, b.xr2.at[j])
            remote(part, part, b.xfs2.at[j], b.xfr2.at[j], sib).start()

        @pl.when((j > 0) & (j < 3))
        def _():
            pass_units(j)

        arrived(b.xall.at[cj, 1 - me.k], b.xfr2.at[j])
        hidden(j, near_tile)
        return carry

    def far_units(j, carry):
        hidden(j, 1 - near_tile)
        return carry

    for m in range(3):
        arrived(column(m, near), b.hr.at[1, m])
    lax.fori_loop(0, nc, near_units, 0)
    for m in range(3):
        arrived(column(m, beyond), b.hr.at[2, m])
    lax.fori_loop(0, nc, far_units, 0)

    def take_dn2(j):
        part = b.dsib.at[j]
        remote(part, part, b.dss.at[j], b.dsr.at[j], sib).wait()
        value = b.dpart[lax.rem(j, 2), me.k].astype(F32) + b.dsib[j].astype(F32)
        b.dsum[j] = value.astype(BF)

        @pl.when(j > 0)
        def _():
            to = (me.in_group(chip_rows(j)[0], me.k), me.s)
            remote(b.dsum.at[j], b.drecv.at[j - 1], b.dps.at[j], b.dpr.at[j], to).start()

    def grad_tokens(i, carry):
        j = nc - 1 - i
        _, rows = chip_rows(j)
        for t in range(width // cols):
            span = slice(t * cols, (t + 1) * cols)
            value = dot(b.act[0, rows, :], b.wf_full[0, :, span], NN)
            value = value + dot(b.act[1, rows, :], b.wf_full[1, :, span], NN)
            b.dpart[lax.rem(j, 2), :, :, span] = value.astype(BF).reshape(2, count, cols)
        part = b.dpart.at[lax.rem(j, 2), 1 - me.k]
        remote(part, b.dsib.at[j], b.dss.at[j], b.dsr.at[j], sib).start()

        @pl.when(i > 0)
        def _():
            take_dn2(j + 1)

        return carry

    lax.fori_loop(0, nc, grad_tokens, 0)
    take_dn2(0)
    for j in range(nc):
        last.append(functools.partial(sent, False, x_own, b.xfs2.at[j], sib))
        if j:
            last.append(functools.partial(sent, False, x_own, b.xs2.at[j], sib))
    for copy in last:
        copy()
    last.clear()
    for m in range(3):
        for way in range(3):
            unit_copy(way, m).wait_send()
    bg = (b.wf_full.at[0], b.wf_full.at[1], b.down)

    def grads(t, then):
        span = pl.ds(tall(t * tile, tile), tile)
        tokens = nc * 2 * count
        for m in range(3):
            left = b.act[m, :, span].T
            for c in range(width // cols):
                part = slice(c * cols, (c + 1) * cols)
                if m < 2:
                    right = b.xall[:, :, :, part].reshape(tokens, cols)
                else:
                    right = b.dyb[:, :, part].reshape(tokens, cols)
                bg[m][span, part] = dot(left, right, NN).astype(BF)
            then(m)

    def band_rows(at):
        return pl.ds(tall(at * band, band), band)

    def send_terms(stage, at, to, m):
        src = bg[m].at[band_rows(at), :]
        remote(src, b.rs.at[stage, m], b.gs.at[stage, m], b.gr.at[stage, m], (me.d, to)).start()

    def cross_terms(m):
        arrived(b.rs.at[0, m], b.gr.at[0, m])
        value = bg[m][band_rows(far), :].astype(F32) + b.rs[0, m].astype(F32)
        bg[m][band_rows(far), :] = value.astype(BF)
        send_terms(2, far, far, m)

    grads(1 - near_tile, lambda m: send_terms(0, beyond, near, m))
    grads(near_tile, lambda m: None)
    def add_branch(j):
        arrived(b.dsib.at[j], b.bsr.at[j])
        value = b.dpart[lax.rem(j, 2), me.k].astype(F32) + b.dsib[j].astype(F32)
        value = value.astype(BF)

        @pl.when(j == 0)
        def _():
            b.xown[...] = value

        @pl.when(j > 0)
        def _():
            remote(b.dsum.at[j], b.drecv.at[j - 1], b.dps.at[j], b.dpr.at[j], sib).wait_send()
            b.dsum[j] = value
            cj = lax.rem(me.gc + nc - j, nc)
            to = (me.in_group(cj, me.k), me.s)
            remote(b.dsum.at[j], b.brr.at[j - 1], b.brs.at[j], b.brr_sem.at[j], to).start()

    def branch(i, carry):
        j = nc - 1 - i
        _, rows = chip_rows(j)

        @pl.when(i > 1)
        def _():
            sent(False, b.dpart.at[0, 0], b.bss.at[j + 2], sib)

        for t in range(width // cols):
            span = slice(t * cols, (t + 1) * cols)
            value = dot(b.act[2, rows, :], b.wf_full[2, :, span], NN)
            b.dpart[lax.rem(j, 2), :, :, span] = value.astype(BF).reshape(2, count, cols)

        @pl.when(i > 0)
        def _():
            add_branch(j + 1)

        part = b.dpart.at[lax.rem(j, 2), 1 - me.k]
        remote(part, b.dsib.at[j], b.bss.at[j], b.bsr.at[j], sib).start()
        return carry

    lax.fori_loop(0, nc, branch, 0)

    add_branch(0)
    cross_terms(0)
    for m in range(3):
        send_terms(1, near, near, m)
    for j in range(min(2, nc)):
        sent(False, b.dpart.at[0, 0], b.bss.at[j], sib)
    for j in range(1, nc):
        arrived(b.drecv.at[j - 1], b.dpr.at[j])

    def add_ln(row, value):
        for t in range(tiles):
            b.lnp[t, row : row + 1, :] += value[:, t * LANES : (t + 1) * LANES]

    b.lnp[...] = jnp.zeros_like(b.lnp)

    def second_back(rows):
        grad = b.dsum[0, rows, :].astype(F32)
        for j in range(1, nc):
            grad = grad + b.drecv[j - 1, rows, :].astype(F32)
        normal = b.norm[rows, :]
        add_ln(2, jnp.sum(grad * normal, axis=0, keepdims=True))
        add_ln(3, jnp.sum(grad, axis=0, keepdims=True))
        dmid = b.ig[rows, :] + norm_back(grad, normal, b.scale[rows, 0:1], b.gain[2:3, :])
        b.ig[rows, :] = dmid
        b.dmb[rows, :] = dmid.astype(BF)

    by_rows(second_back)
    dmb = b.dmb[...]
    for i in range(seq):
        here = jnp.logical_and(i == me.s, owner == me.d)
        sent(here, b.mixed.at[i], b.ms.at[i], sib)
    for hg in range(seq):
        b.mixed[hg] = dot(dmb, b.wo_full[hg * block : (hg + 1) * block, :], NT).astype(BF)
        to = (2 * me.c + hg % 2, me.k * me.half + hg // 2)
        here = jnp.logical_and(to[0] == me.d, to[1] == me.s)
        send_or_keep(
            here, b.mixed.at[hg], b.dmix_row.at[me.s], b.dms.at[hg], b.dmr.at[me.s], to
        )
        last.append(functools.partial(sent, here, b.mixed.at[hg], b.dms.at[hg], sib))
    pieces = width // 2 // count

    def og_rows(parity):
        return b.dyb.at[pl.ds(parity * pieces, pieces)]

    for h in range(seq):
        part = dot(b.mixed_in[h], dmb, TN).astype(BF)
        for t in range(block // cr):
            first = h * (block // cr) + t
            row = (first // 2) * cr
            b.dyb[(first % 2) * pieces + row // count, row % count : row % count + cr, :] = part[
                t * cr : (t + 1) * cr
            ]
    remote(og_rows(1 - me.k), b.ogsib, b.o1.at[0], b.o1.at[1], sib).start()
    for j in range(seq):
        arrived(b.dmix_row.at[j], b.dmr.at[j])
    for m in range(1, 3):
        cross_terms(m)
    b.dk[...] = jnp.zeros_like(b.dk)
    b.dv[...] = jnp.zeros_like(b.dv)

    def og_sum():
        remote(b.ogsib, b.ogsib, b.o1.at[0], b.o1.at[1], sib).wait()
        for i in range(pieces):
            value = b.dyb[me.k * pieces + i].astype(F32) + b.ogsib[i].astype(F32)
            b.dyb[2 * pieces + i] = value.astype(BF)

        def send_og(j, carry):
            chip = lax.rem(me.c + j, me.chips)
            row = chip * cr
            src = b.dyb.at[2 * pieces + row // count, pl.ds(tall(lax.rem(row, count), cr), cr), :]
            remote(src, b.ogpl.at[j], b.o2s.at[j], b.o2r.at[j], (2 * chip + me.k, me.s)).start()
            return carry

        lax.fori_loop(1, me.chips, send_og, 0)

    def og_column():
        row = me.c * cr
        at = pl.ds(tall(lax.rem(row, count), cr), cr)
        acc = b.dyb[2 * pieces + row // count, at, :].astype(F32)
        for j in range(1, me.chips):
            remote(b.ogpl.at[j], b.ogpl.at[j], b.o2s.at[j], b.o2r.at[j], sib).wait()
            acc = acc + b.ogpl[j].astype(F32)
        b.ogc[...] = acc.astype(BF)
        for j in range(1, seq):
            to = lax.rem(me.s + j, seq)
            src = b.ogc.at[pl.ds(tall(to * wr, wr), wr), :]
            remote(src, b.ogz.at[j], b.o3s.at[j], b.o3r.at[j], (me.d, to)).start()

    def attend_back(i, carry):
        rows = pl.ds(tall(i * count, count), count)
        q = b.q[rows, :]
        dm = b.dmix_row[i]
        lse = b.lse[rows, :]
        segment = b.lse[rows, LANES - 1 : LANES]
        bias = jnp.where(segment == b.seg_row[0:1, :], 0.0, -1e30)
        grad_q = jnp.zeros((count, block), F32)
        for h in range(heads):
            mask = head_mask((count, block), h)
            qh = jnp.where(mask, q, jnp.zeros_like(q))
            dmh = jnp.where(mask, dm, jnp.zeros_like(dm))
            score = dot(qh, b.kk[...], NT) * 0.125 + bias
            prob = jnp.exp(score - lse[:, h : h + 1])
            dprob = dot(dmh, b.v[...], NT)
            centre = jnp.sum(prob * dprob, axis=1, keepdims=True)
            ds = (0.125 * prob * (dprob - centre)).astype(BF)
            grad_q = jnp.where(mask, dot(ds, b.kk[...], NN), grad_q)
            b.dk[...] += dot(ds, qh, TN)
            b.dv[...] += dot(prob.astype(BF), dmh, TN)
        cosine = jnp.concatenate([b.cos[rows, :]] * (block // LANES), axis=1)
        sine = jnp.concatenate([b.sin[rows, :]] * (block // LANES), axis=1)
        b.act[0, rows, 0:block] = (grad_q * cosine - swap_halves(grad_q) * sine).astype(BF)

        @pl.when(i == 0)
        def _():
            og_sum()

        return carry

    lax.fori_loop(0, seq, attend_back, 0)

    def back_chunk(i):
        rows = pl.ds(tall(i * count, count), count)
        cosine = jnp.concatenate([b.cos[rows, :]] * (block // LANES), axis=1)
        sine = jnp.concatenate([b.sin[rows, :]] * (block // LANES), axis=1)
        grad_k = b.dk[rows, :]
        dk = (grad_k * cosine - swap_halves(grad_k) * sine).astype(BF)
        dv = b.dv[rows, :].astype(BF)
        b.act[1, rows, 0:block] = dk
        b.act[2, rows, 0:block] = dv
        value = dot(b.act[0, rows, 0:block], b.wq_full[0], NT)
        value = value + dot(dk, b.wq_full[1], NT) + dot(dv, b.wq_full[2], NT)
        at = lax.rem(i, 2) * me.half + i // 2
        b.xall[at // 2, lax.rem(at, 2)] = value.astype(BF)

    def other_half(j, carry):
        back_chunk(2 * j + 1 - me.k)
        return carry

    def own_half_chunks(j, carry):
        back_chunk(2 * j + me.k)
        return carry

    lax.fori_loop(0, me.half, other_half, 0)
    quarter = me.half // 2
    dn_other = b.xall.at[pl.ds((1 - me.k) * quarter, quarter)]
    remote(dn_other, b.dnsib, b.n1.at[0], b.n1.at[1], sib).start()
    lax.fori_loop(0, me.half, own_half_chunks, 0)
    remote(b.dnsib, b.dnsib, b.n1.at[0], b.n1.at[1], sib).wait()
    for j in range(me.half):
        value = b.xall[me.k * quarter + j // 2, j % 2].astype(F32)
        b.dpart[0, j] = (value + b.dnsib[j // 2, j % 2].astype(F32)).astype(BF)
        i = 2 * j + me.k
        here = jnp.logical_and(owner == me.d, i == me.s)
        send_or_keep(
            here, b.dpart.at[0, j], b.dnr.at[me.h], b.n2s.at[j], b.n2r.at[me.h], (owner, i)
        )
        last.append(functools.partial(sent, here, b.dpart.at[0, j], b.n2s.at[j], sib))
    span_rows = 2 * cr
    per_tile = block // span_rows

    def qkv_terms(j, carry):
        at = lax.rem(me.c // per_tile + j, width // block)
        x = b.xrow[:, pl.ds(tall(at * block, block), block)]
        rows = pl.ds(tall(total + at * block, block), block)
        for t in range(3):
            b.act[t, rows, 0:block] = dot(x, b.act[t, 0:total, 0:block], TN).astype(BF)
        for i in range(per_tile):
            chip = at * per_tile + i

            @pl.when(chip != me.c)
            def _(chip=chip):
                src = b.act.at[:, pl.ds(tall(total + chip * span_rows, span_rows), span_rows), 0:block]
                to = (2 * chip + me.k, me.s)
                remote(src, b.qgpl.at[me.c], b.q1s.at[chip], b.q1r.at[me.c], to).start()

        return carry

    lax.fori_loop(1, width // block, qkv_terms, 0)
    qkv_terms(0, 0)
    og_column()
    tok = local(b.tok, b.norm, b.load.at[0])
    tok.start()
    tok.wait()
    for h in range(me.half):
        arrived(b.dnr.at[h], b.n2r.at[h])

    def first_back(rows):
        grad = b.dnr[0, rows, :].astype(F32)
        for h in range(1, me.half):
            grad = grad + b.dnr[h, rows, :].astype(F32)
        normal, scale = normalise(b.norm[rows, :])
        b.ig[rows, :] += norm_back(grad, normal, scale, b.gain[0:1, :])
        add_ln(0, jnp.sum(grad * normal, axis=0, keepdims=True))
        add_ln(1, jnp.sum(grad, axis=0, keepdims=True))

    by_rows(first_back)
    store(1)

    def send_lnp(j, carry):
        other = lax.rem(me.n + j, me.total)
        remote(
            b.lnp.at[other // per], b.lnr.at[me.n], b.lnt.at[0], b.lnt.at[1], me.of_rank(other)
        ).start()
        return carry

    lax.fori_loop(1, me.total, send_lnp, 0)
    b.lnr[me.n] = b.lnp[me.n // per]
    own = pl.ds(tall(total + me.c * span_rows, span_rows), span_rows)
    sums = [b.act[t, own, 0:block].astype(F32) for t in range(3)]
    for j in range(1, me.chips):
        chip = lax.rem(me.c + j, me.chips)
        part = b.qgpl.at[chip]
        remote(part, part, b.q1s.at[chip], b.q1r.at[chip], sib).wait()
        for t in range(3):
            sums[t] = sums[t] + b.qgpl[chip, t].astype(F32)
    for t in range(3):
        b.qgc[t] = sums[t].astype(BF)
    source = me.k * seq + me.s
    for core in range(2):
        for j in range(seq):
            to = lax.rem(me.s + j, seq)
            src = b.qgc.at[:, pl.ds(tall((core * seq + to) * wr, wr), wr), :]
            here = jnp.logical_and(core == me.k, to == me.s)
            send_or_keep(
                here, src, b.qgz.at[source], b.q2s.at[core, j], b.q2r.at[source], (2 * me.c + core, to)
            )
            last.append(functools.partial(sent, here, src, b.q2s.at[core, j], sib))
    value = b.out[...] + b.xown[...].astype(F32)
    for j in range(1, nc):
        remote(b.brr.at[j - 1], b.brr.at[j - 1], b.brs.at[j], b.brr_sem.at[j], sib).wait()
        value = value + b.brr[j - 1].astype(F32)
    b.out[...] = value
    store(0)
    acc = b.ogc[pl.ds(tall(me.s * wr, wr), wr), :].astype(F32)
    for j in range(1, seq):
        remote(b.ogz.at[j], b.ogz.at[j], b.o3s.at[j], b.o3r.at[j], sib).wait()
        acc = acc + b.ogz[j].astype(F32)
    b.og[...] = acc
    store(4)
    for m in range(3):
        for j in range(1, 3):
            arrived(b.rs.at[j, m], b.gr.at[j, m])
        for j in range(3):
            last.append(functools.partial(sent, False, b.rs.at[0, 0], b.gs.at[j, m], sib))
        acc = bg[m][band_rows(me.s), :].astype(F32)
        acc = acc + b.rs[1, m].astype(F32) + b.rs[2, m].astype(F32)
        if me.groups == 1:
            b.fg[m] = acc
        else:
            bg[m][band_rows(me.s), :] = acc.astype(BF)
    if me.groups > 1:
        for m in range(3):
            for j in range(1, me.groups):
                other = lax.rem(me.g + j, me.groups)
                src = bg[m].at[pl.ds(tall(me.s * band + other * units, units), units), :]
                to = (other * me.group + me.p, me.s)
                remote(src, b.grp.at[j, m], b.grs.at[j, m], b.grr.at[j, m], to).start()
        for m in range(3):
            acc = bg[m][pl.ds(tall(me.s * band + me.g * units, units), units), :].astype(F32)
            for j in range(1, me.groups):
                part = b.grp.at[j, m]
                remote(part, part, b.grs.at[j, m], b.grr.at[j, m], sib).wait()
                acc = acc + b.grp[j, m].astype(F32)
            b.fg[m] = acc
    store(5)
    rest = b.lnr.at[pl.ds(0, me.total - 1)]
    remote(rest, rest, b.lnt.at[0], b.lnt.at[1], sib).wait()
    acc = b.lnr[0]
    for j in range(1, me.total):
        acc = acc + b.lnr[j]
    for i in range(fit):

        @pl.when(lax.rem(me.n, fit) == i)
        def _(i=i):
            b.lng[...] = acc[0:4, i * share : (i + 1) * share]

    store(2)
    for j in range(2 * seq):
        arrived(b.qgz.at[j], b.q2r.at[j])
    for hg in range(seq):
        core, h = hg % 2, hg // 2
        acc = b.qgz[core * seq + h].astype(F32) + b.qgz[core * seq + me.half + h].astype(F32)
        b.qg[:, :, hg * block : (hg + 1) * block] = acc
    store(3)
    for copy in last:
        copy()
    for copy in stores:
        copy.wait()


def keep_kernel(count, *refs):
    given, kept, held = refs[:count], refs[count : 2 * count], refs[2 * count : 3 * count]
    sems = refs[-1]
    ins = [local(given[i], held[i], sems.at[0, i]) for i in range(count)]
    outs = [local(held[i], kept[i], sems.at[1, i]) for i in range(count)]
    for copy in ins:
        copy.start()
    for i in range(count):
        ins[i].wait()
        outs[i].start()
    for copy in outs:
        copy.wait()


def body(dp, seq, tokens, ln_params, qkv_weight, out_weight, ffn_weight, lengths, cotangent):
    count, width = tokens.shape[1], tokens.shape[2]
    ranks = dp * seq
    total = count * seq
    wr = qkv_weight.shape[0]
    cr = wr * seq
    units = ffn_weight.shape[0]
    block = width // seq
    half = seq // 2
    group = min(dp, GROUP)
    groups = dp // group
    gchips, chips, slots = group // 2, dp // 2, groups * seq
    held = units * slots
    share = ln_params.shape[1]
    sem = pltpu.SemaphoreType.DMA
    vm = pltpu.VMEM
    anywhere = pl.BlockSpec(memory_space=pl.ANY)
    vmem = pl.BlockSpec(memory_space=pltpu.VMEM)
    operands = dict(
        tok=(tokens.reshape(count, width), anywhere),
        ln=(ln_params, vmem),
        wq=(qkv_weight.transpose(1, 0, 2), anywhere),
        wo=(out_weight, anywhere),
        wf=(ffn_weight.transpose(1, 0, 2), anywhere),
        lens=(lengths, vmem),
        cot=(cotangent.reshape(count, width), anywhere),
    )
    outs = dict(
        out=(count, width),
        ig=(count, width),
        lng=(4, share),
        qg=(3, wr, width),
        og=(wr, width),
        fg=(3, units, width),
    )
    scratch = dict(
        **{name: vm(dims, F32) for name, dims in outs.items()},
        norm=vm((count, width), F32),
        scale=vm((count, LANES), F32),
        lens_own=vm((8, LANES), jnp.int32),
        lens_pair=vm((2, 8, LANES), jnp.int32),
        ln_own=vm((8, LANES), F32),
        ln_all=vm((ranks, 8, LANES), F32),
        gain=vm((8, width), F32),
        wq_own=vm((3, wr, width), BF),
        wcol=vm((3, cr, 2 * block), BF),
        xown=vm((count, width), BF),
        dmb=vm((count, width), BF),
        xrow=vm((total, width), BF),
        wq_full=vm((3, width, block), BF),
        wo_full=vm((width, width), BF),
        dyb=vm((group, count, width), BF),
        q=vm((total, block), BF),
        kk=vm((total, block), BF),
        v=vm((total, block), BF),
        lse=vm((total, LANES), F32),
        cos=vm((total, LANES), F32),
        sin=vm((total, LANES), F32),
        seg_row=vm((8, total), F32),
        mixed=vm((seq, count, block), BF),
        mixed_in=vm((seq, count, block), BF),
        dmix_row=vm((seq, count, block), BF),
        wf_full=vm((3, held, width), BF),
        xall=vm((gchips, 2, count, width), BF),
        act=vm((3, group * count, held), BF),
        dpart=vm((2, 2, count, width), BF),
        dsib=vm((gchips, count, width), BF),
        dsum=vm((gchips, count, width), BF),
        drecv=vm((gchips - 1, count, width), BF),
        brr=vm((gchips - 1, count, width), BF),
        ogsib=vm((width // 2 // count, count, width), BF),
        ogpl=vm((chips, cr, width), BF),
        ogc=vm((cr, width), BF),
        ogz=vm((seq, wr, width), BF),
        dk=vm((total, block), F32),
        dv=vm((total, block), F32),
        dnsib=vm((half // 2, 2, count, width), BF),
        dnr=vm((half, count, width), BF),
        qgpl=vm((chips, 3, 2 * cr, block), BF),
        qgc=vm((3, 2 * cr, block), BF),
        qgz=vm((2 * seq, 3, wr, block), BF),
        rs=vm((3, 3, groups * units, width), BF),
        grp=vm((groups, 3, units, width) if groups > 1 else (8, LANES), BF),
        down=vm((held, width), BF),
        lnp=vm((width // LANES, 8, LANES), F32),
        lnr=vm((ranks, 8, LANES), F32),
        load=sem((7,)),
        keep=sem((6,)),
        lns=sem((2,)),
        lens_sem=sem((2,)),
        wq1s=sem((seq,)),
        wq1r=sem((seq,)),
        wq2s=sem((dp,)),
        wq2r=sem((dp,)),
        wo1s=sem((seq,)),
        wo1r=sem((seq,)),
        wo2s=sem((chips,)),
        wo2r=sem((chips,)),
        wo3s=sem((chips,)),
        wo3r=sem((chips,)),
        xs=sem((half, 2)),
        xr=sem((seq,)),
        xfs=sem((seq,)),
        xfr=sem((seq,)),
        dys=sem((gchips,)),
        dyr=sem((gchips,)),
        dyfs=sem((gchips,)),
        dyfr=sem((gchips,)),
        fgs=sem((groups,)),
        fgr_sem=sem((groups,)),
        hs=sem((3, 3)),
        hr=sem((3, 3)),
        ms=sem((seq,)),
        mr=sem((seq,)),
        xs2=sem((gchips,)),
        xr2=sem((gchips,)),
        xfs2=sem((gchips,)),
        xfr2=sem((gchips,)),
        dss=sem((gchips,)),
        dsr=sem((gchips,)),
        dps=sem((gchips,)),
        dpr=sem((gchips,)),
        bss=sem((gchips,)),
        bsr=sem((gchips,)),
        brs=sem((gchips,)),
        brr_sem=sem((gchips,)),
        dms=sem((seq,)),
        dmr=sem((seq,)),
        gs=sem((3, 3)),
        gr=sem((3, 3)),
        grs=sem((groups, 3)),
        grr=sem((groups, 3)),
        o1=sem((2,)),
        o2s=sem((chips,)),
        o2r=sem((chips,)),
        o3s=sem((seq,)),
        o3r=sem((seq,)),
        n1=sem((2,)),
        n2s=sem((half,)),
        n2r=sem((half,)),
        q1s=sem((chips,)),
        q1r=sem((chips,)),
        q2s=sem((2, seq)),
        q2r=sem((2 * seq,)),
        lnt=sem((2,)),
    )
    names = (*operands, *[name + "_out" for name in outs], *scratch)
    results = pl.pallas_call(
        functools.partial(layer_kernel, names, dp, seq, lengths.shape[1]),
        out_shape=tuple(jax.ShapeDtypeStruct(dims, F32) for dims in outs.values()),
        in_specs=[spec for _, spec in operands.values()],
        out_specs=tuple([anywhere] * len(outs)),
        scratch_shapes=list(scratch.values()),
        compiler_params=pltpu.CompilerParams(
            collective_id=1, has_side_effects=True, vmem_limit_bytes=VMEM_BYTES
        ),
        cost_estimate=pl.CostEstimate(
            flops=32 * 10**9, bytes_accessed=2**24, transcendentals=10**7
        ),
        name="layer",
    )(*[value for value, _ in operands.values()])
    out, input_grad, ln_grad, qg, og, fg = pl.pallas_call(
        functools.partial(keep_kernel, len(outs)),
        out_shape=tuple(jax.ShapeDtypeStruct(dims, F32) for dims in outs.values()),
        in_specs=[anywhere] * len(outs),
        out_specs=tuple([anywhere] * len(outs)),
        scratch_shapes=[*[vm(dims, F32) for dims in outs.values()], sem((2, len(outs)))],
        name="keep",
    )(*results)
    return (
        out.reshape(1, count, width),
        input_grad.reshape(1, count, width),
        ln_grad,
        qg.transpose(1, 0, 2),
        og,
        fg.transpose(1, 0, 2),
    )


def solution(mesh):
    dp, seq = mesh.shape["dp"], mesh.shape["seq"]
    both = ("dp", "seq")
    in_specs = (
        P("dp", "seq", None),
        P(None, both),
        P(both, None, None),
        P(both, None),
        P(both, None, None),
        P("dp", None),
        P("dp", "seq", None),
    )
    out_specs = (
        P("dp", "seq", None),
        P("dp", "seq", None),
        P(None, both),
        P(both, None, None),
        P(both, None),
        P(both, None, None),
    )
    return jax.shard_map(
        functools.partial(body, dp, seq),
        mesh=mesh,
        in_specs=in_specs,
        out_specs=out_specs,
        check_vma=False,
    )
```

```python
import functools
import math
import types

import jax
import jax.numpy as jnp
from jax import lax
from jax.experimental import pallas as pl
from jax.experimental.pallas import tpu as pltpu
from jax.sharding import PartitionSpec as P

HEAD_DIM = 64
GROUP = 8
LANES = 128
BF = jnp.bfloat16
F32 = jnp.float32
MESH = pl.DeviceIdType.MESH
NT = (((1,), (1,)), ((), ()))
NN = (((1,), (0,)), ((), ()))
TN = (((0,), (0,)), ((), ()))
EPS = 1e-05
VMEM_BYTES = 62 * 2**20


def dot(a, b, dims):
    return lax.dot_general(a, b, dims, preferred_element_type=F32)


def remote(src, dst, send, recv, device):
    return pltpu.make_async_remote_copy(
        src_ref=src, dst_ref=dst, send_sem=send, recv_sem=recv, device_id=device, device_id_type=MESH
    )


def local(src, dst, sem):
    return pltpu.make_async_copy(src, dst, sem)


class Place:
    def __init__(self, dp, seq):
        self.dp, self.seq = dp, seq
        self.d, self.s = lax.axis_index("dp"), lax.axis_index("seq")
        self.c, self.k = self.d // 2, lax.rem(self.d, 2)
        self.sib = self.d + 1 - 2 * self.k
        self.chips = dp // 2
        self.group = min(dp, GROUP)
        self.groups = dp // self.group
        self.g, self.p = self.d // self.group, lax.rem(self.d, self.group)
        self.gc = self.p // 2
        self.gchips = self.group // 2
        self.half = seq // 2
        self.r, self.h = self.s // self.half, lax.rem(self.s, self.half)
        self.hg = 2 * self.h + self.k
        self.n = self.d * seq + self.s
        self.total = dp * seq

    def of_rank(self, rank):
        return (rank // self.seq, lax.rem(rank, self.seq))

    def in_group(self, chip, core):
        return self.g * self.group + 2 * chip + core


def normalise(value):
    mean = jnp.mean(value, axis=-1, keepdims=True)
    centred = value - mean
    var = jnp.mean(centred * centred, axis=-1, keepdims=True)
    scale = lax.rsqrt(var + EPS)
    return centred * scale, scale


def norm_back(grad, normal, scale, gain):
    scaled = grad * gain
    return scale * (
        scaled
        - jnp.mean(scaled, axis=-1, keepdims=True)
        - normal * jnp.mean(scaled * normal, axis=-1, keepdims=True)
    )


def swap_halves(value):
    half = HEAD_DIM // 2
    width = value.shape[1]
    lane = lax.broadcasted_iota(jnp.int32, value.shape, 1)
    up = pltpu.roll(value, width - half, 1)
    down = pltpu.roll(value, half, 1)
    return jnp.where(lax.rem(lane, HEAD_DIM) < half, up, down)


def head_mask(shape, h):
    lane = lax.broadcasted_iota(jnp.int32, shape, 1)
    return jnp.logical_and(lane >= h * HEAD_DIM, lane < (h + 1) * HEAD_DIM)


def tall(value, rows):
    return pl.multiple_of(value, rows)


def meet(me):
    barrier = pltpu.get_barrier_semaphore()

    def hello(j, carry):
        other = lax.rem(me.n + j, me.total)
        pl.semaphore_signal(barrier, inc=1, device_id=me.of_rank(other), device_id_type=MESH)
        return carry

    lax.fori_loop(1, me.total, hello, 0)


def met(me):
    pl.semaphore_wait(pltpu.get_barrier_semaphore(), me.total - 1)


def send_or_keep(here, src, dst, send, recv, device):
    @pl.when(jnp.logical_not(here))
    def _():
        remote(src, dst, send, recv, device).start()

    @pl.when(here)
    def _():
        local(src, dst, recv).start()


def sent(here, src, send, device):
    @pl.when(jnp.logical_not(here))
    def _():
        remote(src, src, send, send, device).wait_send()


def arrived(dst, recv):
    local(dst, dst, recv).wait()


def layer_kernel(names, dp, seq, segs, *refs):
    b = types.SimpleNamespace(**dict(zip(names, refs)))
    me = Place(dp, seq)
    count, width = b.out.shape
    total = count * seq
    wr = b.og.shape[0]
    cr = wr * seq
    block = b.q.shape[1]
    heads = block // HEAD_DIM
    units = b.fg.shape[1]
    held = b.wf_full.shape[1]
    band = me.groups * units
    nc = me.gchips
    sib = (me.sib, me.s)
    share = b.ln.shape[1]
    fit = LANES // share
    tiles = width // LANES
    per = me.total // tiles
    halfrows = count // 2
    last = []

    def by_rows(step):
        def one(i, carry):
            step(pl.ds(tall(i * some, some), some))
            return carry

        lax.fori_loop(0, count // some, one, 0)

    some = 64
    results = ("out", "ig", "lng", "qg", "og", "fg")
    stores = []

    def store(i):
        name = results[i]
        stores.append(local(getattr(b, name), getattr(b, name + "_out"), b.keep.at[i]))
        stores[-1].start()

    meet(me)
    loads = [
        local(b.tok, b.out, b.load.at[0]),
        local(b.wq, b.qg, b.load.at[1]),
        local(b.wo, b.og, b.load.at[2]),
        local(b.wf, b.fg, b.load.at[3]),
        local(b.cot, b.ig, b.load.at[4]),
    ]
    for copy in loads:
        copy.start()
    b.lens_own[...] = jnp.zeros_like(b.lens_own)
    b.lens_own[0:1, 0:segs] = b.lens[...]
    b.lens_pair[me.k] = b.lens_own[...]
    gains = jnp.concatenate([b.ln[...].astype(BF).astype(F32)] * fit, axis=1)
    lane = lax.broadcasted_iota(jnp.int32, gains.shape, 1)
    b.ln_own[...] = jnp.zeros_like(b.ln_own)
    b.ln_own[0:4, :] = jnp.where(lane // share == lax.rem(me.n, fit), gains, 0.0)
    b.ln_all[me.n] = b.ln_own[...]
    loads[1].wait()
    b.wq_own[...] = b.qg[...].astype(BF)
    loads[0].wait()

    def first_norm(rows):
        b.norm[rows, :] = normalise(b.out[rows, :])[0]

    by_rows(first_norm)
    met(me)

    def send_ln(j, carry):
        other = lax.rem(me.n + j, me.total)
        remote(
            b.ln_own, b.ln_all.at[me.n], b.lns.at[0], b.lns.at[1], me.of_rank(other)
        ).start()
        return carry

    lax.fori_loop(1, me.total, send_ln, 0)
    len_copy = remote(b.lens_own, b.lens_pair.at[me.k], b.lens_sem.at[0], b.lens_sem.at[1], sib)
    len_copy.start()
    pair = 2 * block
    row0 = tall(me.s * wr, wr)
    out0 = tall(me.n * wr, wr)
    wq_first = []
    for j in range(1, seq):
        to = lax.rem(me.s + j, seq)
        col = tall(lax.rem(to, me.half) * pair, pair)
        wq_first.append(
            remote(
                b.wq_own.at[:, :, pl.ds(col, pair)],
                b.wcol.at[:, pl.ds(row0, wr), :],
                b.wq1s.at[j],
                b.wq1r.at[j],
                (me.d, to),
            )
        )
    for copy in wq_first:
        copy.start()
    own_wq = local(
        b.wq_own.at[:, :, pl.ds(tall(me.h * pair, pair), pair)],
        b.wcol.at[:, pl.ds(row0, wr), :],
        b.load.at[5],
    )
    own_wq.start()
    loads[2].wait()
    b.wo_full[pl.ds(out0, wr), :] = b.og[...].astype(BF)
    rest = b.ln_all.at[pl.ds(0, me.total - 1)]
    remote(rest, rest, b.lns.at[0], b.lns.at[1], sib).wait()
    for t in range(tiles):
        part = b.ln_all[t * per]
        for i in range(1, per):
            part = part + b.ln_all[t * per + i]
        b.gain[:, t * LANES : (t + 1) * LANES] = part

    def first_out(rows):
        b.xown[rows, :] = (b.norm[rows, :] * b.gain[0:1, :] + b.gain[1:2, :]).astype(BF)

    by_rows(first_out)
    rows0 = tall(me.s * count, count)
    for j in range(me.half):
        to = me.k * me.half + lax.rem(me.h + j, me.half)
        for core in range(2):
            src = b.xown.at[pl.ds(core * halfrows, halfrows), :]
            dst = b.xrow.at[pl.ds(rows0 + core * halfrows, halfrows), :]
            here = jnp.logical_and(to == me.s, core == me.k)
            send_or_keep(
                here, src, dst, b.xs.at[j, core], b.xr.at[me.s], (2 * me.c + core, to)
            )
            last.append(
                functools.partial(sent, here, src, b.xs.at[j, core], (2 * me.c + core, to))
            )
    for copy in wq_first:
        copy.wait()
    own_wq.wait()
    crow0 = tall(me.d * cr, cr)

    def send_wq(j, carry):
        to = lax.rem(me.d + j, dp)
        remote(
            b.wcol.at[:, :, pl.ds(tall(lax.rem(to, 2) * block, block), block)],
            b.wq_full.at[:, pl.ds(crow0, cr), :],
            b.wq2s.at[j],
            b.wq2r.at[j],
            (to, me.s),
        ).start()
        return carry

    lax.fori_loop(1, dp, send_wq, 0)
    own_half = local(
        b.wcol.at[:, :, pl.ds(tall(me.k * block, block), block)],
        b.wq_full.at[:, pl.ds(crow0, cr), :],
        b.load.at[6],
    )
    own_half.start()
    len_copy.wait()
    row = b.lens_pair[me.r]
    place_row = lax.broadcasted_iota(jnp.int32, (8, total), 1)
    ends = [row[0:1, 0:1]]
    for j in range(1, segs):
        ends.append(ends[-1] + row[0:1, j : j + 1])
    segr = jnp.zeros((8, total), jnp.int32)
    for end in ends:
        segr = segr + (place_row >= end).astype(jnp.int32)
    b.seg_row[...] = segr.astype(F32)
    half = HEAD_DIM // 2
    lane = lax.broadcasted_iota(jnp.int32, (1, LANES), 1)
    rate = jnp.exp(lax.rem(lane, half).astype(F32) * (-math.log(10000.0) / half))
    sign = jnp.where(lax.rem(lane, HEAD_DIM) < half, -1.0, 1.0)

    def angles(i, carry):
        rows = pl.ds(tall(i * LANES, LANES), LANES)
        place = lax.broadcasted_iota(jnp.int32, (LANES, LANES), 0) + i * LANES
        segment = jnp.zeros((LANES, LANES), jnp.int32)
        begin = jnp.zeros((LANES, LANES), jnp.int32)
        for end in ends:
            past = place >= end
            segment = segment + past.astype(jnp.int32)
            begin = jnp.where(past, end, begin)
        b.lse[rows, :] = segment.astype(F32)
        angle = (place - begin).astype(F32) * rate
        b.cos[rows, :] = jnp.cos(angle)
        b.sin[rows, :] = jnp.sin(angle) * sign
        return carry

    lax.fori_loop(0, total // LANES, angles, 0)
    loads[4].wait()
    b.dyb[me.p] = b.ig[...].astype(BF)
    loads[3].wait()
    own_units = pl.ds(tall(me.s * band + me.g * units, units), units)
    b.wf_full[:, own_units, :] = b.fg[...].astype(BF)
    for j in range(seq):
        source = lax.rem(me.s + j, seq)
        part = b.xrow.at[pl.ds(tall(source * count + me.k * halfrows, halfrows), halfrows), :]
        arrived(part, b.xr.at[source])
        remote(part, part, b.xfs.at[j], b.xfr.at[j], sib).start()
    wo_own = b.wo_full.at[pl.ds(out0, wr), :]
    wo_first = []
    for j in range(1, seq):
        to = (me.d, lax.rem(me.s + j, seq))
        wo_first.append(remote(wo_own, wo_own, b.wo1s.at[j], b.wo1r.at[j], to))
    for copy in wo_first:
        copy.start()
    for j in range(1, me.groups):
        other = lax.rem(me.g + j, me.groups)
        mine = b.wf_full.at[:, own_units, :]
        remote(
            mine, mine, b.fgs.at[j], b.fgr_sem.at[j], (other * me.group + me.p, me.s)
        ).start()
    for j in range(1, me.groups):
        mine = b.wf_full.at[:, own_units, :]
        remote(mine, mine, b.fgs.at[j], b.fgr_sem.at[j], sib).wait()

    near, far = me.s + 1 - 2 * lax.rem(me.s, 2), lax.rem(me.s + 2, seq)
    beyond = lax.rem(near + 2, seq)

    def column(m, at):
        return b.wf_full.at[m, pl.ds(tall(at * band, band), band), :]

    def unit_copy(way, m):
        part = column(m, far if way == 2 else me.s)
        to = (me.d, near if way else far)
        return remote(part, part, b.hs.at[way, m], b.hr.at[way, m], to)

    def send_units(m):
        unit_copy(0, m).start()
        unit_copy(1, m).start()

    def pass_units(m):
        arrived(column(m, far), b.hr.at[0, m])
        unit_copy(2, m).start()

    for j in range(seq):
        part = b.xrow.at[pl.ds(0, halfrows), :]
        arrived(part, b.xfr.at[j])
        last.append(functools.partial(sent, False, part, b.xfs.at[j], sib))

    def wait_wq(j, carry):
        part = b.wq_full.at[:, pl.ds(0, cr), :]
        remote(part, part, b.wq2s.at[j], b.wq2r.at[j], sib).wait()
        return carry

    lax.fori_loop(1, dp, wait_wq, 0)
    own_half.wait()
    def project(i, carry):
        rows = pl.ds(tall(i * count, count), count)
        x = b.xrow[rows, :]
        cosine = jnp.concatenate([b.cos[rows, :]] * (block // LANES), axis=1)
        sine = jnp.concatenate([b.sin[rows, :]] * (block // LANES), axis=1)
        raw = dot(x, b.wq_full[0], NN)
        b.q[rows, :] = (raw * cosine + swap_halves(raw) * sine).astype(BF)
        raw = dot(x, b.wq_full[1], NN)
        b.kk[rows, :] = (raw * cosine + swap_halves(raw) * sine).astype(BF)
        b.v[rows, :] = dot(x, b.wq_full[2], NN).astype(BF)
        return carry

    lax.fori_loop(0, seq, project, 0)
    owner = 2 * me.c + me.r
    mine = b.wo_full.at[pl.ds(crow0, cr), :]
    for copy in wo_first:
        copy.wait()
    remote(mine, mine, b.wo3s.at[0], b.wo3r.at[0], sib).start()
    for j in range(1, me.chips):
        to = 2 * lax.rem(me.c + j, me.chips) + me.k
        remote(mine, mine, b.wo2s.at[j], b.wo2r.at[j], (to, me.s)).start()
    dy_own = b.dyb.at[me.p]
    remote(dy_own, dy_own, b.dyfs.at[0], b.dyfr.at[0], sib).start()
    for j in range(1, nc):
        to = me.in_group(lax.rem(me.gc + j, nc), me.k)
        remote(dy_own, dy_own, b.dys.at[j], b.dyr.at[j], (to, me.s)).start()

    def attend(step, carry):
        i = lax.rem(me.s + step, seq)
        rows = pl.ds(tall(i * count, count), count)
        q = b.q[rows, :]
        segment = b.lse[rows, LANES - 1 : LANES]
        bias = jnp.where(segment == b.seg_row[0:1, :], 0.0, -1e30)
        lane = lax.broadcasted_iota(jnp.int32, (count, LANES), 1)
        lse = b.lse[rows, :]
        out = jnp.zeros((count, block), F32)
        for h in range(heads):
            mask = head_mask((count, block), h)
            score = dot(jnp.where(mask, q, jnp.zeros_like(q)), b.kk[...], NT) * 0.125 + bias
            top = jnp.max(score, axis=1, keepdims=True)
            weight = jnp.exp(score - top)
            tally = jnp.sum(weight, axis=1, keepdims=True)
            prob = (weight * (1.0 / tally)).astype(BF)
            out = jnp.where(mask, dot(prob, b.v[...], NN), out)
            lse = jnp.where(lane == h, top + jnp.log(tally), lse)
        b.lse[rows, :] = lse
        b.mixed[i] = out.astype(BF)
        here = jnp.logical_and(i == me.s, owner == me.d)
        send_or_keep(
            here, b.mixed.at[i], b.mixed_in.at[me.hg], b.ms.at[i], b.mr.at[me.hg], (owner, i)
        )

        return carry

    lax.fori_loop(0, seq, attend, 0)
    for m in range(3):
        send_units(m)
    for j in range(1, me.chips):
        source = 2 * lax.rem(me.c + me.chips - j, me.chips) + me.k
        part = b.wo_full.at[pl.ds(tall(source * cr, cr), cr), :]
        arrived(part, b.wo2r.at[j])
        remote(part, part, b.wo3s.at[j], b.wo3r.at[j], sib).start()
        last.append(functools.partial(sent, False, part, b.wo2s.at[j], sib))
        last.append(functools.partial(sent, False, part, b.wo3s.at[j], sib))
    last.append(functools.partial(sent, False, mine, b.wo3s.at[0], sib))
    for j in range(me.chips):
        arrived(mine, b.wo3r.at[j])
    for j in range(seq):
        arrived(b.mixed_in.at[j], b.mr.at[j])
    for t in range(width // block):
        span = slice(t * block, (t + 1) * block)
        part = b.out[:, span]
        for h in range(seq):
            part = part + dot(b.mixed_in[h], b.wo_full[h * block : (h + 1) * block, span], NN)
        b.out[:, span] = part

    def second_norm(rows):
        normal, scale = normalise(b.out[rows, :])
        b.norm[rows, :] = normal
        b.scale[rows, :] = jnp.broadcast_to(scale, (some, LANES))
        b.xall[me.gc, me.k, rows, :] = (normal * b.gain[2:3, :] + b.gain[3:4, :]).astype(BF)

    by_rows(second_norm)
    x_own = b.xall.at[me.gc, me.k]
    remote(x_own, x_own, b.xfs2.at[0], b.xfr2.at[0], sib).start()
    for j in range(1, nc):
        to = me.in_group(lax.rem(me.gc + j, nc), me.k)
        remote(x_own, x_own, b.xs2.at[j], b.xr2.at[j], (to, me.s)).start()
    pass_units(0)
    for j in range(1, nc):
        source = 2 * lax.rem(me.gc + nc - j, nc) + me.k
        part = b.dyb.at[source]
        arrived(part, b.dyr.at[j])
        remote(part, part, b.dyfs.at[j], b.dyfr.at[j], sib).start()
        last.append(functools.partial(sent, False, part, b.dys.at[j], sib))
        last.append(functools.partial(sent, False, part, b.dyfs.at[j], sib))
    last.append(functools.partial(sent, False, dy_own, b.dyfs.at[0], sib))
    for j in range(nc):
        arrived(dy_own, b.dyfr.at[j])
    tile = 2 * band
    cols = 256
    near_tile = me.s // 2

    def chip_rows(j):
        cj = lax.rem(me.gc + nc - j, nc)
        return cj, pl.ds(tall(cj * 2 * count, 2 * count), 2 * count)

    def hidden(j, t):
        cj, rows = chip_rows(j)
        span = pl.ds(tall(t * tile, tile), tile)
        x = b.xall[cj].reshape(2 * count, width)
        dy = b.dyb[pl.ds(2 * cj, 2)].reshape(2 * count, width)
        gate = dot(x, b.wf_full[0, span, :], NT)
        up = dot(x, b.wf_full[1, span, :], NT)
        dh = dot(dy, b.wf_full[2, span, :], NT)
        sigma = 1.0 / (1.0 + jnp.exp(-gate))
        active = gate * sigma
        b.act[2, rows, span] = (active * up).astype(BF)
        b.act[0, rows, span] = (dh * up * (sigma * (1.0 + gate * (1.0 - sigma)))).astype(BF)
        b.act[1, rows, span] = (dh * active).astype(BF)

    def near_units(j, carry):
        cj, _ = chip_rows(j)

        @pl.when(j > 0)
        def _():
            part = b.xall.at[cj, me.k]
            arrived(part, b.xr2.at[j])
            remote(part, part, b.xfs2.at[j], b.xfr2.at[j], sib).start()

        @pl.when((j > 0) & (j < 3))
        def _():
            pass_units(j)

        arrived(b.xall.at[cj, 1 - me.k], b.xfr2.at[j])
        hidden(j, near_tile)
        return carry

    def far_units(j, carry):
        hidden(j, 1 - near_tile)
        return carry

    for m in range(3):
        arrived(column(m, near), b.hr.at[1, m])
    lax.fori_loop(0, nc, near_units, 0)
    for m in range(3):
        arrived(column(m, beyond), b.hr.at[2, m])
    lax.fori_loop(0, nc, far_units, 0)

    def take_dn2(j):
        part = b.dsib.at[j]
        remote(part, part, b.dss.at[j], b.dsr.at[j], sib).wait()
        value = b.dpart[lax.rem(j, 2), me.k].astype(F32) + b.dsib[j].astype(F32)
        b.dsum[j] = value.astype(BF)

        @pl.when(j > 0)
        def _():
            to = (me.in_group(chip_rows(j)[0], me.k), me.s)
            remote(b.dsum.at[j], b.drecv.at[j - 1], b.dps.at[j], b.dpr.at[j], to).start()

    def grad_tokens(i, carry):
        j = nc - 1 - i
        _, rows = chip_rows(j)
        for t in range(width // cols):
            span = slice(t * cols, (t + 1) * cols)
            value = dot(b.act[0, rows, :], b.wf_full[0, :, span], NN)
            value = value + dot(b.act[1, rows, :], b.wf_full[1, :, span], NN)
            b.dpart[lax.rem(j, 2), :, :, span] = value.astype(BF).reshape(2, count, cols)
        part = b.dpart.at[lax.rem(j, 2), 1 - me.k]
        remote(part, b.dsib.at[j], b.dss.at[j], b.dsr.at[j], sib).start()

        @pl.when(i > 0)
        def _():
            take_dn2(j + 1)

        return carry

    lax.fori_loop(0, nc, grad_tokens, 0)
    take_dn2(0)
    for j in range(nc):
        last.append(functools.partial(sent, False, x_own, b.xfs2.at[j], sib))
        if j:
            last.append(functools.partial(sent, False, x_own, b.xs2.at[j], sib))
    for copy in last:
        copy()
    last.clear()
    for m in range(3):
        for way in range(3):
            unit_copy(way, m).wait_send()
    bg = (b.wf_full.at[0], b.wf_full.at[1], b.down)

    def grads(t, then):
        span = pl.ds(tall(t * tile, tile), tile)
        tokens = nc * 2 * count
        for m in range(3):
            left = b.act[m, :, span].T
            for c in range(width // cols):
                part = slice(c * cols, (c + 1) * cols)
                if m < 2:
                    right = b.xall[:, :, :, part].reshape(tokens, cols)
                else:
                    right = b.dyb[:, :, part].reshape(tokens, cols)
                bg[m][span, part] = dot(left, right, NN).astype(BF)
            then(m)

    def band_rows(at):
        return pl.ds(tall(at * band, band), band)

    def send_terms(stage, at, to, m):
        src = bg[m].at[band_rows(at), :]
        remote(src, b.rs.at[stage, m], b.gs.at[stage, m], b.gr.at[stage, m], (me.d, to)).start()

    def cross_terms(m):
        arrived(b.rs.at[0, m], b.gr.at[0, m])
        value = bg[m][band_rows(far), :].astype(F32) + b.rs[0, m].astype(F32)
        bg[m][band_rows(far), :] = value.astype(BF)
        send_terms(2, far, far, m)

    grads(1 - near_tile, lambda m: send_terms(0, beyond, near, m))
    grads(near_tile, lambda m: None)
    def add_branch(j):
        arrived(b.dsib.at[j], b.bsr.at[j])
        value = b.dpart[lax.rem(j, 2), me.k].astype(F32) + b.dsib[j].astype(F32)
        value = value.astype(BF)

        @pl.when(j == 0)
        def _():
            b.xown[...] = value

        @pl.when(j > 0)
        def _():
            remote(b.dsum.at[j], b.drecv.at[j - 1], b.dps.at[j], b.dpr.at[j], sib).wait_send()
            b.dsum[j] = value
            cj = lax.rem(me.gc + nc - j, nc)
            to = (me.in_group(cj, me.k), me.s)
            remote(b.dsum.at[j], b.brr.at[j - 1], b.brs.at[j], b.brr_sem.at[j], to).start()

    def branch(i, carry):
        j = nc - 1 - i
        _, rows = chip_rows(j)

        @pl.when(i > 1)
        def _():
            sent(False, b.dpart.at[0, 0], b.bss.at[j + 2], sib)

        for t in range(width // cols):
            span = slice(t * cols, (t + 1) * cols)
            value = dot(b.act[2, rows, :], b.wf_full[2, :, span], NN)
            b.dpart[lax.rem(j, 2), :, :, span] = value.astype(BF).reshape(2, count, cols)

        @pl.when(i > 0)
        def _():
            add_branch(j + 1)

        part = b.dpart.at[lax.rem(j, 2), 1 - me.k]
        remote(part, b.dsib.at[j], b.bss.at[j], b.bsr.at[j], sib).start()
        return carry

    lax.fori_loop(0, nc, branch, 0)

    add_branch(0)
    for j in range(min(2, nc)):
        sent(False, b.dpart.at[0, 0], b.bss.at[j], sib)
    for j in range(1, nc):
        arrived(b.drecv.at[j - 1], b.dpr.at[j])

    def add_ln(row, value):
        for t in range(tiles):
            b.lnp[t, row : row + 1, :] += value[:, t * LANES : (t + 1) * LANES]

    b.lnp[...] = jnp.zeros_like(b.lnp)

    def second_back(rows):
        grad = b.dsum[0, rows, :].astype(F32)
        for j in range(1, nc):
            grad = grad + b.drecv[j - 1, rows, :].astype(F32)
        normal = b.norm[rows, :]
        add_ln(2, jnp.sum(grad * normal, axis=0, keepdims=True))
        add_ln(3, jnp.sum(grad, axis=0, keepdims=True))
        dmid = b.ig[rows, :] + norm_back(grad, normal, b.scale[rows, 0:1], b.gain[2:3, :])
        b.ig[rows, :] = dmid
        b.dmb[rows, :] = dmid.astype(BF)

    by_rows(second_back)
    dmb = b.dmb[...]
    for i in range(seq):
        here = jnp.logical_and(i == me.s, owner == me.d)
        sent(here, b.mixed.at[i], b.ms.at[i], sib)
    for hg in range(seq):
        b.mixed[hg] = dot(dmb, b.wo_full[hg * block : (hg + 1) * block, :], NT).astype(BF)
        to = (2 * me.c + hg % 2, me.k * me.half + hg // 2)
        here = jnp.logical_and(to[0] == me.d, to[1] == me.s)
        send_or_keep(
            here, b.mixed.at[hg], b.dmix_row.at[me.s], b.dms.at[hg], b.dmr.at[me.s], to
        )
        last.append(functools.partial(sent, here, b.mixed.at[hg], b.dms.at[hg], sib))
    pieces = width // 2 // count

    def og_rows(parity):
        return b.dyb.at[pl.ds(parity * pieces, pieces)]

    for h in range(seq):
        part = dot(b.mixed_in[h], dmb, TN).astype(BF)
        for t in range(block // cr):
            first = h * (block // cr) + t
            row = (first // 2) * cr
            b.dyb[(first % 2) * pieces + row // count, row % count : row % count + cr, :] = part[
                t * cr : (t + 1) * cr
            ]
    remote(og_rows(1 - me.k), b.ogsib, b.o1.at[0], b.o1.at[1], sib).start()
    for j in range(seq):
        arrived(b.dmix_row.at[j], b.dmr.at[j])
    for m in range(3):
        cross_terms(m)
    for m in range(3):
        send_terms(1, near, near, m)
    b.dk[...] = jnp.zeros_like(b.dk)
    b.dv[...] = jnp.zeros_like(b.dv)

    def og_sum():
        remote(b.ogsib, b.ogsib, b.o1.at[0], b.o1.at[1], sib).wait()
        for i in range(pieces):
            value = b.dyb[me.k * pieces + i].astype(F32) + b.ogsib[i].astype(F32)
            b.dyb[2 * pieces + i] = value.astype(BF)

        def send_og(j, carry):
            chip = lax.rem(me.c + j, me.chips)
            row = chip * cr
            src = b.dyb.at[2 * pieces + row // count, pl.ds(tall(lax.rem(row, count), cr), cr), :]
            remote(src, b.ogpl.at[j], b.o2s.at[j], b.o2r.at[j], (2 * chip + me.k, me.s)).start()
            return carry

        lax.fori_loop(1, me.chips, send_og, 0)

    def og_column():
        row = me.c * cr
        at = pl.ds(tall(lax.rem(row, count), cr), cr)
        acc = b.dyb[2 * pieces + row // count, at, :].astype(F32)
        for j in range(1, me.chips):
            remote(b.ogpl.at[j], b.ogpl.at[j], b.o2s.at[j], b.o2r.at[j], sib).wait()
            acc = acc + b.ogpl[j].astype(F32)
        b.ogc[...] = acc.astype(BF)
        for j in range(1, seq):
            to = lax.rem(me.s + j, seq)
            src = b.ogc.at[pl.ds(tall(to * wr, wr), wr), :]
            remote(src, b.ogz.at[j], b.o3s.at[j], b.o3r.at[j], (me.d, to)).start()

    def attend_back(i, carry):
        rows = pl.ds(tall(i * count, count), count)
        q = b.q[rows, :]
        dm = b.dmix_row[i]
        lse = b.lse[rows, :]
        segment = b.lse[rows, LANES - 1 : LANES]
        bias = jnp.where(segment == b.seg_row[0:1, :], 0.0, -1e30)
        grad_q = jnp.zeros((count, block), F32)
        for h in range(heads):
            mask = head_mask((count, block), h)
            qh = jnp.where(mask, q, jnp.zeros_like(q))
            dmh = jnp.where(mask, dm, jnp.zeros_like(dm))
            score = dot(qh, b.kk[...], NT) * 0.125 + bias
            prob = jnp.exp(score - lse[:, h : h + 1])
            dprob = dot(dmh, b.v[...], NT)
            centre = jnp.sum(prob * dprob, axis=1, keepdims=True)
            ds = (0.125 * prob * (dprob - centre)).astype(BF)
            grad_q = jnp.where(mask, dot(ds, b.kk[...], NN), grad_q)
            b.dk[...] += dot(ds, qh, TN)
            b.dv[...] += dot(prob.astype(BF), dmh, TN)
        cosine = jnp.concatenate([b.cos[rows, :]] * (block // LANES), axis=1)
        sine = jnp.concatenate([b.sin[rows, :]] * (block // LANES), axis=1)
        b.act[0, rows, 0:block] = (grad_q * cosine - swap_halves(grad_q) * sine).astype(BF)

        @pl.when(i == 0)
        def _():
            og_sum()

        return carry

    lax.fori_loop(0, seq, attend_back, 0)

    def back_chunk(i):
        rows = pl.ds(tall(i * count, count), count)
        cosine = jnp.concatenate([b.cos[rows, :]] * (block // LANES), axis=1)
        sine = jnp.concatenate([b.sin[rows, :]] * (block // LANES), axis=1)
        grad_k = b.dk[rows, :]
        dk = (grad_k * cosine - swap_halves(grad_k) * sine).astype(BF)
        dv = b.dv[rows, :].astype(BF)
        b.act[1, rows, 0:block] = dk
        b.act[2, rows, 0:block] = dv
        value = dot(b.act[0, rows, 0:block], b.wq_full[0], NT)
        value = value + dot(dk, b.wq_full[1], NT) + dot(dv, b.wq_full[2], NT)
        at = lax.rem(i, 2) * me.half + i // 2
        b.xall[at // 2, lax.rem(at, 2)] = value.astype(BF)

    def other_half(j, carry):
        back_chunk(2 * j + 1 - me.k)
        return carry

    def own_half_chunks(j, carry):
        back_chunk(2 * j + me.k)
        return carry

    lax.fori_loop(0, me.half, other_half, 0)
    quarter = me.half // 2
    dn_other = b.xall.at[pl.ds((1 - me.k) * quarter, quarter)]
    remote(dn_other, b.dnsib, b.n1.at[0], b.n1.at[1], sib).start()
    lax.fori_loop(0, me.half, own_half_chunks, 0)
    remote(b.dnsib, b.dnsib, b.n1.at[0], b.n1.at[1], sib).wait()
    for j in range(me.half):
        value = b.xall[me.k * quarter + j // 2, j % 2].astype(F32)
        b.dpart[0, j] = (value + b.dnsib[j // 2, j % 2].astype(F32)).astype(BF)
        i = 2 * j + me.k
        here = jnp.logical_and(owner == me.d, i == me.s)
        send_or_keep(
            here, b.dpart.at[0, j], b.dnr.at[me.h], b.n2s.at[j], b.n2r.at[me.h], (owner, i)
        )
        last.append(functools.partial(sent, here, b.dpart.at[0, j], b.n2s.at[j], sib))
    span_rows = 2 * cr
    per_tile = block // span_rows

    def qkv_terms(j, carry):
        at = lax.rem(me.c // per_tile + j, width // block)
        x = b.xrow[:, pl.ds(tall(at * block, block), block)]
        rows = pl.ds(tall(total + at * block, block), block)
        for t in range(3):
            b.act[t, rows, 0:block] = dot(x, b.act[t, 0:total, 0:block], TN).astype(BF)
        for i in range(per_tile):
            chip = at * per_tile + i

            @pl.when(chip != me.c)
            def _(chip=chip):
                src = b.act.at[:, pl.ds(tall(total + chip * span_rows, span_rows), span_rows), 0:block]
                to = (2 * chip + me.k, me.s)
                remote(src, b.qgpl.at[me.c], b.q1s.at[chip], b.q1r.at[me.c], to).start()

        return carry

    lax.fori_loop(1, width // block, qkv_terms, 0)
    qkv_terms(0, 0)
    og_column()
    tok = local(b.tok, b.norm, b.load.at[0])
    tok.start()
    tok.wait()
    for h in range(me.half):
        arrived(b.dnr.at[h], b.n2r.at[h])

    def first_back(rows):
        grad = b.dnr[0, rows, :].astype(F32)
        for h in range(1, me.half):
            grad = grad + b.dnr[h, rows, :].astype(F32)
        normal, scale = normalise(b.norm[rows, :])
        b.ig[rows, :] += norm_back(grad, normal, scale, b.gain[0:1, :])
        add_ln(0, jnp.sum(grad * normal, axis=0, keepdims=True))
        add_ln(1, jnp.sum(grad, axis=0, keepdims=True))

    by_rows(first_back)
    store(1)

    def send_lnp(j, carry):
        other = lax.rem(me.n + j, me.total)
        remote(
            b.lnp.at[other // per], b.lnr.at[me.n], b.lnt.at[0], b.lnt.at[1], me.of_rank(other)
        ).start()
        return carry

    lax.fori_loop(1, me.total, send_lnp, 0)
    b.lnr[me.n] = b.lnp[me.n // per]
    own = pl.ds(tall(total + me.c * span_rows, span_rows), span_rows)
    sums = [b.act[t, own, 0:block].astype(F32) for t in range(3)]
    for j in range(1, me.chips):
        chip = lax.rem(me.c + j, me.chips)
        part = b.qgpl.at[chip]
        remote(part, part, b.q1s.at[chip], b.q1r.at[chip], sib).wait()
        for t in range(3):
            sums[t] = sums[t] + b.qgpl[chip, t].astype(F32)
    for t in range(3):
        b.qgc[t] = sums[t].astype(BF)
    source = me.k * seq + me.s
    for core in range(2):
        for j in range(seq):
            to = lax.rem(me.s + j, seq)
            src = b.qgc.at[:, pl.ds(tall((core * seq + to) * wr, wr), wr), :]
            here = jnp.logical_and(core == me.k, to == me.s)
            send_or_keep(
                here, src, b.qgz.at[source], b.q2s.at[core, j], b.q2r.at[source], (2 * me.c + core, to)
            )
            last.append(functools.partial(sent, here, src, b.q2s.at[core, j], sib))
    value = b.out[...] + b.xown[...].astype(F32)
    for j in range(1, nc):
        remote(b.brr.at[j - 1], b.brr.at[j - 1], b.brs.at[j], b.brr_sem.at[j], sib).wait()
        value = value + b.brr[j - 1].astype(F32)
    b.out[...] = value
    store(0)
    acc = b.ogc[pl.ds(tall(me.s * wr, wr), wr), :].astype(F32)
    for j in range(1, seq):
        remote(b.ogz.at[j], b.ogz.at[j], b.o3s.at[j], b.o3r.at[j], sib).wait()
        acc = acc + b.ogz[j].astype(F32)
    b.og[...] = acc
    store(4)
    for m in range(3):
        for j in range(1, 3):
            arrived(b.rs.at[j, m], b.gr.at[j, m])
        for j in range(3):
            last.append(functools.partial(sent, False, b.rs.at[0, 0], b.gs.at[j, m], sib))
        acc = bg[m][band_rows(me.s), :].astype(F32)
        acc = acc + b.rs[1, m].astype(F32) + b.rs[2, m].astype(F32)
        if me.groups == 1:
            b.fg[m] = acc
        else:
            bg[m][band_rows(me.s), :] = acc.astype(BF)
    if me.groups > 1:
        for m in range(3):
            for j in range(1, me.groups):
                other = lax.rem(me.g + j, me.groups)
                src = bg[m].at[pl.ds(tall(me.s * band + other * units, units), units), :]
                to = (other * me.group + me.p, me.s)
                remote(src, b.grp.at[j, m], b.grs.at[j, m], b.grr.at[j, m], to).start()
        for m in range(3):
            acc = bg[m][pl.ds(tall(me.s * band + me.g * units, units), units), :].astype(F32)
            for j in range(1, me.groups):
                part = b.grp.at[j, m]
                remote(part, part, b.grs.at[j, m], b.grr.at[j, m], sib).wait()
                acc = acc + b.grp[j, m].astype(F32)
            b.fg[m] = acc
    store(5)
    rest = b.lnr.at[pl.ds(0, me.total - 1)]
    remote(rest, rest, b.lnt.at[0], b.lnt.at[1], sib).wait()
    acc = b.lnr[0]
    for j in range(1, me.total):
        acc = acc + b.lnr[j]
    for i in range(fit):

        @pl.when(lax.rem(me.n, fit) == i)
        def _(i=i):
            b.lng[...] = acc[0:4, i * share : (i + 1) * share]

    store(2)
    for j in range(2 * seq):
        arrived(b.qgz.at[j], b.q2r.at[j])
    for hg in range(seq):
        core, h = hg % 2, hg // 2
        acc = b.qgz[core * seq + h].astype(F32) + b.qgz[core * seq + me.half + h].astype(F32)
        b.qg[:, :, hg * block : (hg + 1) * block] = acc
    store(3)
    for copy in last:
        copy()
    for copy in stores:
        copy.wait()


def keep_kernel(count, *refs):
    given, kept, held = refs[:count], refs[count : 2 * count], refs[2 * count : 3 * count]
    sems = refs[-1]
    ins = [local(given[i], held[i], sems.at[0, i]) for i in range(count)]
    outs = [local(held[i], kept[i], sems.at[1, i]) for i in range(count)]
    for copy in ins:
        copy.start()
    for i in range(count):
        ins[i].wait()
        outs[i].start()
    for copy in outs:
        copy.wait()


def body(dp, seq, tokens, ln_params, qkv_weight, out_weight, ffn_weight, lengths, cotangent):
    count, width = tokens.shape[1], tokens.shape[2]
    ranks = dp * seq
    total = count * seq
    wr = qkv_weight.shape[0]
    cr = wr * seq
    units = ffn_weight.shape[0]
    block = width // seq
    half = seq // 2
    group = min(dp, GROUP)
    groups = dp // group
    gchips, chips, slots = group // 2, dp // 2, groups * seq
    held = units * slots
    share = ln_params.shape[1]
    sem = pltpu.SemaphoreType.DMA
    vm = pltpu.VMEM
    anywhere = pl.BlockSpec(memory_space=pl.ANY)
    vmem = pl.BlockSpec(memory_space=pltpu.VMEM)
    operands = dict(
        tok=(tokens.reshape(count, width), anywhere),
        ln=(ln_params, vmem),
        wq=(qkv_weight.transpose(1, 0, 2), anywhere),
        wo=(out_weight, anywhere),
        wf=(ffn_weight.transpose(1, 0, 2), anywhere),
        lens=(lengths, vmem),
        cot=(cotangent.reshape(count, width), anywhere),
    )
    outs = dict(
        out=(count, width),
        ig=(count, width),
        lng=(4, share),
        qg=(3, wr, width),
        og=(wr, width),
        fg=(3, units, width),
    )
    scratch = dict(
        **{name: vm(dims, F32) for name, dims in outs.items()},
        norm=vm((count, width), F32),
        scale=vm((count, LANES), F32),
        lens_own=vm((8, LANES), jnp.int32),
        lens_pair=vm((2, 8, LANES), jnp.int32),
        ln_own=vm((8, LANES), F32),
        ln_all=vm((ranks, 8, LANES), F32),
        gain=vm((8, width), F32),
        wq_own=vm((3, wr, width), BF),
        wcol=vm((3, cr, 2 * block), BF),
        xown=vm((count, width), BF),
        dmb=vm((count, width), BF),
        xrow=vm((total, width), BF),
        wq_full=vm((3, width, block), BF),
        wo_full=vm((width, width), BF),
        dyb=vm((group, count, width), BF),
        q=vm((total, block), BF),
        kk=vm((total, block), BF),
        v=vm((total, block), BF),
        lse=vm((total, LANES), F32),
        cos=vm((total, LANES), F32),
        sin=vm((total, LANES), F32),
        seg_row=vm((8, total), F32),
        mixed=vm((seq, count, block), BF),
        mixed_in=vm((seq, count, block), BF),
        dmix_row=vm((seq, count, block), BF),
        wf_full=vm((3, held, width), BF),
        xall=vm((gchips, 2, count, width), BF),
        act=vm((3, group * count, held), BF),
        dpart=vm((2, 2, count, width), BF),
        dsib=vm((gchips, count, width), BF),
        dsum=vm((gchips, count, width), BF),
        drecv=vm((gchips - 1, count, width), BF),
        brr=vm((gchips - 1, count, width), BF),
        ogsib=vm((width // 2 // count, count, width), BF),
        ogpl=vm((chips, cr, width), BF),
        ogc=vm((cr, width), BF),
        ogz=vm((seq, wr, width), BF),
        dk=vm((total, block), F32),
        dv=vm((total, block), F32),
        dnsib=vm((half // 2, 2, count, width), BF),
        dnr=vm((half, count, width), BF),
        qgpl=vm((chips, 3, 2 * cr, block), BF),
        qgc=vm((3, 2 * cr, block), BF),
        qgz=vm((2 * seq, 3, wr, block), BF),
        rs=vm((3, 3, groups * units, width), BF),
        grp=vm((groups, 3, units, width) if groups > 1 else (8, LANES), BF),
        down=vm((held, width), BF),
        lnp=vm((width // LANES, 8, LANES), F32),
        lnr=vm((ranks, 8, LANES), F32),
        load=sem((7,)),
        keep=sem((6,)),
        lns=sem((2,)),
        lens_sem=sem((2,)),
        wq1s=sem((seq,)),
        wq1r=sem((seq,)),
        wq2s=sem((dp,)),
        wq2r=sem((dp,)),
        wo1s=sem((seq,)),
        wo1r=sem((seq,)),
        wo2s=sem((chips,)),
        wo2r=sem((chips,)),
        wo3s=sem((chips,)),
        wo3r=sem((chips,)),
        xs=sem((half, 2)),
        xr=sem((seq,)),
        xfs=sem((seq,)),
        xfr=sem((seq,)),
        dys=sem((gchips,)),
        dyr=sem((gchips,)),
        dyfs=sem((gchips,)),
        dyfr=sem((gchips,)),
        fgs=sem((groups,)),
        fgr_sem=sem((groups,)),
        hs=sem((3, 3)),
        hr=sem((3, 3)),
        ms=sem((seq,)),
        mr=sem((seq,)),
        xs2=sem((gchips,)),
        xr2=sem((gchips,)),
        xfs2=sem((gchips,)),
        xfr2=sem((gchips,)),
        dss=sem((gchips,)),
        dsr=sem((gchips,)),
        dps=sem((gchips,)),
        dpr=sem((gchips,)),
        bss=sem((gchips,)),
        bsr=sem((gchips,)),
        brs=sem((gchips,)),
        brr_sem=sem((gchips,)),
        dms=sem((seq,)),
        dmr=sem((seq,)),
        gs=sem((3, 3)),
        gr=sem((3, 3)),
        grs=sem((groups, 3)),
        grr=sem((groups, 3)),
        o1=sem((2,)),
        o2s=sem((chips,)),
        o2r=sem((chips,)),
        o3s=sem((seq,)),
        o3r=sem((seq,)),
        n1=sem((2,)),
        n2s=sem((half,)),
        n2r=sem((half,)),
        q1s=sem((chips,)),
        q1r=sem((chips,)),
        q2s=sem((2, seq)),
        q2r=sem((2 * seq,)),
        lnt=sem((2,)),
    )
    names = (*operands, *[name + "_out" for name in outs], *scratch)
    results = pl.pallas_call(
        functools.partial(layer_kernel, names, dp, seq, lengths.shape[1]),
        out_shape=tuple(jax.ShapeDtypeStruct(dims, F32) for dims in outs.values()),
        in_specs=[spec for _, spec in operands.values()],
        out_specs=tuple([anywhere] * len(outs)),
        scratch_shapes=list(scratch.values()),
        compiler_params=pltpu.CompilerParams(
            collective_id=1, has_side_effects=True, vmem_limit_bytes=VMEM_BYTES
        ),
        cost_estimate=pl.CostEstimate(
            flops=32 * 10**9, bytes_accessed=2**24, transcendentals=10**7
        ),
        name="layer",
    )(*[value for value, _ in operands.values()])
    out, input_grad, ln_grad, qg, og, fg = pl.pallas_call(
        functools.partial(keep_kernel, len(outs)),
        out_shape=tuple(jax.ShapeDtypeStruct(dims, F32) for dims in outs.values()),
        in_specs=[anywhere] * len(outs),
        out_specs=tuple([anywhere] * len(outs)),
        scratch_shapes=[*[vm(dims, F32) for dims in outs.values()], sem((2, len(outs)))],
        name="keep",
    )(*results)
    return (
        out.reshape(1, count, width),
        input_grad.reshape(1, count, width),
        ln_grad,
        qg.transpose(1, 0, 2),
        og,
        fg.transpose(1, 0, 2),
    )


def solution(mesh):
    dp, seq = mesh.shape["dp"], mesh.shape["seq"]
    both = ("dp", "seq")
    in_specs = (
        P("dp", "seq", None),
        P(None, both),
        P(both, None, None),
        P(both, None),
        P(both, None, None),
        P("dp", None),
        P("dp", "seq", None),
    )
    out_specs = (
        P("dp", "seq", None),
        P("dp", "seq", None),
        P(None, both),
        P(both, None, None),
        P(both, None),
        P(both, None, None),
    )
    return jax.shard_map(
        functools.partial(body, dp, seq),
        mesh=mesh,
        in_specs=in_specs,
        out_specs=out_specs,
        check_vma=False,
    )
```

```python
import functools
import math
import types

import jax
import jax.numpy as jnp
from jax import lax
from jax.experimental import pallas as pl
from jax.experimental.pallas import tpu as pltpu
from jax.sharding import PartitionSpec as P

HEAD_DIM = 64
GROUP = 8
LANES = 128
BF = jnp.bfloat16
F32 = jnp.float32
MESH = pl.DeviceIdType.MESH
NT = (((1,), (1,)), ((), ()))
NN = (((1,), (0,)), ((), ()))
TN = (((0,), (0,)), ((), ()))
EPS = 1e-05
VMEM_BYTES = 62 * 2**20


def dot(a, b, dims):
    return lax.dot_general(a, b, dims, preferred_element_type=F32)


def remote(src, dst, send, recv, device):
    return pltpu.make_async_remote_copy(
        src_ref=src, dst_ref=dst, send_sem=send, recv_sem=recv, device_id=device, device_id_type=MESH
    )


def local(src, dst, sem):
    return pltpu.make_async_copy(src, dst, sem)


class Place:
    def __init__(self, dp, seq):
        self.dp, self.seq = dp, seq
        self.d, self.s = lax.axis_index("dp"), lax.axis_index("seq")
        self.c, self.k = self.d // 2, lax.rem(self.d, 2)
        self.sib = self.d + 1 - 2 * self.k
        self.chips = dp // 2
        self.group = min(dp, GROUP)
        self.groups = dp // self.group
        self.g, self.p = self.d // self.group, lax.rem(self.d, self.group)
        self.gc = self.p // 2
        self.gchips = self.group // 2
        self.half = seq // 2
        self.r, self.h = self.s // self.half, lax.rem(self.s, self.half)
        self.hg = 2 * self.h + self.k
        self.n = self.d * seq + self.s
        self.total = dp * seq

    def of_rank(self, rank):
        return (rank // self.seq, lax.rem(rank, self.seq))

    def in_group(self, chip, core):
        return self.g * self.group + 2 * chip + core


def normalise(value):
    mean = jnp.mean(value, axis=-1, keepdims=True)
    centred = value - mean
    var = jnp.mean(centred * centred, axis=-1, keepdims=True)
    scale = lax.rsqrt(var + EPS)
    return centred * scale, scale


def norm_back(grad, normal, scale, gain):
    scaled = grad * gain
    return scale * (
        scaled
        - jnp.mean(scaled, axis=-1, keepdims=True)
        - normal * jnp.mean(scaled * normal, axis=-1, keepdims=True)
    )


def swap_halves(value):
    half = HEAD_DIM // 2
    width = value.shape[1]
    lane = lax.broadcasted_iota(jnp.int32, value.shape, 1)
    up = pltpu.roll(value, width - half, 1)
    down = pltpu.roll(value, half, 1)
    return jnp.where(lax.rem(lane, HEAD_DIM) < half, up, down)


def head_mask(shape, h):
    lane = lax.broadcasted_iota(jnp.int32, shape, 1)
    return jnp.logical_and(lane >= h * HEAD_DIM, lane < (h + 1) * HEAD_DIM)


def tall(value, rows):
    return pl.multiple_of(value, rows)


def meet(me):
    barrier = pltpu.get_barrier_semaphore()

    def hello(j, carry):
        other = lax.rem(me.n + j, me.total)
        pl.semaphore_signal(barrier, inc=1, device_id=me.of_rank(other), device_id_type=MESH)
        return carry

    lax.fori_loop(1, me.total, hello, 0)


def met(me):
    pl.semaphore_wait(pltpu.get_barrier_semaphore(), me.total - 1)


def send_or_keep(here, src, dst, send, recv, device):
    @pl.when(jnp.logical_not(here))
    def _():
        remote(src, dst, send, recv, device).start()

    @pl.when(here)
    def _():
        local(src, dst, recv).start()


def sent(here, src, send, device):
    @pl.when(jnp.logical_not(here))
    def _():
        remote(src, src, send, send, device).wait_send()


def arrived(dst, recv):
    local(dst, dst, recv).wait()


def layer_kernel(names, dp, seq, segs, *refs):
    b = types.SimpleNamespace(**dict(zip(names, refs)))
    me = Place(dp, seq)
    count, width = b.out.shape
    total = count * seq
    wr = b.og.shape[0]
    cr = wr * seq
    block = b.q.shape[1]
    heads = block // HEAD_DIM
    units = b.fg.shape[1]
    held = b.wf_full.shape[1]
    band = me.groups * units
    nc = me.gchips
    sib = (me.sib, me.s)
    share = b.ln.shape[1]
    fit = LANES // share
    tiles = width // LANES
    per = me.total // tiles
    halfrows = count // 2
    last = []

    def by_rows(step):
        def one(i, carry):
            step(pl.ds(tall(i * some, some), some))
            return carry

        lax.fori_loop(0, count // some, one, 0)

    some = 64
    results = ("out", "ig", "lng", "qg", "og", "fg")
    stores = []

    def store(i):
        name = results[i]
        stores.append(local(getattr(b, name), getattr(b, name + "_out"), b.keep.at[i]))
        stores[-1].start()

    meet(me)
    loads = [
        local(b.tok, b.out, b.load.at[0]),
        local(b.wq, b.qg, b.load.at[1]),
        local(b.wo, b.og, b.load.at[2]),
        local(b.wf, b.fg, b.load.at[3]),
        local(b.cot, b.ig, b.load.at[4]),
    ]
    for copy in loads:
        copy.start()
    b.lens_own[...] = jnp.zeros_like(b.lens_own)
    b.lens_own[0:1, 0:segs] = b.lens[...]
    b.lens_pair[me.k] = b.lens_own[...]
    gains = jnp.concatenate([b.ln[...].astype(BF).astype(F32)] * fit, axis=1)
    lane = lax.broadcasted_iota(jnp.int32, gains.shape, 1)
    b.ln_own[...] = jnp.zeros_like(b.ln_own)
    b.ln_own[0:4, :] = jnp.where(lane // share == lax.rem(me.n, fit), gains, 0.0)
    b.ln_all[me.n] = b.ln_own[...]
    loads[1].wait()
    b.wq_own[...] = b.qg[...].astype(BF)
    loads[0].wait()

    def first_norm(rows):
        b.norm[rows, :] = normalise(b.out[rows, :])[0]

    by_rows(first_norm)
    met(me)

    def send_ln(j, carry):
        other = lax.rem(me.n + j, me.total)
        remote(
            b.ln_own, b.ln_all.at[me.n], b.lns.at[0], b.lns.at[1], me.of_rank(other)
        ).start()
        return carry

    lax.fori_loop(1, me.total, send_ln, 0)
    len_copy = remote(b.lens_own, b.lens_pair.at[me.k], b.lens_sem.at[0], b.lens_sem.at[1], sib)
    len_copy.start()
    pair = 2 * block
    row0 = tall(me.s * wr, wr)
    out0 = tall(me.n * wr, wr)
    wq_first = []
    for j in range(1, seq):
        to = lax.rem(me.s + j, seq)
        col = tall(lax.rem(to, me.half) * pair, pair)
        wq_first.append(
            remote(
                b.wq_own.at[:, :, pl.ds(col, pair)],
                b.wcol.at[:, pl.ds(row0, wr), :],
                b.wq1s.at[j],
                b.wq1r.at[j],
                (me.d, to),
            )
        )
    for copy in wq_first:
        copy.start()
    own_wq = local(
        b.wq_own.at[:, :, pl.ds(tall(me.h * pair, pair), pair)],
        b.wcol.at[:, pl.ds(row0, wr), :],
        b.load.at[5],
    )
    own_wq.start()
    loads[2].wait()
    b.wo_full[pl.ds(out0, wr), :] = b.og[...].astype(BF)
    rest = b.ln_all.at[pl.ds(0, me.total - 1)]
    remote(rest, rest, b.lns.at[0], b.lns.at[1], sib).wait()
    for t in range(tiles):
        part = b.ln_all[t * per]
        for i in range(1, per):
            part = part + b.ln_all[t * per + i]
        b.gain[:, t * LANES : (t + 1) * LANES] = part

    def first_out(rows):
        b.xown[rows, :] = (b.norm[rows, :] * b.gain[0:1, :] + b.gain[1:2, :]).astype(BF)

    by_rows(first_out)
    rows0 = tall(me.s * count, count)
    for j in range(me.half):
        to = me.k * me.half + lax.rem(me.h + j, me.half)
        for core in range(2):
            src = b.xown.at[pl.ds(core * halfrows, halfrows), :]
            dst = b.xrow.at[pl.ds(rows0 + core * halfrows, halfrows), :]
            here = jnp.logical_and(to == me.s, core == me.k)
            send_or_keep(
                here, src, dst, b.xs.at[j, core], b.xr.at[me.s], (2 * me.c + core, to)
            )
            last.append(
                functools.partial(sent, here, src, b.xs.at[j, core], (2 * me.c + core, to))
            )
    for copy in wq_first:
        copy.wait()
    own_wq.wait()
    crow0 = tall(me.d * cr, cr)

    def send_wq(j, carry):
        to = lax.rem(me.d + j, dp)
        remote(
            b.wcol.at[:, :, pl.ds(tall(lax.rem(to, 2) * block, block), block)],
            b.wq_full.at[:, pl.ds(crow0, cr), :],
            b.wq2s.at[j],
            b.wq2r.at[j],
            (to, me.s),
        ).start()
        return carry

    lax.fori_loop(1, dp, send_wq, 0)
    own_half = local(
        b.wcol.at[:, :, pl.ds(tall(me.k * block, block), block)],
        b.wq_full.at[:, pl.ds(crow0, cr), :],
        b.load.at[6],
    )
    own_half.start()
    len_copy.wait()
    row = b.lens_pair[me.r]
    place_row = lax.broadcasted_iota(jnp.int32, (8, total), 1)
    ends = [row[0:1, 0:1]]
    for j in range(1, segs):
        ends.append(ends[-1] + row[0:1, j : j + 1])
    segr = jnp.zeros((8, total), jnp.int32)
    for end in ends:
        segr = segr + (place_row >= end).astype(jnp.int32)
    b.seg_row[...] = segr.astype(F32)
    half = HEAD_DIM // 2
    lane = lax.broadcasted_iota(jnp.int32, (1, LANES), 1)
    rate = jnp.exp(lax.rem(lane, half).astype(F32) * (-math.log(10000.0) / half))
    sign = jnp.where(lax.rem(lane, HEAD_DIM) < half, -1.0, 1.0)

    def angles(i, carry):
        rows = pl.ds(tall(i * LANES, LANES), LANES)
        place = lax.broadcasted_iota(jnp.int32, (LANES, LANES), 0) + i * LANES
        segment = jnp.zeros((LANES, LANES), jnp.int32)
        begin = jnp.zeros((LANES, LANES), jnp.int32)
        for end in ends:
            past = place >= end
            segment = segment + past.astype(jnp.int32)
            begin = jnp.where(past, end, begin)
        b.lse[rows, :] = segment.astype(F32)
        angle = (place - begin).astype(F32) * rate
        b.cos[rows, :] = jnp.cos(angle)
        b.sin[rows, :] = jnp.sin(angle) * sign
        return carry

    lax.fori_loop(0, total // LANES, angles, 0)
    loads[4].wait()
    b.dyb[me.p] = b.ig[...].astype(BF)
    loads[3].wait()
    own_units = pl.ds(tall(me.s * band + me.g * units, units), units)
    b.wf_full[:, own_units, :] = b.fg[...].astype(BF)
    for j in range(seq):
        source = lax.rem(me.s + j, seq)
        part = b.xrow.at[pl.ds(tall(source * count + me.k * halfrows, halfrows), halfrows), :]
        arrived(part, b.xr.at[source])
        remote(part, part, b.xfs.at[j], b.xfr.at[j], sib).start()
    wo_own = b.wo_full.at[pl.ds(out0, wr), :]
    wo_first = []
    for j in range(1, seq):
        to = (me.d, lax.rem(me.s + j, seq))
        wo_first.append(remote(wo_own, wo_own, b.wo1s.at[j], b.wo1r.at[j], to))
    for copy in wo_first:
        copy.start()
    for j in range(1, me.groups):
        other = lax.rem(me.g + j, me.groups)
        mine = b.wf_full.at[:, own_units, :]
        remote(
            mine, mine, b.fgs.at[j], b.fgr_sem.at[j], (other * me.group + me.p, me.s)
        ).start()
    for j in range(1, me.groups):
        mine = b.wf_full.at[:, own_units, :]
        remote(mine, mine, b.fgs.at[j], b.fgr_sem.at[j], sib).wait()

    near, far = me.s + 1 - 2 * lax.rem(me.s, 2), lax.rem(me.s + 2, seq)
    beyond = lax.rem(near + 2, seq)

    def column(m, at):
        return b.wf_full.at[m, pl.ds(tall(at * band, band), band), :]

    def unit_copy(way, m):
        part = column(m, far if way == 2 else me.s)
        to = (me.d, near if way else far)
        return remote(part, part, b.hs.at[way, m], b.hr.at[way, m], to)

    def send_units(m):
        unit_copy(0, m).start()
        unit_copy(1, m).start()

    def pass_units(m):
        arrived(column(m, far), b.hr.at[0, m])
        unit_copy(2, m).start()

    for j in range(seq):
        part = b.xrow.at[pl.ds(0, halfrows), :]
        arrived(part, b.xfr.at[j])
        last.append(functools.partial(sent, False, part, b.xfs.at[j], sib))

    def wait_wq(j, carry):
        part = b.wq_full.at[:, pl.ds(0, cr), :]
        remote(part, part, b.wq2s.at[j], b.wq2r.at[j], sib).wait()
        return carry

    lax.fori_loop(1, dp, wait_wq, 0)
    own_half.wait()
    def project(i, carry):
        rows = pl.ds(tall(i * count, count), count)
        x = b.xrow[rows, :]
        cosine = jnp.concatenate([b.cos[rows, :]] * (block // LANES), axis=1)
        sine = jnp.concatenate([b.sin[rows, :]] * (block // LANES), axis=1)
        raw = dot(x, b.wq_full[0], NN)
        b.q[rows, :] = (raw * cosine + swap_halves(raw) * sine).astype(BF)
        raw = dot(x, b.wq_full[1], NN)
        b.kk[rows, :] = (raw * cosine + swap_halves(raw) * sine).astype(BF)
        b.v[rows, :] = dot(x, b.wq_full[2], NN).astype(BF)
        return carry

    lax.fori_loop(0, seq, project, 0)
    owner = 2 * me.c + me.r
    mine = b.wo_full.at[pl.ds(crow0, cr), :]
    for copy in wo_first:
        copy.wait()
    remote(mine, mine, b.wo3s.at[0], b.wo3r.at[0], sib).start()
    for j in range(1, me.chips):
        to = 2 * lax.rem(me.c + j, me.chips) + me.k
        remote(mine, mine, b.wo2s.at[j], b.wo2r.at[j], (to, me.s)).start()
    dy_own = b.dyb.at[me.p]
    remote(dy_own, dy_own, b.dyfs.at[0], b.dyfr.at[0], sib).start()
    for j in range(1, nc):
        to = me.in_group(lax.rem(me.gc + j, nc), me.k)
        remote(dy_own, dy_own, b.dys.at[j], b.dyr.at[j], (to, me.s)).start()

    def attend(step, carry):
        i = lax.rem(me.s + step, seq)
        rows = pl.ds(tall(i * count, count), count)
        q = b.q[rows, :]
        segment = b.lse[rows, LANES - 1 : LANES]
        bias = jnp.where(segment == b.seg_row[0:1, :], 0.0, -1e30)
        lane = lax.broadcasted_iota(jnp.int32, (count, LANES), 1)
        lse = b.lse[rows, :]
        out = jnp.zeros((count, block), F32)
        for h in range(heads):
            mask = head_mask((count, block), h)
            score = dot(jnp.where(mask, q, jnp.zeros_like(q)), b.kk[...], NT) * 0.125 + bias
            top = jnp.max(score, axis=1, keepdims=True)
            weight = jnp.exp(score - top)
            tally = jnp.sum(weight, axis=1, keepdims=True)
            prob = (weight * (1.0 / tally)).astype(BF)
            out = jnp.where(mask, dot(prob, b.v[...], NN), out)
            lse = jnp.where(lane == h, top + jnp.log(tally), lse)
        b.lse[rows, :] = lse
        b.mixed[i] = out.astype(BF)
        here = jnp.logical_and(i == me.s, owner == me.d)
        send_or_keep(
            here, b.mixed.at[i], b.mixed_in.at[me.hg], b.ms.at[i], b.mr.at[me.hg], (owner, i)
        )

        return carry

    lax.fori_loop(0, seq, attend, 0)
    for m in range(3):
        send_units(m)
    for j in range(1, me.chips):
        source = 2 * lax.rem(me.c + me.chips - j, me.chips) + me.k
        part = b.wo_full.at[pl.ds(tall(source * cr, cr), cr), :]
        arrived(part, b.wo2r.at[j])
        remote(part, part, b.wo3s.at[j], b.wo3r.at[j], sib).start()
        last.append(functools.partial(sent, False, part, b.wo2s.at[j], sib))
        last.append(functools.partial(sent, False, part, b.wo3s.at[j], sib))
    last.append(functools.partial(sent, False, mine, b.wo3s.at[0], sib))
    for j in range(me.chips):
        arrived(mine, b.wo3r.at[j])
    for j in range(seq):
        arrived(b.mixed_in.at[j], b.mr.at[j])
    for t in range(width // block):
        span = slice(t * block, (t + 1) * block)
        part = b.out[:, span]
        for h in range(seq):
            part = part + dot(b.mixed_in[h], b.wo_full[h * block : (h + 1) * block, span], NN)
        b.out[:, span] = part

    def second_norm(rows):
        normal, scale = normalise(b.out[rows, :])
        b.norm[rows, :] = normal
        b.scale[rows, :] = jnp.broadcast_to(scale, (some, LANES))
        b.xall[me.gc, me.k, rows, :] = (normal * b.gain[2:3, :] + b.gain[3:4, :]).astype(BF)

    by_rows(second_norm)
    x_own = b.xall.at[me.gc, me.k]
    remote(x_own, x_own, b.xfs2.at[0], b.xfr2.at[0], sib).start()
    for j in range(1, nc):
        to = me.in_group(lax.rem(me.gc + j, nc), me.k)
        remote(x_own, x_own, b.xs2.at[j], b.xr2.at[j], (to, me.s)).start()
    pass_units(0)
    for j in range(1, nc):
        source = 2 * lax.rem(me.gc + nc - j, nc) + me.k
        part = b.dyb.at[source]
        arrived(part, b.dyr.at[j])
        remote(part, part, b.dyfs.at[j], b.dyfr.at[j], sib).start()
        last.append(functools.partial(sent, False, part, b.dys.at[j], sib))
        last.append(functools.partial(sent, False, part, b.dyfs.at[j], sib))
    last.append(functools.partial(sent, False, dy_own, b.dyfs.at[0], sib))
    for j in range(nc):
        arrived(dy_own, b.dyfr.at[j])
    tile = 2 * band
    cols = 256
    near_tile = me.s // 2

    def chip_rows(j):
        cj = lax.rem(me.gc + nc - j, nc)
        return cj, pl.ds(tall(cj * 2 * count, 2 * count), 2 * count)

    def hidden(j, t):
        cj, rows = chip_rows(j)
        span = pl.ds(tall(t * tile, tile), tile)
        x = b.xall[cj].reshape(2 * count, width)
        dy = b.dyb[pl.ds(2 * cj, 2)].reshape(2 * count, width)
        gate = dot(x, b.wf_full[0, span, :], NT)
        up = dot(x, b.wf_full[1, span, :], NT)
        dh = dot(dy, b.wf_full[2, span, :], NT)
        sigma = 1.0 / (1.0 + jnp.exp(-gate))
        active = gate * sigma
        b.act[2, rows, span] = (active * up).astype(BF)
        b.act[0, rows, span] = (dh * up * (sigma * (1.0 + gate * (1.0 - sigma)))).astype(BF)
        b.act[1, rows, span] = (dh * active).astype(BF)

    def near_units(j, carry):
        cj, _ = chip_rows(j)

        @pl.when(j > 0)
        def _():
            part = b.xall.at[cj, me.k]
            arrived(part, b.xr2.at[j])
            remote(part, part, b.xfs2.at[j], b.xfr2.at[j], sib).start()

        @pl.when((j > 0) & (j < 3))
        def _():
            pass_units(j)

        arrived(b.xall.at[cj, 1 - me.k], b.xfr2.at[j])
        hidden(j, near_tile)
        return carry

    def far_units(j, carry):
        hidden(j, 1 - near_tile)
        return carry

    for m in range(3):
        arrived(column(m, near), b.hr.at[1, m])
    lax.fori_loop(0, nc, near_units, 0)
    for m in range(3):
        arrived(column(m, beyond), b.hr.at[2, m])
    lax.fori_loop(0, nc, far_units, 0)

    def take_dn2(j):
        part = b.dsib.at[j]
        remote(part, part, b.dss.at[j], b.dsr.at[j], sib).wait()
        value = b.dpart[lax.rem(j, 2), me.k].astype(F32) + b.dsib[j].astype(F32)
        b.dsum[j] = value.astype(BF)

        @pl.when(j > 0)
        def _():
            to = (me.in_group(chip_rows(j)[0], me.k), me.s)
            remote(b.dsum.at[j], b.drecv.at[j - 1], b.dps.at[j], b.dpr.at[j], to).start()

    def grad_tokens(i, carry):
        j = nc - 1 - i
        _, rows = chip_rows(j)
        for t in range(width // cols):
            span = slice(t * cols, (t + 1) * cols)
            value = dot(b.act[0, rows, :], b.wf_full[0, :, span], NN)
            value = value + dot(b.act[1, rows, :], b.wf_full[1, :, span], NN)
            b.dpart[lax.rem(j, 2), :, :, span] = value.astype(BF).reshape(2, count, cols)
        part = b.dpart.at[lax.rem(j, 2), 1 - me.k]
        remote(part, b.dsib.at[j], b.dss.at[j], b.dsr.at[j], sib).start()

        @pl.when(i > 0)
        def _():
            take_dn2(j + 1)

        return carry

    lax.fori_loop(0, nc, grad_tokens, 0)
    take_dn2(0)
    for j in range(nc):
        last.append(functools.partial(sent, False, x_own, b.xfs2.at[j], sib))
        if j:
            last.append(functools.partial(sent, False, x_own, b.xs2.at[j], sib))
    for copy in last:
        copy()
    last.clear()
    for m in range(3):
        for way in range(3):
            unit_copy(way, m).wait_send()
    bg = (b.wf_full.at[0], b.wf_full.at[1], b.down)

    def grads(t, then):
        span = pl.ds(tall(t * tile, tile), tile)
        tokens = nc * 2 * count
        for m in range(3):
            left = b.act[m, :, span].T
            for c in range(width // cols):
                part = slice(c * cols, (c + 1) * cols)
                if m < 2:
                    right = b.xall[:, :, :, part].reshape(tokens, cols)
                else:
                    right = b.dyb[:, :, part].reshape(tokens, cols)
                bg[m][span, part] = dot(left, right, NN).astype(BF)
            then(m)

    def band_rows(at):
        return pl.ds(tall(at * band, band), band)

    def send_terms(stage, at, to, m):
        src = bg[m].at[band_rows(at), :]
        remote(src, b.rs.at[stage, m], b.gs.at[stage, m], b.gr.at[stage, m], (me.d, to)).start()

    def cross_terms(m):
        arrived(b.rs.at[0, m], b.gr.at[0, m])
        value = bg[m][band_rows(far), :].astype(F32) + b.rs[0, m].astype(F32)
        bg[m][band_rows(far), :] = value.astype(BF)
        send_terms(2, far, far, m)

    grads(1 - near_tile, lambda m: send_terms(0, beyond, near, m))
    grads(near_tile, lambda m: None)
    for j in range(1, nc):
        arrived(b.drecv.at[j - 1], b.dpr.at[j])

    def add_ln(row, value):
        for t in range(tiles):
            b.lnp[t, row : row + 1, :] += value[:, t * LANES : (t + 1) * LANES]

    b.lnp[...] = jnp.zeros_like(b.lnp)

    def second_back(rows):
        grad = b.dsum[0, rows, :].astype(F32)
        for j in range(1, nc):
            grad = grad + b.drecv[j - 1, rows, :].astype(F32)
        normal = b.norm[rows, :]
        add_ln(2, jnp.sum(grad * normal, axis=0, keepdims=True))
        add_ln(3, jnp.sum(grad, axis=0, keepdims=True))
        dmid = b.ig[rows, :] + norm_back(grad, normal, b.scale[rows, 0:1], b.gain[2:3, :])
        b.ig[rows, :] = dmid
        b.dmb[rows, :] = dmid.astype(BF)

    by_rows(second_back)
    dmb = b.dmb[...]
    for i in range(seq):
        here = jnp.logical_and(i == me.s, owner == me.d)
        sent(here, b.mixed.at[i], b.ms.at[i], sib)
    for hg in range(seq):
        b.mixed[hg] = dot(dmb, b.wo_full[hg * block : (hg + 1) * block, :], NT).astype(BF)
        to = (2 * me.c + hg % 2, me.k * me.half + hg // 2)
        here = jnp.logical_and(to[0] == me.d, to[1] == me.s)
        send_or_keep(
            here, b.mixed.at[hg], b.dmix_row.at[me.s], b.dms.at[hg], b.dmr.at[me.s], to
        )
        last.append(functools.partial(sent, here, b.mixed.at[hg], b.dms.at[hg], sib))
    pieces = width // 2 // count

    def og_rows(parity):
        return b.dyb.at[pl.ds(parity * pieces, pieces)]

    for h in range(seq):
        part = dot(b.mixed_in[h], dmb, TN).astype(BF)
        for t in range(block // cr):
            first = h * (block // cr) + t
            row = (first // 2) * cr
            b.dyb[(first % 2) * pieces + row // count, row % count : row % count + cr, :] = part[
                t * cr : (t + 1) * cr
            ]
    remote(og_rows(1 - me.k), b.ogsib, b.o1.at[0], b.o1.at[1], sib).start()
    def add_branch(j):
        arrived(b.dsib.at[j], b.bsr.at[j])
        value = b.dpart[lax.rem(j, 2), me.k].astype(F32) + b.dsib[j].astype(F32)
        value = value.astype(BF)

        @pl.when(j == 0)
        def _():
            b.xown[...] = value

        @pl.when(j > 0)
        def _():
            remote(b.dsum.at[j], b.drecv.at[j - 1], b.dps.at[j], b.dpr.at[j], sib).wait_send()
            b.dsum[j] = value
            cj = lax.rem(me.gc + nc - j, nc)
            to = (me.in_group(cj, me.k), me.s)
            remote(b.dsum.at[j], b.brr.at[j - 1], b.brs.at[j], b.brr_sem.at[j], to).start()

    def branch(i, carry):
        j = nc - 1 - i
        _, rows = chip_rows(j)

        @pl.when(i > 1)
        def _():
            sent(False, b.dpart.at[0, 0], b.bss.at[j + 2], sib)

        for t in range(width // cols):
            span = slice(t * cols, (t + 1) * cols)
            value = dot(b.act[2, rows, :], b.wf_full[2, :, span], NN)
            b.dpart[lax.rem(j, 2), :, :, span] = value.astype(BF).reshape(2, count, cols)

        @pl.when(i > 0)
        def _():
            add_branch(j + 1)

        part = b.dpart.at[lax.rem(j, 2), 1 - me.k]
        remote(part, b.dsib.at[j], b.bss.at[j], b.bsr.at[j], sib).start()
        return carry

    lax.fori_loop(0, nc, branch, 0)

    add_branch(0)
    for j in range(min(2, nc)):
        sent(False, b.dpart.at[0, 0], b.bss.at[j], sib)
    for j in range(seq):
        arrived(b.dmix_row.at[j], b.dmr.at[j])
    for m in range(3):
        cross_terms(m)
    for m in range(3):
        send_terms(1, near, near, m)
    b.dk[...] = jnp.zeros_like(b.dk)
    b.dv[...] = jnp.zeros_like(b.dv)

    def og_sum():
        remote(b.ogsib, b.ogsib, b.o1.at[0], b.o1.at[1], sib).wait()
        for i in range(pieces):
            value = b.dyb[me.k * pieces + i].astype(F32) + b.ogsib[i].astype(F32)
            b.dyb[2 * pieces + i] = value.astype(BF)

        def send_og(j, carry):
            chip = lax.rem(me.c + j, me.chips)
            row = chip * cr
            src = b.dyb.at[2 * pieces + row // count, pl.ds(tall(lax.rem(row, count), cr), cr), :]
            remote(src, b.ogpl.at[j], b.o2s.at[j], b.o2r.at[j], (2 * chip + me.k, me.s)).start()
            return carry

        lax.fori_loop(1, me.chips, send_og, 0)

    def og_column():
        row = me.c * cr
        at = pl.ds(tall(lax.rem(row, count), cr), cr)
        acc = b.dyb[2 * pieces + row // count, at, :].astype(F32)
        for j in range(1, me.chips):
            remote(b.ogpl.at[j], b.ogpl.at[j], b.o2s.at[j], b.o2r.at[j], sib).wait()
            acc = acc + b.ogpl[j].astype(F32)
        b.ogc[...] = acc.astype(BF)
        for j in range(1, seq):
            to = lax.rem(me.s + j, seq)
            src = b.ogc.at[pl.ds(tall(to * wr, wr), wr), :]
            remote(src, b.ogz.at[j], b.o3s.at[j], b.o3r.at[j], (me.d, to)).start()

    def attend_back(i, carry):
        rows = pl.ds(tall(i * count, count), count)
        q = b.q[rows, :]
        dm = b.dmix_row[i]
        lse = b.lse[rows, :]
        segment = b.lse[rows, LANES - 1 : LANES]
        bias = jnp.where(segment == b.seg_row[0:1, :], 0.0, -1e30)
        grad_q = jnp.zeros((count, block), F32)
        for h in range(heads):
            mask = head_mask((count, block), h)
            qh = jnp.where(mask, q, jnp.zeros_like(q))
            dmh = jnp.where(mask, dm, jnp.zeros_like(dm))
            score = dot(qh, b.kk[...], NT) * 0.125 + bias
            prob = jnp.exp(score - lse[:, h : h + 1])
            dprob = dot(dmh, b.v[...], NT)
            centre = jnp.sum(prob * dprob, axis=1, keepdims=True)
            ds = (0.125 * prob * (dprob - centre)).astype(BF)
            grad_q = jnp.where(mask, dot(ds, b.kk[...], NN), grad_q)
            b.dk[...] += dot(ds, qh, TN)
            b.dv[...] += dot(prob.astype(BF), dmh, TN)
        cosine = jnp.concatenate([b.cos[rows, :]] * (block // LANES), axis=1)
        sine = jnp.concatenate([b.sin[rows, :]] * (block // LANES), axis=1)
        b.act[0, rows, 0:block] = (grad_q * cosine - swap_halves(grad_q) * sine).astype(BF)

        @pl.when(i == 0)
        def _():
            og_sum()

        return carry

    lax.fori_loop(0, seq, attend_back, 0)

    def back_chunk(i):
        rows = pl.ds(tall(i * count, count), count)
        cosine = jnp.concatenate([b.cos[rows, :]] * (block // LANES), axis=1)
        sine = jnp.concatenate([b.sin[rows, :]] * (block // LANES), axis=1)
        grad_k = b.dk[rows, :]
        dk = (grad_k * cosine - swap_halves(grad_k) * sine).astype(BF)
        dv = b.dv[rows, :].astype(BF)
        b.act[1, rows, 0:block] = dk
        b.act[2, rows, 0:block] = dv
        value = dot(b.act[0, rows, 0:block], b.wq_full[0], NT)
        value = value + dot(dk, b.wq_full[1], NT) + dot(dv, b.wq_full[2], NT)
        at = lax.rem(i, 2) * me.half + i // 2
        b.xall[at // 2, lax.rem(at, 2)] = value.astype(BF)

    def other_half(j, carry):
        back_chunk(2 * j + 1 - me.k)
        return carry

    def own_half_chunks(j, carry):
        back_chunk(2 * j + me.k)
        return carry

    lax.fori_loop(0, me.half, other_half, 0)
    quarter = me.half // 2
    dn_other = b.xall.at[pl.ds((1 - me.k) * quarter, quarter)]
    remote(dn_other, b.dnsib, b.n1.at[0], b.n1.at[1], sib).start()
    lax.fori_loop(0, me.half, own_half_chunks, 0)
    remote(b.dnsib, b.dnsib, b.n1.at[0], b.n1.at[1], sib).wait()
    for j in range(me.half):
        value = b.xall[me.k * quarter + j // 2, j % 2].astype(F32)
        b.dpart[0, j] = (value + b.dnsib[j // 2, j % 2].astype(F32)).astype(BF)
        i = 2 * j + me.k
        here = jnp.logical_and(owner == me.d, i == me.s)
        send_or_keep(
            here, b.dpart.at[0, j], b.dnr.at[me.h], b.n2s.at[j], b.n2r.at[me.h], (owner, i)
        )
        last.append(functools.partial(sent, here, b.dpart.at[0, j], b.n2s.at[j], sib))
    span_rows = 2 * cr
    per_tile = block // span_rows

    def qkv_terms(j, carry):
        at = lax.rem(me.c // per_tile + j, width // block)
        x = b.xrow[:, pl.ds(tall(at * block, block), block)]
        rows = pl.ds(tall(total + at * block, block), block)
        for t in range(3):
            b.act[t, rows, 0:block] = dot(x, b.act[t, 0:total, 0:block], TN).astype(BF)
        for i in range(per_tile):
            chip = at * per_tile + i

            @pl.when(chip != me.c)
            def _(chip=chip):
                src = b.act.at[:, pl.ds(tall(total + chip * span_rows, span_rows), span_rows), 0:block]
                to = (2 * chip + me.k, me.s)
                remote(src, b.qgpl.at[me.c], b.q1s.at[chip], b.q1r.at[me.c], to).start()

        return carry

    lax.fori_loop(1, width // block, qkv_terms, 0)
    qkv_terms(0, 0)
    og_column()
    tok = local(b.tok, b.norm, b.load.at[0])
    tok.start()
    tok.wait()
    for h in range(me.half):
        arrived(b.dnr.at[h], b.n2r.at[h])

    def first_back(rows):
        grad = b.dnr[0, rows, :].astype(F32)
        for h in range(1, me.half):
            grad = grad + b.dnr[h, rows, :].astype(F32)
        normal, scale = normalise(b.norm[rows, :])
        b.ig[rows, :] += norm_back(grad, normal, scale, b.gain[0:1, :])
        add_ln(0, jnp.sum(grad * normal, axis=0, keepdims=True))
        add_ln(1, jnp.sum(grad, axis=0, keepdims=True))

    by_rows(first_back)
    store(1)

    def send_lnp(j, carry):
        other = lax.rem(me.n + j, me.total)
        remote(
            b.lnp.at[other // per], b.lnr.at[me.n], b.lnt.at[0], b.lnt.at[1], me.of_rank(other)
        ).start()
        return carry

    lax.fori_loop(1, me.total, send_lnp, 0)
    b.lnr[me.n] = b.lnp[me.n // per]
    own = pl.ds(tall(total + me.c * span_rows, span_rows), span_rows)
    sums = [b.act[t, own, 0:block].astype(F32) for t in range(3)]
    for j in range(1, me.chips):
        chip = lax.rem(me.c + j, me.chips)
        part = b.qgpl.at[chip]
        remote(part, part, b.q1s.at[chip], b.q1r.at[chip], sib).wait()
        for t in range(3):
            sums[t] = sums[t] + b.qgpl[chip, t].astype(F32)
    for t in range(3):
        b.qgc[t] = sums[t].astype(BF)
    source = me.k * seq + me.s
    for core in range(2):
        for j in range(seq):
            to = lax.rem(me.s + j, seq)
            src = b.qgc.at[:, pl.ds(tall((core * seq + to) * wr, wr), wr), :]
            here = jnp.logical_and(core == me.k, to == me.s)
            send_or_keep(
                here, src, b.qgz.at[source], b.q2s.at[core, j], b.q2r.at[source], (2 * me.c + core, to)
            )
            last.append(functools.partial(sent, here, src, b.q2s.at[core, j], sib))
    value = b.out[...] + b.xown[...].astype(F32)
    for j in range(1, nc):
        remote(b.brr.at[j - 1], b.brr.at[j - 1], b.brs.at[j], b.brr_sem.at[j], sib).wait()
        value = value + b.brr[j - 1].astype(F32)
    b.out[...] = value
    store(0)
    acc = b.ogc[pl.ds(tall(me.s * wr, wr), wr), :].astype(F32)
    for j in range(1, seq):
        remote(b.ogz.at[j], b.ogz.at[j], b.o3s.at[j], b.o3r.at[j], sib).wait()
        acc = acc + b.ogz[j].astype(F32)
    b.og[...] = acc
    store(4)
    for m in range(3):
        for j in range(1, 3):
            arrived(b.rs.at[j, m], b.gr.at[j, m])
        for j in range(3):
            last.append(functools.partial(sent, False, b.rs.at[0, 0], b.gs.at[j, m], sib))
        acc = bg[m][band_rows(me.s), :].astype(F32)
        acc = acc + b.rs[1, m].astype(F32) + b.rs[2, m].astype(F32)
        if me.groups == 1:
            b.fg[m] = acc
        else:
            bg[m][band_rows(me.s), :] = acc.astype(BF)
    if me.groups > 1:
        for m in range(3):
            for j in range(1, me.groups):
                other = lax.rem(me.g + j, me.groups)
                src = bg[m].at[pl.ds(tall(me.s * band + other * units, units), units), :]
                to = (other * me.group + me.p, me.s)
                remote(src, b.grp.at[j, m], b.grs.at[j, m], b.grr.at[j, m], to).start()
        for m in range(3):
            acc = bg[m][pl.ds(tall(me.s * band + me.g * units, units), units), :].astype(F32)
            for j in range(1, me.groups):
                part = b.grp.at[j, m]
                remote(part, part, b.grs.at[j, m], b.grr.at[j, m], sib).wait()
                acc = acc + b.grp[j, m].astype(F32)
            b.fg[m] = acc
    store(5)
    rest = b.lnr.at[pl.ds(0, me.total - 1)]
    remote(rest, rest, b.lnt.at[0], b.lnt.at[1], sib).wait()
    acc = b.lnr[0]
    for j in range(1, me.total):
        acc = acc + b.lnr[j]
    for i in range(fit):

        @pl.when(lax.rem(me.n, fit) == i)
        def _(i=i):
            b.lng[...] = acc[0:4, i * share : (i + 1) * share]

    store(2)
    for j in range(2 * seq):
        arrived(b.qgz.at[j], b.q2r.at[j])
    for hg in range(seq):
        core, h = hg % 2, hg // 2
        acc = b.qgz[core * seq + h].astype(F32) + b.qgz[core * seq + me.half + h].astype(F32)
        b.qg[:, :, hg * block : (hg + 1) * block] = acc
    store(3)
    for copy in last:
        copy()
    for copy in stores:
        copy.wait()


def keep_kernel(count, *refs):
    given, kept, held = refs[:count], refs[count : 2 * count], refs[2 * count : 3 * count]
    sems = refs[-1]
    ins = [local(given[i], held[i], sems.at[0, i]) for i in range(count)]
    outs = [local(held[i], kept[i], sems.at[1, i]) for i in range(count)]
    for copy in ins:
        copy.start()
    for i in range(count):
        ins[i].wait()
        outs[i].start()
    for copy in outs:
        copy.wait()


def body(dp, seq, tokens, ln_params, qkv_weight, out_weight, ffn_weight, lengths, cotangent):
    count, width = tokens.shape[1], tokens.shape[2]
    ranks = dp * seq
    total = count * seq
    wr = qkv_weight.shape[0]
    cr = wr * seq
    units = ffn_weight.shape[0]
    block = width // seq
    half = seq // 2
    group = min(dp, GROUP)
    groups = dp // group
    gchips, chips, slots = group // 2, dp // 2, groups * seq
    held = units * slots
    share = ln_params.shape[1]
    sem = pltpu.SemaphoreType.DMA
    vm = pltpu.VMEM
    anywhere = pl.BlockSpec(memory_space=pl.ANY)
    vmem = pl.BlockSpec(memory_space=pltpu.VMEM)
    operands = dict(
        tok=(tokens.reshape(count, width), anywhere),
        ln=(ln_params, vmem),
        wq=(qkv_weight.transpose(1, 0, 2), anywhere),
        wo=(out_weight, anywhere),
        wf=(ffn_weight.transpose(1, 0, 2), anywhere),
        lens=(lengths, vmem),
        cot=(cotangent.reshape(count, width), anywhere),
    )
    outs = dict(
        out=(count, width),
        ig=(count, width),
        lng=(4, share),
        qg=(3, wr, width),
        og=(wr, width),
        fg=(3, units, width),
    )
    scratch = dict(
        **{name: vm(dims, F32) for name, dims in outs.items()},
        norm=vm((count, width), F32),
        scale=vm((count, LANES), F32),
        lens_own=vm((8, LANES), jnp.int32),
        lens_pair=vm((2, 8, LANES), jnp.int32),
        ln_own=vm((8, LANES), F32),
        ln_all=vm((ranks, 8, LANES), F32),
        gain=vm((8, width), F32),
        wq_own=vm((3, wr, width), BF),
        wcol=vm((3, cr, 2 * block), BF),
        xown=vm((count, width), BF),
        dmb=vm((count, width), BF),
        xrow=vm((total, width), BF),
        wq_full=vm((3, width, block), BF),
        wo_full=vm((width, width), BF),
        dyb=vm((group, count, width), BF),
        q=vm((total, block), BF),
        kk=vm((total, block), BF),
        v=vm((total, block), BF),
        lse=vm((total, LANES), F32),
        cos=vm((total, LANES), F32),
        sin=vm((total, LANES), F32),
        seg_row=vm((8, total), F32),
        mixed=vm((seq, count, block), BF),
        mixed_in=vm((seq, count, block), BF),
        dmix_row=vm((seq, count, block), BF),
        wf_full=vm((3, held, width), BF),
        xall=vm((gchips, 2, count, width), BF),
        act=vm((3, group * count, held), BF),
        dpart=vm((2, 2, count, width), BF),
        dsib=vm((gchips, count, width), BF),
        dsum=vm((gchips, count, width), BF),
        drecv=vm((gchips - 1, count, width), BF),
        brr=vm((gchips - 1, count, width), BF),
        ogsib=vm((width // 2 // count, count, width), BF),
        ogpl=vm((chips, cr, width), BF),
        ogc=vm((cr, width), BF),
        ogz=vm((seq, wr, width), BF),
        dk=vm((total, block), F32),
        dv=vm((total, block), F32),
        dnsib=vm((half // 2, 2, count, width), BF),
        dnr=vm((half, count, width), BF),
        qgpl=vm((chips, 3, 2 * cr, block), BF),
        qgc=vm((3, 2 * cr, block), BF),
        qgz=vm((2 * seq, 3, wr, block), BF),
        rs=vm((3, 3, groups * units, width), BF),
        grp=vm((groups, 3, units, width) if groups > 1 else (8, LANES), BF),
        down=vm((held, width), BF),
        lnp=vm((width // LANES, 8, LANES), F32),
        lnr=vm((ranks, 8, LANES), F32),
        load=sem((7,)),
        keep=sem((6,)),
        lns=sem((2,)),
        lens_sem=sem((2,)),
        wq1s=sem((seq,)),
        wq1r=sem((seq,)),
        wq2s=sem((dp,)),
        wq2r=sem((dp,)),
        wo1s=sem((seq,)),
        wo1r=sem((seq,)),
        wo2s=sem((chips,)),
        wo2r=sem((chips,)),
        wo3s=sem((chips,)),
        wo3r=sem((chips,)),
        xs=sem((half, 2)),
        xr=sem((seq,)),
        xfs=sem((seq,)),
        xfr=sem((seq,)),
        dys=sem((gchips,)),
        dyr=sem((gchips,)),
        dyfs=sem((gchips,)),
        dyfr=sem((gchips,)),
        fgs=sem((groups,)),
        fgr_sem=sem((groups,)),
        hs=sem((3, 3)),
        hr=sem((3, 3)),
        ms=sem((seq,)),
        mr=sem((seq,)),
        xs2=sem((gchips,)),
        xr2=sem((gchips,)),
        xfs2=sem((gchips,)),
        xfr2=sem((gchips,)),
        dss=sem((gchips,)),
        dsr=sem((gchips,)),
        dps=sem((gchips,)),
        dpr=sem((gchips,)),
        bss=sem((gchips,)),
        bsr=sem((gchips,)),
        brs=sem((gchips,)),
        brr_sem=sem((gchips,)),
        dms=sem((seq,)),
        dmr=sem((seq,)),
        gs=sem((3, 3)),
        gr=sem((3, 3)),
        grs=sem((groups, 3)),
        grr=sem((groups, 3)),
        o1=sem((2,)),
        o2s=sem((chips,)),
        o2r=sem((chips,)),
        o3s=sem((seq,)),
        o3r=sem((seq,)),
        n1=sem((2,)),
        n2s=sem((half,)),
        n2r=sem((half,)),
        q1s=sem((chips,)),
        q1r=sem((chips,)),
        q2s=sem((2, seq)),
        q2r=sem((2 * seq,)),
        lnt=sem((2,)),
    )
    names = (*operands, *[name + "_out" for name in outs], *scratch)
    results = pl.pallas_call(
        functools.partial(layer_kernel, names, dp, seq, lengths.shape[1]),
        out_shape=tuple(jax.ShapeDtypeStruct(dims, F32) for dims in outs.values()),
        in_specs=[spec for _, spec in operands.values()],
        out_specs=tuple([anywhere] * len(outs)),
        scratch_shapes=list(scratch.values()),
        compiler_params=pltpu.CompilerParams(
            collective_id=1, has_side_effects=True, vmem_limit_bytes=VMEM_BYTES
        ),
        cost_estimate=pl.CostEstimate(
            flops=32 * 10**9, bytes_accessed=2**24, transcendentals=10**7
        ),
        name="layer",
    )(*[value for value, _ in operands.values()])
    out, input_grad, ln_grad, qg, og, fg = pl.pallas_call(
        functools.partial(keep_kernel, len(outs)),
        out_shape=tuple(jax.ShapeDtypeStruct(dims, F32) for dims in outs.values()),
        in_specs=[anywhere] * len(outs),
        out_specs=tuple([anywhere] * len(outs)),
        scratch_shapes=[*[vm(dims, F32) for dims in outs.values()], sem((2, len(outs)))],
        name="keep",
    )(*results)
    return (
        out.reshape(1, count, width),
        input_grad.reshape(1, count, width),
        ln_grad,
        qg.transpose(1, 0, 2),
        og,
        fg.transpose(1, 0, 2),
    )


def solution(mesh):
    dp, seq = mesh.shape["dp"], mesh.shape["seq"]
    both = ("dp", "seq")
    in_specs = (
        P("dp", "seq", None),
        P(None, both),
        P(both, None, None),
        P(both, None),
        P(both, None, None),
        P("dp", None),
        P("dp", "seq", None),
    )
    out_specs = (
        P("dp", "seq", None),
        P("dp", "seq", None),
        P(None, both),
        P(both, None, None),
        P(both, None),
        P(both, None, None),
    )
    return jax.shard_map(
        functools.partial(body, dp, seq),
        mesh=mesh,
        in_specs=in_specs,
        out_specs=out_specs,
        check_vma=False,
    )
```

```python
import functools
import math
import types

import jax
import jax.numpy as jnp
from jax import lax
from jax.experimental import pallas as pl
from jax.experimental.pallas import tpu as pltpu
from jax.sharding import PartitionSpec as P

HEAD_DIM = 64
GROUP = 8
LANES = 128
BF = jnp.bfloat16
F32 = jnp.float32
MESH = pl.DeviceIdType.MESH
NT = (((1,), (1,)), ((), ()))
NN = (((1,), (0,)), ((), ()))
TN = (((0,), (0,)), ((), ()))
EPS = 1e-05
VMEM_BYTES = 62 * 2**20


def dot(a, b, dims):
    return lax.dot_general(a, b, dims, preferred_element_type=F32)


def remote(src, dst, send, recv, device):
    return pltpu.make_async_remote_copy(
        src_ref=src, dst_ref=dst, send_sem=send, recv_sem=recv, device_id=device, device_id_type=MESH
    )


def local(src, dst, sem):
    return pltpu.make_async_copy(src, dst, sem)


class Place:
    def __init__(self, dp, seq):
        self.dp, self.seq = dp, seq
        self.d, self.s = lax.axis_index("dp"), lax.axis_index("seq")
        self.c, self.k = self.d // 2, lax.rem(self.d, 2)
        self.sib = self.d + 1 - 2 * self.k
        self.chips = dp // 2
        self.group = min(dp, GROUP)
        self.groups = dp // self.group
        self.g, self.p = self.d // self.group, lax.rem(self.d, self.group)
        self.gc = self.p // 2
        self.gchips = self.group // 2
        self.half = seq // 2
        self.r, self.h = self.s // self.half, lax.rem(self.s, self.half)
        self.hg = 2 * self.h + self.k
        self.n = self.d * seq + self.s
        self.total = dp * seq

    def of_rank(self, rank):
        return (rank // self.seq, lax.rem(rank, self.seq))

    def in_group(self, chip, core):
        return self.g * self.group + 2 * chip + core


def normalise(value):
    mean = jnp.mean(value, axis=-1, keepdims=True)
    centred = value - mean
    var = jnp.mean(centred * centred, axis=-1, keepdims=True)
    scale = lax.rsqrt(var + EPS)
    return centred * scale, scale


def norm_back(grad, normal, scale, gain):
    scaled = grad * gain
    return scale * (
        scaled
        - jnp.mean(scaled, axis=-1, keepdims=True)
        - normal * jnp.mean(scaled * normal, axis=-1, keepdims=True)
    )


def swap_halves(value):
    half = HEAD_DIM // 2
    width = value.shape[1]
    lane = lax.broadcasted_iota(jnp.int32, value.shape, 1)
    up = pltpu.roll(value, width - half, 1)
    down = pltpu.roll(value, half, 1)
    return jnp.where(lax.rem(lane, HEAD_DIM) < half, up, down)


def head_mask(shape, h):
    lane = lax.broadcasted_iota(jnp.int32, shape, 1)
    return jnp.logical_and(lane >= h * HEAD_DIM, lane < (h + 1) * HEAD_DIM)


def tall(value, rows):
    return pl.multiple_of(value, rows)


def meet(me):
    barrier = pltpu.get_barrier_semaphore()

    def hello(j, carry):
        other = lax.rem(me.n + j, me.total)
        pl.semaphore_signal(barrier, inc=1, device_id=me.of_rank(other), device_id_type=MESH)
        return carry

    lax.fori_loop(1, me.total, hello, 0)


def met(me):
    pl.semaphore_wait(pltpu.get_barrier_semaphore(), me.total - 1)


def send_or_keep(here, src, dst, send, recv, device):
    @pl.when(jnp.logical_not(here))
    def _():
        remote(src, dst, send, recv, device).start()

    @pl.when(here)
    def _():
        local(src, dst, recv).start()


def sent(here, src, send, device):
    @pl.when(jnp.logical_not(here))
    def _():
        remote(src, src, send, send, device).wait_send()


def arrived(dst, recv):
    local(dst, dst, recv).wait()


def layer_kernel(names, dp, seq, segs, *refs):
    b = types.SimpleNamespace(**dict(zip(names, refs)))
    me = Place(dp, seq)
    count, width = b.out.shape
    total = count * seq
    wr = b.og.shape[0]
    cr = wr * seq
    block = b.q.shape[1]
    heads = block // HEAD_DIM
    units = b.fg.shape[1]
    held = b.wf_full.shape[1]
    band = me.groups * units
    nc = me.gchips
    sib = (me.sib, me.s)
    share = b.ln.shape[1]
    fit = LANES // share
    tiles = width // LANES
    per = me.total // tiles
    halfrows = count // 2
    last = []

    def by_rows(step):
        def one(i, carry):
            step(pl.ds(tall(i * some, some), some))
            return carry

        lax.fori_loop(0, count // some, one, 0)

    some = 64
    results = ("out", "ig", "lng", "qg", "og", "fg")
    stores = []

    def store(i):
        name = results[i]
        stores.append(local(getattr(b, name), getattr(b, name + "_out"), b.keep.at[i]))
        stores[-1].start()

    meet(me)
    loads = [
        local(b.tok, b.out, b.load.at[0]),
        local(b.wq, b.qg, b.load.at[1]),
        local(b.wo, b.og, b.load.at[2]),
        local(b.wf, b.fg, b.load.at[3]),
        local(b.cot, b.ig, b.load.at[4]),
    ]
    for copy in loads:
        copy.start()
    b.lens_own[...] = jnp.zeros_like(b.lens_own)
    b.lens_own[0:1, 0:segs] = b.lens[...]
    b.lens_pair[me.k] = b.lens_own[...]
    gains = jnp.concatenate([b.ln[...].astype(BF).astype(F32)] * fit, axis=1)
    lane = lax.broadcasted_iota(jnp.int32, gains.shape, 1)
    b.ln_own[...] = jnp.zeros_like(b.ln_own)
    b.ln_own[0:4, :] = jnp.where(lane // share == lax.rem(me.n, fit), gains, 0.0)
    b.ln_all[me.n] = b.ln_own[...]
    loads[1].wait()
    b.wq_own[...] = b.qg[...].astype(BF)
    loads[0].wait()

    def first_norm(rows):
        b.norm[rows, :] = normalise(b.out[rows, :])[0]

    by_rows(first_norm)
    met(me)

    def send_ln(j, carry):
        other = lax.rem(me.n + j, me.total)
        remote(
            b.ln_own, b.ln_all.at[me.n], b.lns.at[0], b.lns.at[1], me.of_rank(other)
        ).start()
        return carry

    lax.fori_loop(1, me.total, send_ln, 0)
    len_copy = remote(b.lens_own, b.lens_pair.at[me.k], b.lens_sem.at[0], b.lens_sem.at[1], sib)
    len_copy.start()
    pair = 2 * block
    row0 = tall(me.s * wr, wr)
    out0 = tall(me.n * wr, wr)
    wq_first = []
    for j in range(1, seq):
        to = lax.rem(me.s + j, seq)
        col = tall(lax.rem(to, me.half) * pair, pair)
        wq_first.append(
            remote(
                b.wq_own.at[:, :, pl.ds(col, pair)],
                b.wcol.at[:, pl.ds(row0, wr), :],
                b.wq1s.at[j],
                b.wq1r.at[j],
                (me.d, to),
            )
        )
    for copy in wq_first:
        copy.start()
    own_wq = local(
        b.wq_own.at[:, :, pl.ds(tall(me.h * pair, pair), pair)],
        b.wcol.at[:, pl.ds(row0, wr), :],
        b.load.at[5],
    )
    own_wq.start()
    loads[2].wait()
    b.wo_full[pl.ds(out0, wr), :] = b.og[...].astype(BF)
    rest = b.ln_all.at[pl.ds(0, me.total - 1)]
    remote(rest, rest, b.lns.at[0], b.lns.at[1], sib).wait()
    for t in range(tiles):
        part = b.ln_all[t * per]
        for i in range(1, per):
            part = part + b.ln_all[t * per + i]
        b.gain[:, t * LANES : (t + 1) * LANES] = part

    def first_out(rows):
        b.xown[rows, :] = (b.norm[rows, :] * b.gain[0:1, :] + b.gain[1:2, :]).astype(BF)

    by_rows(first_out)
    rows0 = tall(me.s * count, count)
    for j in range(me.half):
        to = me.k * me.half + lax.rem(me.h + j, me.half)
        for core in range(2):
            src = b.xown.at[pl.ds(core * halfrows, halfrows), :]
            dst = b.xrow.at[pl.ds(rows0 + core * halfrows, halfrows), :]
            here = jnp.logical_and(to == me.s, core == me.k)
            send_or_keep(
                here, src, dst, b.xs.at[j, core], b.xr.at[me.s], (2 * me.c + core, to)
            )
            last.append(
                functools.partial(sent, here, src, b.xs.at[j, core], (2 * me.c + core, to))
            )
    for copy in wq_first:
        copy.wait()
    own_wq.wait()
    crow0 = tall(me.d * cr, cr)

    def send_wq(j, carry):
        to = lax.rem(me.d + j, dp)
        remote(
            b.wcol.at[:, :, pl.ds(tall(lax.rem(to, 2) * block, block), block)],
            b.wq_full.at[:, pl.ds(crow0, cr), :],
            b.wq2s.at[j],
            b.wq2r.at[j],
            (to, me.s),
        ).start()
        return carry

    lax.fori_loop(1, dp, send_wq, 0)
    own_half = local(
        b.wcol.at[:, :, pl.ds(tall(me.k * block, block), block)],
        b.wq_full.at[:, pl.ds(crow0, cr), :],
        b.load.at[6],
    )
    own_half.start()
    len_copy.wait()
    row = b.lens_pair[me.r]
    place_row = lax.broadcasted_iota(jnp.int32, (8, total), 1)
    ends = [row[0:1, 0:1]]
    for j in range(1, segs):
        ends.append(ends[-1] + row[0:1, j : j + 1])
    segr = jnp.zeros((8, total), jnp.int32)
    for end in ends:
        segr = segr + (place_row >= end).astype(jnp.int32)
    b.seg_row[...] = segr.astype(F32)
    half = HEAD_DIM // 2
    lane = lax.broadcasted_iota(jnp.int32, (1, LANES), 1)
    rate = jnp.exp(lax.rem(lane, half).astype(F32) * (-math.log(10000.0) / half))
    sign = jnp.where(lax.rem(lane, HEAD_DIM) < half, -1.0, 1.0)

    def angles(i, carry):
        rows = pl.ds(tall(i * LANES, LANES), LANES)
        place = lax.broadcasted_iota(jnp.int32, (LANES, LANES), 0) + i * LANES
        segment = jnp.zeros((LANES, LANES), jnp.int32)
        begin = jnp.zeros((LANES, LANES), jnp.int32)
        for end in ends:
            past = place >= end
            segment = segment + past.astype(jnp.int32)
            begin = jnp.where(past, end, begin)
        b.lse[rows, :] = segment.astype(F32)
        angle = (place - begin).astype(F32) * rate
        b.cos[rows, :] = jnp.cos(angle)
        b.sin[rows, :] = jnp.sin(angle) * sign
        return carry

    lax.fori_loop(0, total // LANES, angles, 0)
    loads[4].wait()
    b.dyb[me.p] = b.ig[...].astype(BF)
    loads[3].wait()
    own_units = pl.ds(tall(me.s * band + me.g * units, units), units)
    b.wf_full[:, own_units, :] = b.fg[...].astype(BF)
    for j in range(seq):
        source = lax.rem(me.s + j, seq)
        part = b.xrow.at[pl.ds(tall(source * count + me.k * halfrows, halfrows), halfrows), :]
        arrived(part, b.xr.at[source])
        remote(part, part, b.xfs.at[j], b.xfr.at[j], sib).start()
    wo_own = b.wo_full.at[pl.ds(out0, wr), :]
    wo_first = []
    for j in range(1, seq):
        to = (me.d, lax.rem(me.s + j, seq))
        wo_first.append(remote(wo_own, wo_own, b.wo1s.at[j], b.wo1r.at[j], to))
    for copy in wo_first:
        copy.start()
    for j in range(1, me.groups):
        other = lax.rem(me.g + j, me.groups)
        mine = b.wf_full.at[:, own_units, :]
        remote(
            mine, mine, b.fgs.at[j], b.fgr_sem.at[j], (other * me.group + me.p, me.s)
        ).start()
    for j in range(1, me.groups):
        mine = b.wf_full.at[:, own_units, :]
        remote(mine, mine, b.fgs.at[j], b.fgr_sem.at[j], sib).wait()

    near, far = me.s + 1 - 2 * lax.rem(me.s, 2), lax.rem(me.s + 2, seq)
    beyond = lax.rem(near + 2, seq)

    def column(m, at):
        return b.wf_full.at[m, pl.ds(tall(at * band, band), band), :]

    def unit_copy(way, m):
        part = column(m, far if way == 2 else me.s)
        to = (me.d, near if way else far)
        return remote(part, part, b.hs.at[way, m], b.hr.at[way, m], to)

    def send_units(m):
        unit_copy(0, m).start()
        unit_copy(1, m).start()

    def pass_units(m):
        arrived(column(m, far), b.hr.at[0, m])
        unit_copy(2, m).start()

    for j in range(seq):
        part = b.xrow.at[pl.ds(0, halfrows), :]
        arrived(part, b.xfr.at[j])
        last.append(functools.partial(sent, False, part, b.xfs.at[j], sib))

    def wait_wq(j, carry):
        part = b.wq_full.at[:, pl.ds(0, cr), :]
        remote(part, part, b.wq2s.at[j], b.wq2r.at[j], sib).wait()
        return carry

    lax.fori_loop(1, dp, wait_wq, 0)
    own_half.wait()
    def project(i, carry):
        rows = pl.ds(tall(i * count, count), count)
        x = b.xrow[rows, :]
        cosine = jnp.concatenate([b.cos[rows, :]] * (block // LANES), axis=1)
        sine = jnp.concatenate([b.sin[rows, :]] * (block // LANES), axis=1)
        raw = dot(x, b.wq_full[0], NN)
        b.q[rows, :] = (raw * cosine + swap_halves(raw) * sine).astype(BF)
        raw = dot(x, b.wq_full[1], NN)
        b.kk[rows, :] = (raw * cosine + swap_halves(raw) * sine).astype(BF)
        b.v[rows, :] = dot(x, b.wq_full[2], NN).astype(BF)
        return carry

    lax.fori_loop(0, seq, project, 0)
    owner = 2 * me.c + me.r
    mine = b.wo_full.at[pl.ds(crow0, cr), :]
    for copy in wo_first:
        copy.wait()
    remote(mine, mine, b.wo3s.at[0], b.wo3r.at[0], sib).start()
    for j in range(1, me.chips):
        to = 2 * lax.rem(me.c + j, me.chips) + me.k
        remote(mine, mine, b.wo2s.at[j], b.wo2r.at[j], (to, me.s)).start()
    dy_own = b.dyb.at[me.p]
    remote(dy_own, dy_own, b.dyfs.at[0], b.dyfr.at[0], sib).start()
    for j in range(1, nc):
        to = me.in_group(lax.rem(me.gc + j, nc), me.k)
        remote(dy_own, dy_own, b.dys.at[j], b.dyr.at[j], (to, me.s)).start()

    def attend(step, carry):
        i = lax.rem(me.s + step, seq)
        rows = pl.ds(tall(i * count, count), count)
        q = b.q[rows, :]
        segment = b.lse[rows, LANES - 1 : LANES]
        bias = jnp.where(segment == b.seg_row[0:1, :], 0.0, -1e30)
        lane = lax.broadcasted_iota(jnp.int32, (count, LANES), 1)
        lse = b.lse[rows, :]
        out = jnp.zeros((count, block), F32)
        for h in range(heads):
            mask = head_mask((count, block), h)
            score = dot(jnp.where(mask, q, jnp.zeros_like(q)), b.kk[...], NT) * 0.125 + bias
            top = jnp.max(score, axis=1, keepdims=True)
            weight = jnp.exp(score - top)
            tally = jnp.sum(weight, axis=1, keepdims=True)
            prob = (weight * (1.0 / tally)).astype(BF)
            out = jnp.where(mask, dot(prob, b.v[...], NN), out)
            lse = jnp.where(lane == h, top + jnp.log(tally), lse)
        b.lse[rows, :] = lse
        b.mixed[i] = out.astype(BF)
        here = jnp.logical_and(i == me.s, owner == me.d)
        send_or_keep(
            here, b.mixed.at[i], b.mixed_in.at[me.hg], b.ms.at[i], b.mr.at[me.hg], (owner, i)
        )

        return carry

    lax.fori_loop(0, seq, attend, 0)
    for m in range(3):
        send_units(m)
    for j in range(1, me.chips):
        source = 2 * lax.rem(me.c + me.chips - j, me.chips) + me.k
        part = b.wo_full.at[pl.ds(tall(source * cr, cr), cr), :]
        arrived(part, b.wo2r.at[j])
        remote(part, part, b.wo3s.at[j], b.wo3r.at[j], sib).start()
        last.append(functools.partial(sent, False, part, b.wo2s.at[j], sib))
        last.append(functools.partial(sent, False, part, b.wo3s.at[j], sib))
    last.append(functools.partial(sent, False, mine, b.wo3s.at[0], sib))
    for j in range(me.chips):
        arrived(mine, b.wo3r.at[j])
    for j in range(seq):
        arrived(b.mixed_in.at[j], b.mr.at[j])
    for t in range(width // block):
        span = slice(t * block, (t + 1) * block)
        part = b.out[:, span]
        for h in range(seq):
            part = part + dot(b.mixed_in[h], b.wo_full[h * block : (h + 1) * block, span], NN)
        b.out[:, span] = part

    def second_norm(rows):
        normal, scale = normalise(b.out[rows, :])
        b.norm[rows, :] = normal
        b.scale[rows, :] = jnp.broadcast_to(scale, (some, LANES))
        b.xall[me.gc, me.k, rows, :] = (normal * b.gain[2:3, :] + b.gain[3:4, :]).astype(BF)

    by_rows(second_norm)
    x_own = b.xall.at[me.gc, me.k]
    remote(x_own, x_own, b.xfs2.at[0], b.xfr2.at[0], sib).start()
    for j in range(1, nc):
        to = me.in_group(lax.rem(me.gc + j, nc), me.k)
        remote(x_own, x_own, b.xs2.at[j], b.xr2.at[j], (to, me.s)).start()
    pass_units(0)
    for j in range(1, nc):
        source = 2 * lax.rem(me.gc + nc - j, nc) + me.k
        part = b.dyb.at[source]
        arrived(part, b.dyr.at[j])
        remote(part, part, b.dyfs.at[j], b.dyfr.at[j], sib).start()
        last.append(functools.partial(sent, False, part, b.dys.at[j], sib))
        last.append(functools.partial(sent, False, part, b.dyfs.at[j], sib))
    last.append(functools.partial(sent, False, dy_own, b.dyfs.at[0], sib))
    for j in range(nc):
        arrived(dy_own, b.dyfr.at[j])
    tile = 2 * band
    cols = 256
    near_tile = me.s // 2

    def chip_rows(j):
        cj = lax.rem(me.gc + nc - j, nc)
        return cj, pl.ds(tall(cj * 2 * count, 2 * count), 2 * count)

    def hidden(j, t):
        cj, rows = chip_rows(j)
        span = pl.ds(tall(t * tile, tile), tile)
        x = b.xall[cj].reshape(2 * count, width)
        dy = b.dyb[pl.ds(2 * cj, 2)].reshape(2 * count, width)
        gate = dot(x, b.wf_full[0, span, :], NT)
        up = dot(x, b.wf_full[1, span, :], NT)
        dh = dot(dy, b.wf_full[2, span, :], NT)
        sigma = 1.0 / (1.0 + jnp.exp(-gate))
        active = gate * sigma
        b.act[2, rows, span] = (active * up).astype(BF)
        b.act[0, rows, span] = (dh * up * (sigma * (1.0 + gate * (1.0 - sigma)))).astype(BF)
        b.act[1, rows, span] = (dh * active).astype(BF)

    def near_units(j, carry):
        cj, _ = chip_rows(j)

        @pl.when(j > 0)
        def _():
            part = b.xall.at[cj, me.k]
            arrived(part, b.xr2.at[j])
            remote(part, part, b.xfs2.at[j], b.xfr2.at[j], sib).start()

        @pl.when((j > 0) & (j < 3))
        def _():
            pass_units(j)

        arrived(b.xall.at[cj, 1 - me.k], b.xfr2.at[j])
        hidden(j, near_tile)
        return carry

    def far_units(j, carry):
        hidden(j, 1 - near_tile)
        return carry

    for m in range(3):
        arrived(column(m, near), b.hr.at[1, m])
    lax.fori_loop(0, nc, near_units, 0)
    for m in range(3):
        arrived(column(m, beyond), b.hr.at[2, m])
    lax.fori_loop(0, nc, far_units, 0)

    def take_dn2(j):
        part = b.dsib.at[j]
        remote(part, part, b.dss.at[j], b.dsr.at[j], sib).wait()
        value = b.dpart[lax.rem(j, 2), me.k].astype(F32) + b.dsib[j].astype(F32)
        b.dsum[j] = value.astype(BF)

        @pl.when(j > 0)
        def _():
            to = (me.in_group(chip_rows(j)[0], me.k), me.s)
            remote(b.dsum.at[j], b.drecv.at[j - 1], b.dps.at[j], b.dpr.at[j], to).start()

    def grad_tokens(i, carry):
        j = nc - 1 - i
        _, rows = chip_rows(j)
        for t in range(width // cols):
            span = slice(t * cols, (t + 1) * cols)
            value = dot(b.act[0, rows, :], b.wf_full[0, :, span], NN)
            value = value + dot(b.act[1, rows, :], b.wf_full[1, :, span], NN)
            b.dpart[lax.rem(j, 2), :, :, span] = value.astype(BF).reshape(2, count, cols)
        part = b.dpart.at[lax.rem(j, 2), 1 - me.k]
        remote(part, b.dsib.at[j], b.dss.at[j], b.dsr.at[j], sib).start()

        @pl.when(i > 0)
        def _():
            take_dn2(j + 1)

        return carry

    lax.fori_loop(0, nc, grad_tokens, 0)
    take_dn2(0)
    for j in range(nc):
        last.append(functools.partial(sent, False, x_own, b.xfs2.at[j], sib))
        if j:
            last.append(functools.partial(sent, False, x_own, b.xs2.at[j], sib))
    for copy in last:
        copy()
    last.clear()
    for m in range(3):
        for way in range(3):
            unit_copy(way, m).wait_send()
    bg = (b.wf_full.at[0], b.wf_full.at[1], b.down)

    def grads(t, then):
        span = pl.ds(tall(t * tile, tile), tile)
        tokens = nc * 2 * count
        for m in range(3):
            left = b.act[m, :, span].T
            for c in range(width // cols):
                part = slice(c * cols, (c + 1) * cols)
                if m < 2:
                    right = b.xall[:, :, :, part].reshape(tokens, cols)
                else:
                    right = b.dyb[:, :, part].reshape(tokens, cols)
                bg[m][span, part] = dot(left, right, NN).astype(BF)
            then(m)

    def band_rows(at):
        return pl.ds(tall(at * band, band), band)

    def send_terms(stage, at, to, m):
        src = bg[m].at[band_rows(at), :]
        remote(src, b.rs.at[stage, m], b.gs.at[stage, m], b.gr.at[stage, m], (me.d, to)).start()

    def cross_terms(m):
        arrived(b.rs.at[0, m], b.gr.at[0, m])
        value = bg[m][band_rows(far), :].astype(F32) + b.rs[0, m].astype(F32)
        bg[m][band_rows(far), :] = value.astype(BF)
        send_terms(2, far, far, m)

    grads(1 - near_tile, lambda m: send_terms(0, beyond, near, m))
    grads(near_tile, lambda m: None)
    for j in range(1, nc):
        arrived(b.drecv.at[j - 1], b.dpr.at[j])

    def add_ln(row, value):
        for t in range(tiles):
            b.lnp[t, row : row + 1, :] += value[:, t * LANES : (t + 1) * LANES]

    b.lnp[...] = jnp.zeros_like(b.lnp)

    def second_back(rows):
        grad = b.dsum[0, rows, :].astype(F32)
        for j in range(1, nc):
            grad = grad + b.drecv[j - 1, rows, :].astype(F32)
        normal = b.norm[rows, :]
        add_ln(2, jnp.sum(grad * normal, axis=0, keepdims=True))
        add_ln(3, jnp.sum(grad, axis=0, keepdims=True))
        dmid = b.ig[rows, :] + norm_back(grad, normal, b.scale[rows, 0:1], b.gain[2:3, :])
        b.ig[rows, :] = dmid
        b.dmb[rows, :] = dmid.astype(BF)

    by_rows(second_back)
    dmb = b.dmb[...]
    for i in range(seq):
        here = jnp.logical_and(i == me.s, owner == me.d)
        sent(here, b.mixed.at[i], b.ms.at[i], sib)
    for hg in range(seq):
        b.mixed[hg] = dot(dmb, b.wo_full[hg * block : (hg + 1) * block, :], NT).astype(BF)
        to = (2 * me.c + hg % 2, me.k * me.half + hg // 2)
        here = jnp.logical_and(to[0] == me.d, to[1] == me.s)
        send_or_keep(
            here, b.mixed.at[hg], b.dmix_row.at[me.s], b.dms.at[hg], b.dmr.at[me.s], to
        )
        last.append(functools.partial(sent, here, b.mixed.at[hg], b.dms.at[hg], sib))
    pieces = width // 2 // count

    def og_rows(parity):
        return b.dyb.at[pl.ds(parity * pieces, pieces)]

    for h in range(seq):
        part = dot(b.mixed_in[h], dmb, TN).astype(BF)
        for t in range(block // cr):
            first = h * (block // cr) + t
            row = (first // 2) * cr
            b.dyb[(first % 2) * pieces + row // count, row % count : row % count + cr, :] = part[
                t * cr : (t + 1) * cr
            ]
    remote(og_rows(1 - me.k), b.ogsib, b.o1.at[0], b.o1.at[1], sib).start()
    def add_branch(j):
        arrived(b.dsib.at[j], b.bsr.at[j])
        value = b.dpart[lax.rem(j, 2), me.k].astype(F32) + b.dsib[j].astype(F32)
        value = value.astype(BF)

        @pl.when(j == 0)
        def _():
            b.xown[...] = value

        @pl.when(j > 0)
        def _():
            remote(b.dsum.at[j], b.drecv.at[j - 1], b.dps.at[j], b.dpr.at[j], sib).wait_send()
            b.dsum[j] = value
            cj = lax.rem(me.gc + nc - j, nc)
            to = (me.in_group(cj, me.k), me.s)
            remote(b.dsum.at[j], b.brr.at[j - 1], b.brs.at[j], b.brr_sem.at[j], to).start()

    def branch(i, carry):
        j = nc - 1 - i
        _, rows = chip_rows(j)

        @pl.when(i > 1)
        def _():
            sent(False, b.dpart.at[0, 0], b.bss.at[j + 2], sib)

        for t in range(width // cols):
            span = slice(t * cols, (t + 1) * cols)
            value = dot(b.act[2, rows, :], b.wf_full[2, :, span], NN)
            b.dpart[lax.rem(j, 2), :, :, span] = value.astype(BF).reshape(2, count, cols)

        @pl.when(i > 0)
        def _():
            add_branch(j + 1)

        part = b.dpart.at[lax.rem(j, 2), 1 - me.k]
        remote(part, b.dsib.at[j], b.bss.at[j], b.bsr.at[j], sib).start()
        return carry

    lax.fori_loop(0, nc, branch, 0)

    add_branch(0)
    for j in range(min(2, nc)):
        sent(False, b.dpart.at[0, 0], b.bss.at[j], sib)
    for j in range(seq):
        arrived(b.dmix_row.at[j], b.dmr.at[j])
    for m in range(3):
        cross_terms(m)
    for m in range(3):
        send_terms(1, near, near, m)
    b.dk[...] = jnp.zeros_like(b.dk)
    b.dv[...] = jnp.zeros_like(b.dv)

    def og_sum():
        remote(b.ogsib, b.ogsib, b.o1.at[0], b.o1.at[1], sib).wait()
        for i in range(pieces):
            value = b.dyb[me.k * pieces + i].astype(F32) + b.ogsib[i].astype(F32)
            b.dyb[2 * pieces + i] = value.astype(BF)

        def send_og(j, carry):
            chip = lax.rem(me.c + j, me.chips)
            row = chip * cr
            src = b.dyb.at[2 * pieces + row // count, pl.ds(tall(lax.rem(row, count), cr), cr), :]
            remote(src, b.ogpl.at[j], b.o2s.at[j], b.o2r.at[j], (2 * chip + me.k, me.s)).start()
            return carry

        lax.fori_loop(1, me.chips, send_og, 0)

    def og_column():
        row = me.c * cr
        at = pl.ds(tall(lax.rem(row, count), cr), cr)
        acc = b.dyb[2 * pieces + row // count, at, :].astype(F32)
        for j in range(1, me.chips):
            remote(b.ogpl.at[j], b.ogpl.at[j], b.o2s.at[j], b.o2r.at[j], sib).wait()
            acc = acc + b.ogpl[j].astype(F32)
        b.ogc[...] = acc.astype(BF)
        for j in range(1, seq):
            to = lax.rem(me.s + j, seq)
            src = b.ogc.at[pl.ds(tall(to * wr, wr), wr), :]
            remote(src, b.ogz.at[j], b.o3s.at[j], b.o3r.at[j], (me.d, to)).start()

    def attend_back(i, carry):
        rows = pl.ds(tall(i * count, count), count)
        q = b.q[rows, :]
        dm = b.dmix_row[i]
        lse = b.lse[rows, :]
        segment = b.lse[rows, LANES - 1 : LANES]
        bias = jnp.where(segment == b.seg_row[0:1, :], 0.0, -1e30)
        grad_q = jnp.zeros((count, block), F32)
        for h in range(heads):
            mask = head_mask((count, block), h)
            qh = jnp.where(mask, q, jnp.zeros_like(q))
            dmh = jnp.where(mask, dm, jnp.zeros_like(dm))
            score = dot(qh, b.kk[...], NT) * 0.125 + bias
            prob = jnp.exp(score - lse[:, h : h + 1])
            dprob = dot(dmh, b.v[...], NT)
            centre = jnp.sum(prob * dprob, axis=1, keepdims=True)
            ds = (0.125 * prob * (dprob - centre)).astype(BF)
            grad_q = jnp.where(mask, dot(ds, b.kk[...], NN), grad_q)
            b.dk[...] += dot(ds, qh, TN)
            b.dv[...] += dot(prob.astype(BF), dmh, TN)
        cosine = jnp.concatenate([b.cos[rows, :]] * (block // LANES), axis=1)
        sine = jnp.concatenate([b.sin[rows, :]] * (block // LANES), axis=1)
        b.act[0, rows, 0:block] = (grad_q * cosine - swap_halves(grad_q) * sine).astype(BF)

        @pl.when(i == 0)
        def _():
            og_sum()

        return carry

    lax.fori_loop(0, seq, attend_back, 0)

    def back_chunk(i):
        rows = pl.ds(tall(i * count, count), count)
        cosine = jnp.concatenate([b.cos[rows, :]] * (block // LANES), axis=1)
        sine = jnp.concatenate([b.sin[rows, :]] * (block // LANES), axis=1)
        grad_k = b.dk[rows, :]
        dk = (grad_k * cosine - swap_halves(grad_k) * sine).astype(BF)
        dv = b.dv[rows, :].astype(BF)
        b.act[1, rows, 0:block] = dk
        b.act[2, rows, 0:block] = dv
        value = dot(b.act[0, rows, 0:block], b.wq_full[0], NT)
        value = value + dot(dk, b.wq_full[1], NT) + dot(dv, b.wq_full[2], NT)
        at = lax.rem(i, 2) * me.half + i // 2
        b.xall[at // 2, lax.rem(at, 2)] = value.astype(BF)

    def other_half(j, carry):
        back_chunk(2 * j + 1 - me.k)
        return carry

    lax.fori_loop(0, me.half, other_half, 0)
    quarter = me.half // 2
    dn_other = b.xall.at[pl.ds((1 - me.k) * quarter, quarter)]
    remote(dn_other, b.dnsib, b.n1.at[0], b.n1.at[1], sib).start()
    for j in range(me.half):
        back_chunk(2 * j + me.k)
        if j == 0:
            remote(b.dnsib, b.dnsib, b.n1.at[0], b.n1.at[1], sib).wait()
        value = b.xall[me.k * quarter + j // 2, j % 2].astype(F32)
        b.dpart[0, j] = (value + b.dnsib[j // 2, j % 2].astype(F32)).astype(BF)
        i = 2 * j + me.k
        here = jnp.logical_and(owner == me.d, i == me.s)
        send_or_keep(
            here, b.dpart.at[0, j], b.dnr.at[me.h], b.n2s.at[j], b.n2r.at[me.h], (owner, i)
        )
        last.append(functools.partial(sent, here, b.dpart.at[0, j], b.n2s.at[j], sib))
    span_rows = 2 * cr
    per_tile = block // span_rows

    def qkv_terms(j, carry):
        at = lax.rem(me.c // per_tile + j, width // block)
        x = b.xrow[:, pl.ds(tall(at * block, block), block)]
        rows = pl.ds(tall(total + at * block, block), block)
        for t in range(3):
            b.act[t, rows, 0:block] = dot(x, b.act[t, 0:total, 0:block], TN).astype(BF)
        for i in range(per_tile):
            chip = at * per_tile + i

            @pl.when(chip != me.c)
            def _(chip=chip):
                src = b.act.at[:, pl.ds(tall(total + chip * span_rows, span_rows), span_rows), 0:block]
                to = (2 * chip + me.k, me.s)
                remote(src, b.qgpl.at[me.c], b.q1s.at[chip], b.q1r.at[me.c], to).start()

        return carry

    lax.fori_loop(1, width // block, qkv_terms, 0)
    qkv_terms(0, 0)
    og_column()
    tok = local(b.tok, b.norm, b.load.at[0])
    tok.start()
    tok.wait()
    for h in range(me.half):
        arrived(b.dnr.at[h], b.n2r.at[h])

    def first_back(rows):
        grad = b.dnr[0, rows, :].astype(F32)
        for h in range(1, me.half):
            grad = grad + b.dnr[h, rows, :].astype(F32)
        normal, scale = normalise(b.norm[rows, :])
        b.ig[rows, :] += norm_back(grad, normal, scale, b.gain[0:1, :])
        add_ln(0, jnp.sum(grad * normal, axis=0, keepdims=True))
        add_ln(1, jnp.sum(grad, axis=0, keepdims=True))

    by_rows(first_back)
    store(1)

    def send_lnp(j, carry):
        other = lax.rem(me.n + j, me.total)
        remote(
            b.lnp.at[other // per], b.lnr.at[me.n], b.lnt.at[0], b.lnt.at[1], me.of_rank(other)
        ).start()
        return carry

    lax.fori_loop(1, me.total, send_lnp, 0)
    b.lnr[me.n] = b.lnp[me.n // per]
    own = pl.ds(tall(total + me.c * span_rows, span_rows), span_rows)
    sums = [b.act[t, own, 0:block].astype(F32) for t in range(3)]
    for j in range(1, me.chips):
        chip = lax.rem(me.c + j, me.chips)
        part = b.qgpl.at[chip]
        remote(part, part, b.q1s.at[chip], b.q1r.at[chip], sib).wait()
        for t in range(3):
            sums[t] = sums[t] + b.qgpl[chip, t].astype(F32)
    for t in range(3):
        b.qgc[t] = sums[t].astype(BF)
    source = me.k * seq + me.s
    for core in range(2):
        for j in range(seq):
            to = lax.rem(me.s + j, seq)
            src = b.qgc.at[:, pl.ds(tall((core * seq + to) * wr, wr), wr), :]
            here = jnp.logical_and(core == me.k, to == me.s)
            send_or_keep(
                here, src, b.qgz.at[source], b.q2s.at[core, j], b.q2r.at[source], (2 * me.c + core, to)
            )
            last.append(functools.partial(sent, here, src, b.q2s.at[core, j], sib))
    value = b.out[...] + b.xown[...].astype(F32)
    for j in range(1, nc):
        remote(b.brr.at[j - 1], b.brr.at[j - 1], b.brs.at[j], b.brr_sem.at[j], sib).wait()
        value = value + b.brr[j - 1].astype(F32)
    b.out[...] = value
    store(0)
    acc = b.ogc[pl.ds(tall(me.s * wr, wr), wr), :].astype(F32)
    for j in range(1, seq):
        remote(b.ogz.at[j], b.ogz.at[j], b.o3s.at[j], b.o3r.at[j], sib).wait()
        acc = acc + b.ogz[j].astype(F32)
    b.og[...] = acc
    store(4)
    for m in range(3):
        for j in range(1, 3):
            arrived(b.rs.at[j, m], b.gr.at[j, m])
        for j in range(3):
            last.append(functools.partial(sent, False, b.rs.at[0, 0], b.gs.at[j, m], sib))
        acc = bg[m][band_rows(me.s), :].astype(F32)
        acc = acc + b.rs[1, m].astype(F32) + b.rs[2, m].astype(F32)
        if me.groups == 1:
            b.fg[m] = acc
        else:
            bg[m][band_rows(me.s), :] = acc.astype(BF)
    if me.groups > 1:
        for m in range(3):
            for j in range(1, me.groups):
                other = lax.rem(me.g + j, me.groups)
                src = bg[m].at[pl.ds(tall(me.s * band + other * units, units), units), :]
                to = (other * me.group + me.p, me.s)
                remote(src, b.grp.at[j, m], b.grs.at[j, m], b.grr.at[j, m], to).start()
        for m in range(3):
            acc = bg[m][pl.ds(tall(me.s * band + me.g * units, units), units), :].astype(F32)
            for j in range(1, me.groups):
                part = b.grp.at[j, m]
                remote(part, part, b.grs.at[j, m], b.grr.at[j, m], sib).wait()
                acc = acc + b.grp[j, m].astype(F32)
            b.fg[m] = acc
    store(5)
    rest = b.lnr.at[pl.ds(0, me.total - 1)]
    remote(rest, rest, b.lnt.at[0], b.lnt.at[1], sib).wait()
    acc = b.lnr[0]
    for j in range(1, me.total):
        acc = acc + b.lnr[j]
    for i in range(fit):

        @pl.when(lax.rem(me.n, fit) == i)
        def _(i=i):
            b.lng[...] = acc[0:4, i * share : (i + 1) * share]

    store(2)
    for j in range(2 * seq):
        arrived(b.qgz.at[j], b.q2r.at[j])
    for hg in range(seq):
        core, h = hg % 2, hg // 2
        acc = b.qgz[core * seq + h].astype(F32) + b.qgz[core * seq + me.half + h].astype(F32)
        b.qg[:, :, hg * block : (hg + 1) * block] = acc
    store(3)
    for copy in last:
        copy()
    for copy in stores:
        copy.wait()


def keep_kernel(count, *refs):
    given, kept, held = refs[:count], refs[count : 2 * count], refs[2 * count : 3 * count]
    sems = refs[-1]
    ins = [local(given[i], held[i], sems.at[0, i]) for i in range(count)]
    outs = [local(held[i], kept[i], sems.at[1, i]) for i in range(count)]
    for copy in ins:
        copy.start()
    for i in range(count):
        ins[i].wait()
        outs[i].start()
    for copy in outs:
        copy.wait()


def body(dp, seq, tokens, ln_params, qkv_weight, out_weight, ffn_weight, lengths, cotangent):
    count, width = tokens.shape[1], tokens.shape[2]
    ranks = dp * seq
    total = count * seq
    wr = qkv_weight.shape[0]
    cr = wr * seq
    units = ffn_weight.shape[0]
    block = width // seq
    half = seq // 2
    group = min(dp, GROUP)
    groups = dp // group
    gchips, chips, slots = group // 2, dp // 2, groups * seq
    held = units * slots
    share = ln_params.shape[1]
    sem = pltpu.SemaphoreType.DMA
    vm = pltpu.VMEM
    anywhere = pl.BlockSpec(memory_space=pl.ANY)
    vmem = pl.BlockSpec(memory_space=pltpu.VMEM)
    operands = dict(
        tok=(tokens.reshape(count, width), anywhere),
        ln=(ln_params, vmem),
        wq=(qkv_weight.transpose(1, 0, 2), anywhere),
        wo=(out_weight, anywhere),
        wf=(ffn_weight.transpose(1, 0, 2), anywhere),
        lens=(lengths, vmem),
        cot=(cotangent.reshape(count, width), anywhere),
    )
    outs = dict(
        out=(count, width),
        ig=(count, width),
        lng=(4, share),
        qg=(3, wr, width),
        og=(wr, width),
        fg=(3, units, width),
    )
    scratch = dict(
        **{name: vm(dims, F32) for name, dims in outs.items()},
        norm=vm((count, width), F32),
        scale=vm((count, LANES), F32),
        lens_own=vm((8, LANES), jnp.int32),
        lens_pair=vm((2, 8, LANES), jnp.int32),
        ln_own=vm((8, LANES), F32),
        ln_all=vm((ranks, 8, LANES), F32),
        gain=vm((8, width), F32),
        wq_own=vm((3, wr, width), BF),
        wcol=vm((3, cr, 2 * block), BF),
        xown=vm((count, width), BF),
        dmb=vm((count, width), BF),
        xrow=vm((total, width), BF),
        wq_full=vm((3, width, block), BF),
        wo_full=vm((width, width), BF),
        dyb=vm((group, count, width), BF),
        q=vm((total, block), BF),
        kk=vm((total, block), BF),
        v=vm((total, block), BF),
        lse=vm((total, LANES), F32),
        cos=vm((total, LANES), F32),
        sin=vm((total, LANES), F32),
        seg_row=vm((8, total), F32),
        mixed=vm((seq, count, block), BF),
        mixed_in=vm((seq, count, block), BF),
        dmix_row=vm((seq, count, block), BF),
        wf_full=vm((3, held, width), BF),
        xall=vm((gchips, 2, count, width), BF),
        act=vm((3, group * count, held), BF),
        dpart=vm((2, 2, count, width), BF),
        dsib=vm((gchips, count, width), BF),
        dsum=vm((gchips, count, width), BF),
        drecv=vm((gchips - 1, count, width), BF),
        brr=vm((gchips - 1, count, width), BF),
        ogsib=vm((width // 2 // count, count, width), BF),
        ogpl=vm((chips, cr, width), BF),
        ogc=vm((cr, width), BF),
        ogz=vm((seq, wr, width), BF),
        dk=vm((total, block), F32),
        dv=vm((total, block), F32),
        dnsib=vm((half // 2, 2, count, width), BF),
        dnr=vm((half, count, width), BF),
        qgpl=vm((chips, 3, 2 * cr, block), BF),
        qgc=vm((3, 2 * cr, block), BF),
        qgz=vm((2 * seq, 3, wr, block), BF),
        rs=vm((3, 3, groups * units, width), BF),
        grp=vm((groups, 3, units, width) if groups > 1 else (8, LANES), BF),
        down=vm((held, width), BF),
        lnp=vm((width // LANES, 8, LANES), F32),
        lnr=vm((ranks, 8, LANES), F32),
        load=sem((7,)),
        keep=sem((6,)),
        lns=sem((2,)),
        lens_sem=sem((2,)),
        wq1s=sem((seq,)),
        wq1r=sem((seq,)),
        wq2s=sem((dp,)),
        wq2r=sem((dp,)),
        wo1s=sem((seq,)),
        wo1r=sem((seq,)),
        wo2s=sem((chips,)),
        wo2r=sem((chips,)),
        wo3s=sem((chips,)),
        wo3r=sem((chips,)),
        xs=sem((half, 2)),
        xr=sem((seq,)),
        xfs=sem((seq,)),
        xfr=sem((seq,)),
        dys=sem((gchips,)),
        dyr=sem((gchips,)),
        dyfs=sem((gchips,)),
        dyfr=sem((gchips,)),
        fgs=sem((groups,)),
        fgr_sem=sem((groups,)),
        hs=sem((3, 3)),
        hr=sem((3, 3)),
        ms=sem((seq,)),
        mr=sem((seq,)),
        xs2=sem((gchips,)),
        xr2=sem((gchips,)),
        xfs2=sem((gchips,)),
        xfr2=sem((gchips,)),
        dss=sem((gchips,)),
        dsr=sem((gchips,)),
        dps=sem((gchips,)),
        dpr=sem((gchips,)),
        bss=sem((gchips,)),
        bsr=sem((gchips,)),
        brs=sem((gchips,)),
        brr_sem=sem((gchips,)),
        dms=sem((seq,)),
        dmr=sem((seq,)),
        gs=sem((3, 3)),
        gr=sem((3, 3)),
        grs=sem((groups, 3)),
        grr=sem((groups, 3)),
        o1=sem((2,)),
        o2s=sem((chips,)),
        o2r=sem((chips,)),
        o3s=sem((seq,)),
        o3r=sem((seq,)),
        n1=sem((2,)),
        n2s=sem((half,)),
        n2r=sem((half,)),
        q1s=sem((chips,)),
        q1r=sem((chips,)),
        q2s=sem((2, seq)),
        q2r=sem((2 * seq,)),
        lnt=sem((2,)),
    )
    names = (*operands, *[name + "_out" for name in outs], *scratch)
    results = pl.pallas_call(
        functools.partial(layer_kernel, names, dp, seq, lengths.shape[1]),
        out_shape=tuple(jax.ShapeDtypeStruct(dims, F32) for dims in outs.values()),
        in_specs=[spec for _, spec in operands.values()],
        out_specs=tuple([anywhere] * len(outs)),
        scratch_shapes=list(scratch.values()),
        compiler_params=pltpu.CompilerParams(
            collective_id=1, has_side_effects=True, vmem_limit_bytes=VMEM_BYTES
        ),
        cost_estimate=pl.CostEstimate(
            flops=32 * 10**9, bytes_accessed=2**24, transcendentals=10**7
        ),
        name="layer",
    )(*[value for value, _ in operands.values()])
    out, input_grad, ln_grad, qg, og, fg = pl.pallas_call(
        functools.partial(keep_kernel, len(outs)),
        out_shape=tuple(jax.ShapeDtypeStruct(dims, F32) for dims in outs.values()),
        in_specs=[anywhere] * len(outs),
        out_specs=tuple([anywhere] * len(outs)),
        scratch_shapes=[*[vm(dims, F32) for dims in outs.values()], sem((2, len(outs)))],
        name="keep",
    )(*results)
    return (
        out.reshape(1, count, width),
        input_grad.reshape(1, count, width),
        ln_grad,
        qg.transpose(1, 0, 2),
        og,
        fg.transpose(1, 0, 2),
    )


def solution(mesh):
    dp, seq = mesh.shape["dp"], mesh.shape["seq"]
    both = ("dp", "seq")
    in_specs = (
        P("dp", "seq", None),
        P(None, both),
        P(both, None, None),
        P(both, None),
        P(both, None, None),
        P("dp", None),
        P("dp", "seq", None),
    )
    out_specs = (
        P("dp", "seq", None),
        P("dp", "seq", None),
        P(None, both),
        P(both, None, None),
        P(both, None),
        P(both, None, None),
    )
    return jax.shard_map(
        functools.partial(body, dp, seq),
        mesh=mesh,
        in_specs=in_specs,
        out_specs=out_specs,
        check_vma=False,
    )
```
